32 devices in a mesh: lat: 8 (over z, x), rad: 4 (over y, core).
Axes of the slice: x: 2, y: 2, z: 4, core: 2. Of those that a mesh axis runs over, the one named last changes fastest.
Arguments:
- kernels: float32 [3, 256000], P(None, 'lat'), may hold values from -6 to 6
- cells: int32 [3, 2048], P(None, 'lat'), may hold values from 0 to 251, as said below
- tiles: int32 [2048, 1], P('lat'), may hold values from 0 to 7; in each aligned block of 256 rows (0 to 255, 256 to 511, ...) at most 64 rows name the same one
- width_class: int32 [8], P('lat'), may hold values from 0 to 3
Outputs:
- smoothed: float32 [3, 64, 128, 256], P(None, 'lat', 'rad')
The draws below stay inside these ranges and needn't reach their ends.
Inputs may be any that keep to these rules, and one draw needn't show every extreme that they name: `tiles`: of the elements of one index of lat, at most 64 name the same tile, a bound that some block reaches of them. cells[0, e] <= 3, cells[1, e] <= 123 and cells[2, e] <= 251, so that each element's 5 x 5 x 5 block lies in its tile; each bound is reached.
All inputs are finite; a program needn't handle non-finite values.
Results may differ from the reference program's by a relative error of at most 0.000078.
Values sent between devices are 32-bit elements; how exact they have to be, the bound alone decides.
A program may use at most 192 MiB of HBM per device.

```python
import math
import jax
import jax.numpy as jnp
import numpy as np

CX = 8
NY = 256
E_DEV = 256
NGLL = 125
HW = 4
HY = 8
HZ = 4
NX = 64
NZ = 128
ELEMS = 2048
CAP = 64
N_LAT = 8


def draw_cells(key, part):
    key_x, key_y, key_z = jax.random.split(jax.random.fold_in(key, 11), 3)
    base_x = jax.random.randint(key_x, (ELEMS,), 0, CX - 4)
    base_y = jax.random.randint(key_y, (ELEMS,), 0, NY - 4)
    base_z = jax.random.randint(key_z, (ELEMS,), 0, NZ - 4)
    base_x = base_x.at[0].set(0).at[1].set(CX - 5)
    base_y = base_y.at[0].set(0).at[1].set(NY - 5)
    base_z = base_z.at[0].set(0).at[1].set(NZ - 5)
    return jnp.stack([base_x, base_z, base_y]).astype(jnp.int32)


def set_ends(values, key, least, top_value):
    longest = values.shape.index(max(values.shape))
    spots = []
    for shift in (0, 1):
        where = [jax.random.randint(jax.random.fold_in(key, axis), (), 0, length) for axis, length in enumerate(values.shape)]
        where[longest] = (where[longest] + shift) % values.shape[longest]
        spots.append(tuple(where))
    return values.at[spots[0]].set(least).at[spots[1]].set(top_value)


def shard_levels(rng, shape, cuts, smallest, top_value):
    def one(axis_at, parts):
        heights = jax.random.uniform(jax.random.fold_in(jax.random.fold_in(rng, 6), axis_at), (parts,), jnp.float32, smallest / len(cuts), top_value / len(cuts))
        return jnp.repeat(jnp.exp(heights), shape[axis_at] // parts).reshape((-1,) + (1,) * (len(shape) - axis_at - 1))

    level = one(*cuts[0])
    for cut in cuts[1:]:
        level = level * one(*cut)
    return level


def deal_out(rng, own, number, rows, count, top, limit, skew):
    sequence = jax.random.permutation(rng, count)
    packed, common = load_shares(count, rows * top, limit, skew, True), load_shares(count, rows * top, limit, skew, False)
    places = jnp.arange(count)

    def named(sizes, rotation):
        used = int((sizes > 0).sum())
        fixed = max(1, used // 4)
        shifted = fixed + (places - fixed + rotation * (used - fixed)) % max(1, count - fixed)
        return jnp.zeros((count,), jnp.int32).at[sequence[jnp.where(places < fixed, places, shifted)]].set(jnp.asarray(sizes, jnp.int32))

    sizes = jnp.where(number % 4 == 0, named(packed, number // 4), named(common, number - number // 4 - 1))
    mixed = jax.random.permutation(jax.random.fold_in(own, 3), count)
    source_of, sink = mixed[0:count // 2 * 2:2], mixed[1:count // 2 * 2:2]
    room = jnp.minimum(sizes[source_of] - 1, limit - sizes[sink]) // 2
    room = jnp.where((source_of == sequence[0]) | (sink == sequence[0]) | (sizes[sink] == 0), 0, jnp.maximum(room, 0))
    shifted = jax.random.randint(jax.random.fold_in(own, 4), (count // 2,), 0, 1 << 20) % (room + 1)
    sizes = sizes.at[source_of].add(-shifted).at[sink].add(shifted)
    members = jnp.searchsorted(jnp.cumsum(sizes), jnp.arange(rows * top), side="right").astype(jnp.int32)
    table = members.reshape(top, rows).T
    table = table[jax.random.permutation(jax.random.fold_in(own, 1), rows)]
    rotation = jax.random.randint(jax.random.fold_in(own, 2), (rows, 1), 0, top)
    return jnp.take_along_axis(table, (jnp.arange(top)[None, :] + rotation) % top, axis=1)


def load_shares(number_of, total, most, lean, full):
    weights = [(1 << 20) // math.isqrt(standing ** lean) + 1 for standing in range(1, number_of + 1)]
    largest = most if full else min(most, max(-(-total // number_of), total * weights[0] // sum(weights)))
    least = 1 if total - largest >= number_of - 1 else 0
    counts, spare = [largest] + [least] * (number_of - 1), total - largest - least * (number_of - 1)
    while spare > 0:
        movable = [i for i in range(1, number_of) if counts[i] < largest] or [i for i in range(1, number_of) if counts[i] < most]
        whole, left = sum([weights[i] for i in movable]), spare
        for i in movable:
            more = min(most - counts[i], max(1, left * weights[i] // whole), spare)
            counts[i] = counts[i] + more
            spare = spare - more
    return np.array(counts)


def bell_draw(stream_key, dims, width, limit, cuts=(), held_as=jnp.bfloat16):
    values = width * jax.random.normal(stream_key, dims, jnp.float32)
    if cuts:
        values = values * shard_levels(stream_key, dims, cuts, -0.22, 0.18)
    return jnp.clip(values, -limit, limit).astype(held_as)


def setup_inputs(seed: int = 0) -> dict:
    key_list = jax.random.split(jax.random.key(seed), 5)
    kernels = bell_draw(key_list[0], (3, ELEMS * NGLL), 1.0, 6.0, ((1, 8),), jnp.float32)
    cells = draw_cells(jax.random.fold_in(key_list[4], 71), 0)
    tiles_keys = jax.random.split(jax.random.fold_in(key_list[2], 1), ELEMS // E_DEV)
    tiles_turns = jax.random.permutation(jax.random.fold_in(key_list[2], 3), ELEMS // E_DEV)
    tiles = jax.vmap(lambda own, number: deal_out(jax.random.fold_in(key_list[2], 2), own, number, E_DEV, N_LAT, 1, CAP, 2))(tiles_keys, tiles_turns).reshape((ELEMS, 1))
    width_class = set_ends(jax.random.randint(key_list[3], (N_LAT,), 0, 4), jax.random.fold_in(key_list[3], 1), 0, 3).astype(jnp.int32)
    return {"kernels": kernels, "cells": cells, "tiles": tiles, "width_class": width_class}


def band_weights(count, sigma, half):
    place = jnp.arange(count)
    offsets = jnp.arange(-half, half + 1)
    target = place[:, None] + offsets[None, :]
    valid = (target >= 0) & (target < count)
    gauss = jnp.exp(-(offsets[None, :].astype(jnp.float32) ** 2) / (2.0 * sigma[:, None] ** 2))
    gauss = jnp.where(valid, gauss, jnp.float32(0.0))
    return gauss / jnp.sum(gauss, axis=1, keepdims=True)


def lax_slice(array, axis, start, length):
    return jax.lax.slice_in_dim(array, start, start + length, axis=axis)


def band_apply(field, weights, axis, half):
    count = field.shape[axis]
    widths = [(0, 0)] * field.ndim
    widths[axis] = (half, half)
    padded = jnp.pad(field, widths)
    shape = [1] * field.ndim
    shape[axis] = count
    total = jnp.zeros_like(field)
    for offset in range(-half, half + 1):
        piece = lax_slice(padded, axis, half + offset, count)
        total = total + weights[:, offset + half].reshape(shape) * piece
    return total


def point_cells(cells, depth):
    points = jnp.arange(NGLL, dtype=jnp.int32)
    along_x = points // 25
    along_z = (points // 5) % 5
    along_y = points % 5
    return (cells[0][:, None] + along_x[None, :]) * (depth * NY) + (cells[1][:, None] + along_z[None, :]) * NY + (cells[2][:, None] + along_y[None, :])


def reference(kernels, cells, tiles, width_class):
    flat = point_cells(cells, NZ)
    global_cells = (tiles[:, 0][:, None] * (CX * NZ * NY) + flat).reshape(-1)
    summed = jnp.zeros((3, NX * NZ * NY), jnp.float32).at[:, global_cells].add(kernels)
    summed = summed.reshape(3, NX, NZ, NY)
    sigma_x = 1.0 + 0.75 * width_class[jnp.arange(NX) // CX].astype(jnp.float32)
    lateral = band_apply(summed, band_weights(NX, sigma_x, HW), 1, HW)
    across = band_apply(lateral, band_weights(NY, jnp.full((NY,), 2.5, jnp.float32), HY), 3, HY)
    return band_apply(across, band_weights(NZ, jnp.full((NZ,), 1.5, jnp.float32), HZ), 2, HZ)
```

```python
import functools

import jax
import jax.numpy as jnp
import numpy as np
from jax import lax
from jax.experimental import pallas as pl
from jax.experimental.pallas import tpu as pltpu
from jax.sharding import PartitionSpec as P

CX = 8
NY = 256
CZ = 32
NGLL = 125
HW = 4
HY = 8
HZ = 4
ZP = CZ + 4 * HZ
LANES = 128
TAPS = 2 * HZ + 1
PADX = CX + 2 * HW
PACK_UNROLL = 4
SUM_UNROLL = 4
VMEM_LIMIT = 48 * 2**20
MESH = pl.DeviceIdType.MESH


def band_matrix(count, sigma, half):
    place = np.arange(count)
    gap = place[None, :] - place[:, None]
    gauss = np.where(np.abs(gap) <= half, np.exp(-(gap**2) / (2.0 * sigma**2)), 0.0)
    return gauss / gauss.sum(axis=1, keepdims=True)


def z_taps(n_rad):
    full = np.pad(band_matrix(CZ * n_rad, 1.5, HZ), ((0, 0), (HZ, HZ)))
    return np.stack([full[z, z : z + TAPS] for z in range(CZ * n_rad)]).astype(np.float32)


def pack_kernel(
    n_lat, n_rad, share, elements, tiles_ref, cells_hbm, kern_hbm, out_ref, count, todo, place, cells_ref, kern_ref, sems
):
    slab = lax.axis_index("rad")
    rows = elements * NGLL // LANES
    bring_cells = pltpu.make_async_copy(cells_hbm, cells_ref, sems.at[0])
    bring_kern = pltpu.make_async_copy(kern_hbm, kern_ref, sems.at[1])
    bring_cells.start()
    bring_kern.start()
    out_ref[...] = jnp.full(out_ref.shape, -1000.0, jnp.float32)
    lane = lax.broadcasted_iota(jnp.int32, (3, LANES), 1)

    @pl.loop(0, n_lat)
    def _(t):
        count[t] = 0

    def listed(e, n):
        t = tiles_ref[e]
        rank = count[t]
        count[t] = rank + 1
        slot = lax.div(rank, n_rad)
        todo[n] = e
        place[n] = t * share + slot
        return n + jnp.where(rank - slot * n_rad == slab, 1, 0)

    n = lax.fori_loop(0, elements, listed, 0, unroll=4)
    for more in range(PACK_UNROLL):
        todo[n + more] = 0
        place[n + more] = n_lat * share
    bring_cells.wait()
    bring_kern.wait()

    def packed(step, _):
        for u in range(PACK_UNROLL):
            e = todo[step * PACK_UNROLL + u]
            at = place[step * PACK_UNROLL + u]
            start = e * NGLL
            row = lax.shift_right_logical(start, 7)
            off = start & (LANES - 1)
            after = jnp.minimum(row + 1, rows - 1)
            a = kern_ref[:, pl.ds(pl.multiple_of(row * LANES, LANES), LANES)]
            b = kern_ref[:, pl.ds(pl.multiple_of(after * LANES, LANES), LANES)]
            v = pltpu.roll(jnp.where(lane >= off, a, b), (LANES - off) & (LANES - 1), 1)
            v = jnp.where(lane == NGLL, cells_ref[0, e].astype(jnp.float32), v)
            v = jnp.where(lane == NGLL + 1, cells_ref[1, e].astype(jnp.float32), v)
            v = jnp.where(lane == NGLL + 2, cells_ref[2, e].astype(jnp.float32), v)
            t = lax.div(at, share)
            slot = at - t * share
            for c in range(3):
                out_ref[t, pl.ds(c * share + slot, 1), :] = v[c : c + 1]
        return 0

    lax.fori_loop(0, lax.div(n + PACK_UNROLL - 1, PACK_UNROLL), packed, 0)


def exchange_kernel(n_lat, n_rad, send_ref, recv_ref, own_sem, send_sem, recv_sem, fwd_sem, got_sem):
    tile, slab = lax.axis_index("lat"), lax.axis_index("rad")
    barrier = pltpu.get_barrier_semaphore()

    @pl.loop(1, n_lat)
    def _(k):
        pl.semaphore_signal(barrier, inc=1, device_id=(lax.rem(tile + k, n_lat), slab), device_id_type=MESH)

    pair = slab + 1 - 2 * lax.rem(slab, 2)
    other = slab + 2 - 4 * lax.div(slab, 2)
    for peer in (pair, other):
        pl.semaphore_signal(barrier, inc=1, device_id=(tile, peer), device_id_type=MESH)
    pl.semaphore_wait(barrier, n_lat - 1 + 2)

    def across(k):
        to = lax.rem(tile + k, n_lat)
        return pltpu.make_async_remote_copy(
            src_ref=send_ref.at[to],
            dst_ref=recv_ref.at[slab, tile],
            send_sem=send_sem.at[k],
            recv_sem=recv_sem.at[k],
            device_id=(to, slab),
            device_id_type=MESH,
        )

    def share(k, of, to, way):
        block = recv_ref.at[of, lax.rem(tile + n_lat - k, n_lat)]
        return pltpu.make_async_remote_copy(
            src_ref=block,
            dst_ref=block,
            send_sem=fwd_sem.at[way, k],
            recv_sem=got_sem.at[way, k],
            device_id=(tile, to),
            device_id_type=MESH,
        )

    def forward(k):
        share(k, slab, other, 0).start()
        share(k, slab, pair, 1).start()

    def relay(k):
        share(k, other, other, 0).wait_recv()
        share(k, other, pair, 2).start()

    @pl.loop(1, n_lat)
    def _(k):
        across(k).start()

    own = pltpu.make_async_copy(send_ref.at[tile], recv_ref.at[slab, tile], own_sem)
    own.start()
    own.wait()
    forward(0)

    @pl.loop(1, n_lat)
    def _(k):
        across(k).wait_recv()
        forward(k)

    @pl.loop(0, n_lat)
    def _(k):
        relay(k)

    @pl.loop(0, n_lat)
    def _(k):
        share(k, pair, pair, 1).wait_recv()
        share(k, other + pair - slab, pair, 2).wait_recv()

    @pl.loop(1, n_lat)
    def _(k):
        across(k).wait_send()

    @pl.loop(0, n_lat)
    def _(k):
        share(k, slab, other, 0).wait_send()
        share(k, slab, pair, 1).wait_send()
        share(k, other, pair, 2).wait_send()


def sum_kernel(blocks, share, meta_ref, recv_ref, acc, todo):
    slab = lax.axis_index("rad")
    slots = blocks * share
    acc[...] = jnp.zeros(acc.shape, jnp.float32)
    lane = lax.broadcasted_iota(jnp.int32, (8, LANES), 1)
    sub = lax.broadcasted_iota(jnp.int32, (8, LANES), 0)
    ramp = 25 * sub + lane
    low = slab * CZ - 2 * HZ

    def listed(s, n):
        zb = meta_ref[slots + s] - low
        todo[n] = s
        return n + jnp.where((zb >= 0) & (zb < CZ + 3 * HZ), 1, 0)

    n = lax.fori_loop(0, slots, listed, 0, unroll=8)
    for more in range(SUM_UNROLL):
        todo[n + more] = 0

    def place(at, values, index, mask):
        for j in range(5):
            picked = jnp.where(mask, index + 5 * j, NGLL)
            for c in range(3):
                piece = jnp.take_along_axis(values[c], picked, axis=1, mode="promise_in_bounds")
                acc[pl.ds(pl.multiple_of(at + (3 * j + c) * 8, 8), 8), :] += piece

    def summed(step, _):
        later = []
        for u in range(SUM_UNROLL):
            s = todo[step * SUM_UNROLL + u]
            good = step * SUM_UNROLL + u < n
            x0 = jnp.clip(meta_ref[s], 0, CX - 5)
            zb = jnp.clip(meta_ref[slots + s] - low, 0, CZ + 3 * HZ - 1)
            y0 = jnp.clip(meta_ref[2 * slots + s], 0, NY - 5)
            block = lax.div(s, share)
            slot = s - block * share
            values = []
            for c in range(3):
                row = jnp.broadcast_to(recv_ref[block, pl.ds(c * share + slot, 1), :], (8, LANES))
                values.append(jnp.where(lane < NGLL, row, 0.0))
            half = lax.shift_right_logical(y0, 7)
            yl = y0 & (LANES - 1)
            index = ramp - (25 * x0 + yl)
            rows = (sub >= x0) & (sub < jnp.where(good, x0 + 5, 0))
            at = (half * ZP + zb) * 24
            place(at, values, index, rows & (lane >= yl) & (lane < yl + 5))
            later.append((at, values, index, rows, yl))
        widest = functools.reduce(jnp.maximum, [entry[4] for entry in later])

        @pl.when(widest > LANES - 5)
        def _():
            for at, values, index, rows, yl in later:
                over = rows & (lane < yl + 5 - LANES)

                @pl.when(yl > LANES - 5)
                def _():
                    place(at + ZP * 24, values, index + LANES, over)

        return 0

    lax.fori_loop(0, lax.div(n + SUM_UNROLL - 1, SUM_UNROLL), summed, 0)


def finish_kernel(n_lat, taps_ref, wx_ref, acc, wy_ref, out_ref, planes, rows_ref, send_sem, recv_sem):
    tile, slab = lax.axis_index("lat"), lax.axis_index("rad")
    barrier = pltpu.get_barrier_semaphore()
    has_prev, has_next = tile > 0, tile < n_lat - 1
    halo = HW * CZ

    @pl.when(has_prev)
    def _():
        pl.semaphore_signal(barrier, inc=1, device_id=(tile - 1, slab), device_id_type=MESH)

    @pl.when(has_next)
    def _():
        pl.semaphore_signal(barrier, inc=1, device_id=(tile + 1, slab), device_id_type=MESH)

    def at(c, row, count):
        return rows_ref.at[:, pl.ds(c * PADX * CZ + row, count), :]

    def to_next(c):
        return pltpu.make_async_remote_copy(
            src_ref=at(c, CX * CZ, halo),
            dst_ref=at(c, 0, halo),
            send_sem=send_sem.at[0, c],
            recv_sem=recv_sem.at[0, c],
            device_id=(tile + 1, slab),
            device_id_type=MESH,
        )

    def to_prev(c):
        return pltpu.make_async_remote_copy(
            src_ref=at(c, halo, halo),
            dst_ref=at(c, halo + CX * CZ, halo),
            send_sem=send_sem.at[1, c],
            recv_sem=recv_sem.at[1, c],
            device_id=(tile - 1, slab),
            device_id_type=MESH,
        )

    for c in range(3):

        @pl.loop(0, CZ, unroll=4)
        def _(z):
            for half in range(NY // LANES):
                total = jnp.zeros((CX, LANES), jnp.float32)
                for d in range(TAPS):
                    weight = taps_ref[(slab * CZ + z) * TAPS + d]
                    row = pl.multiple_of(((half * ZP + z + HZ + d) * 3 + c) * CX, 8)
                    total = total + weight * acc[pl.ds(row, CX), :]
                cols = slice(half * LANES, (half + 1) * LANES)
                planes[pl.ds(pl.multiple_of(z * CX, 8), CX), cols] = total

        product = jnp.dot(planes[...], wy_ref[...], precision=lax.Precision.HIGHEST)
        for z in range(CZ):
            for half in range(NY // LANES):
                piece = product[z * CX : (z + 1) * CX, half * LANES : (half + 1) * LANES]
                rows_ref[half, pl.ds(c * PADX * CZ + halo + z, CX, stride=CZ), :] = piece

        if c == 0:
            beside = jnp.minimum(tile, 1) + jnp.minimum(n_lat - 1 - tile, 1)
            pl.semaphore_wait(barrier, beside)

        @pl.when(has_next)
        def _():
            to_next(c).start()

        @pl.when(has_prev)
        def _():
            to_prev(c).start()

        zeros = jnp.zeros((NY // LANES, halo, LANES), jnp.float32)

        @pl.when(tile == 0)
        def _():
            rows_ref[:, c * PADX * CZ : c * PADX * CZ + halo, :] = zeros

        @pl.when(tile == n_lat - 1)
        def _():
            rows_ref[:, c * PADX * CZ + halo + CX * CZ : (c + 1) * PADX * CZ, :] = zeros

    for c in range(3):

        @pl.when(has_prev)
        def _():
            to_next(c).wait_recv()

        @pl.when(has_next)
        def _():
            to_prev(c).wait_recv()

        @pl.loop(0, CX)
        def _(x):
            for half in range(NY // LANES):
                total = jnp.zeros((CZ, LANES), jnp.float32)
                for d in range(2 * HW + 1):
                    row = pl.multiple_of(c * PADX * CZ + (x + d) * CZ, 8)
                    total = total + wx_ref[x * (2 * HW + 1) + d] * rows_ref[half, pl.ds(row, CZ), :]
                out_ref[c, x, :, half * LANES : (half + 1) * LANES] = total

    for c in range(3):

        @pl.when(has_next)
        def _():
            to_next(c).wait_send()

        @pl.when(has_prev)
        def _():
            to_prev(c).wait_send()


def x_weights(width_class, n_lat):
    rows = lax.axis_index("lat") * CX + jnp.arange(CX)
    sigma = 1.0 + 0.75 * width_class[0].astype(jnp.float32)
    offsets = jnp.arange(-HW, HW + 1)
    target = rows[:, None] + offsets[None, :]
    valid = (target >= 0) & (target < CX * n_lat)
    gauss = jnp.exp(-(offsets[None, :].astype(jnp.float32) ** 2) / (2.0 * sigma**2))
    gauss = jnp.where(valid, gauss, 0.0)
    return gauss / jnp.sum(gauss, axis=1, keepdims=True)


def on_device(n_lat, n_rad, kernels, cells, tiles, width_class):
    elements = tiles.shape[0]
    cap = max(2, 2 * elements // n_lat)
    share = -(-cap // n_rad)
    blocks = n_rad * n_lat
    slots = blocks * share
    params = pltpu.CompilerParams(vmem_limit_bytes=VMEM_LIMIT)
    smem = pl.BlockSpec(memory_space=pltpu.SMEM)
    vmem = pl.BlockSpec(memory_space=pltpu.VMEM)
    hbm = pl.BlockSpec(memory_space=pl.ANY)
    send = pl.pallas_call(
        functools.partial(pack_kernel, n_lat, n_rad, share, elements),
        out_shape=jax.ShapeDtypeStruct((n_lat + 1, 3 * share, LANES), jnp.float32),
        in_specs=[smem, hbm, hbm],
        out_specs=vmem,
        scratch_shapes=[
            pltpu.SMEM((n_lat,), jnp.int32),
            pltpu.SMEM((elements + PACK_UNROLL,), jnp.int32),
            pltpu.SMEM((elements + PACK_UNROLL,), jnp.int32),
            pltpu.SMEM(cells.shape, jnp.int32),
            pltpu.VMEM(kernels.shape, jnp.float32),
            pltpu.SemaphoreType.DMA((2,)),
        ],
        compiler_params=params,
    )(tiles.reshape(-1), cells, kernels)
    recv = pl.pallas_call(
        functools.partial(exchange_kernel, n_lat, n_rad),
        out_shape=jax.ShapeDtypeStruct((n_rad, n_lat, 3 * share, LANES), jnp.float32),
        in_specs=[vmem],
        out_specs=vmem,
        scratch_shapes=[
            pltpu.SemaphoreType.DMA,
            pltpu.SemaphoreType.DMA((n_lat,)),
            pltpu.SemaphoreType.DMA((n_lat,)),
            pltpu.SemaphoreType.DMA((3, n_lat)),
            pltpu.SemaphoreType.DMA((3, n_lat)),
        ],
        compiler_params=pltpu.CompilerParams(
            vmem_limit_bytes=VMEM_LIMIT, collective_id=0, has_side_effects=True
        ),
    )(send)
    recv = recv.reshape(blocks, 3 * share, LANES)
    meta = recv[:, :share, NGLL:].transpose(2, 0, 1).reshape(-1).astype(jnp.int32)
    grid_rows = NY // LANES * ZP * 24
    summed = pl.pallas_call(
        functools.partial(sum_kernel, blocks, share),
        out_shape=jax.ShapeDtypeStruct((grid_rows, LANES), jnp.float32),
        in_specs=[smem, vmem],
        out_specs=vmem,
        scratch_shapes=[pltpu.SMEM((slots + SUM_UNROLL,), jnp.int32)],
        compiler_params=params,
    )(meta, recv)
    return pl.pallas_call(
        functools.partial(finish_kernel, n_lat),
        out_shape=jax.ShapeDtypeStruct((3, CX, CZ, NY), jnp.float32),
        in_specs=[smem, smem, vmem, vmem],
        out_specs=vmem,
        scratch_shapes=[
            pltpu.VMEM((CZ * CX, NY), jnp.float32),
            pltpu.VMEM((NY // LANES, 3 * PADX * CZ, LANES), jnp.float32),
            pltpu.SemaphoreType.DMA((2, 3)),
            pltpu.SemaphoreType.DMA((2, 3)),
        ],
        compiler_params=pltpu.CompilerParams(
            vmem_limit_bytes=VMEM_LIMIT, collective_id=1, has_side_effects=True
        ),
    )(
        jnp.asarray(z_taps(n_rad).reshape(-1)),
        x_weights(width_class, n_lat).reshape(-1),
        summed,
        jnp.asarray(band_matrix(NY, 2.5, HY).T.astype(np.float32)),
    )

ROW_TILES = 3
Z_BINS = 11
Y_TILES = 17
WINDOW = CZ + 2 * HZ
DEPTH = 2 * CX * WINDOW
SUM_WAYS = 4


def gather_kernel(n_lat, n_rad, block, width_ref, tiles_hbm, cells_hbm, kern_hbm, data_ref, words_ref, whi_ref, wlo_ref,
                  kern_ref, tiles_ref, cells_ref, index_ref, compact_ref, in_sem, is_sem, ir_sem, zs, zr, xs, xr, ys, yr, bs, br):
    lat, rad = lax.axis_index("lat"), lax.axis_index("rad")
    levels = n_lat // 2
    z, x = lax.div(lat, 2), lax.rem(lat, 2)
    y, k = lax.div(rad, 2), lax.rem(rad, 2)
    across_x, across_y, across_k = lat + 1 - 2 * x, rad + 2 - 4 * y, rad + 1 - 2 * k
    barrier = pltpu.get_barrier_semaphore()

    @pl.loop(1, n_lat)
    def _(step):
        pl.semaphore_signal(barrier, inc=1, device_id=(lax.rem(lat + step, n_lat), rad), device_id_type=MESH)

    for peer in (across_y, across_k):
        pl.semaphore_signal(barrier, inc=1, device_id=(lat, peer), device_id_type=MESH)
    brought = [
        pltpu.make_async_copy(kern_hbm, kern_ref, in_sem.at[0]),
        pltpu.make_async_copy(tiles_hbm, tiles_ref, in_sem.at[1]),
        pltpu.make_async_copy(cells_hbm, cells_ref, in_sem.at[2]),
    ]
    for copy in brought:
        copy.start()

    half = block // 2
    edge = half // 8 // 3 * 8 + 8
    inner = half - 2 * edge
    mine = k * half
    spans = {"send": (mine + y * (edge + inner), edge), "inner": (mine + edge, inner), "take": (mine + (1 - y) * (edge + inner), edge)}
    theirs = (1 - k) * half
    other = {"send": (theirs + y * (edge + inner), edge), "inner": (theirs + edge, inner), "take": (theirs + (1 - y) * (edge + inner), edge)}
    parts = ("send", "inner")

    def piece(i, span):
        return data_ref.at[pl.ds(pl.multiple_of(i * block + span[0], 8), span[1])]

    def move(i, span, send_sem, recv_sem, device):
        return pltpu.make_async_remote_copy(
            src_ref=piece(i, span), dst_ref=piece(i, span), send_sem=send_sem, recv_sem=recv_sem,
            device_id=device, device_id_type=MESH)

    def z_move(i, j, up):
        return move(i, spans[parts[j]], zs.at[i, 2 * j + (0 if up else 1)], zr.at[i, j], (lat + (2 if up else -2), rad))

    def x_move(i, j):
        return move(i, spans[parts[j]], xs.at[i, j], xr.at[i, j], (across_x, rad))

    def y_move(i, name):
        return move(i, spans[name], ys.at[i], yr.at[i], (lat, across_y))

    def k_move(i, j, of):
        return move(i, of[("send", "inner", "take")[j]], bs.at[i, j], br.at[i, j], (lat, across_k))

    def index_move(step):
        to = lax.rem(lat + step, n_lat)
        return pltpu.make_async_remote_copy(
            src_ref=index_ref.at[lat], dst_ref=index_ref.at[lat], send_sem=is_sem.at[step], recv_sem=ir_sem.at[step],
            device_id=(to, rad), device_id_type=MESH)

    def index_take(step):
        whose = index_ref.at[lax.rem(lat + n_lat - step, n_lat)]
        return pltpu.make_async_remote_copy(
            src_ref=whose, dst_ref=whose, send_sem=is_sem.at[step], recv_sem=ir_sem.at[step],
            device_id=(lax.rem(lat + step, n_lat), rad), device_id_type=MESH)

    can_up, can_down = z < levels - 1, z > 0
    brought[1].wait()
    brought[2].wait()
    index_ref[lat] = jnp.concatenate([tiles_ref[...], cells_ref[...], jnp.zeros((4, tiles_ref.shape[1]), jnp.int32)], axis=0)
    brought[0].wait()
    base = pl.multiple_of(lat * block, 8)
    lane_tiles = kern_ref.shape[1] // LANES
    groups = lane_tiles // 8

    def packed(at, row, count):
        rows = [kern_ref[:, pl.ds(pl.multiple_of(at + u * LANES, LANES), LANES)] for u in range(count)]
        return jnp.concatenate(rows, axis=0)

    @pl.loop(0, groups, unroll=4)
    def _(g):
        data_ref[pl.ds(base + pl.multiple_of(g * 24, 8), 24), :] = packed(g * 8 * LANES, 0, 8)

    left = lane_tiles - groups * 8
    if left:
        tail = packed(groups * 8 * LANES, 0, left)
        room = block - groups * 24
        tail = jnp.concatenate([tail, jnp.zeros((room - 3 * left, LANES), jnp.float32)], axis=0)
        data_ref[pl.ds(base + groups * 24, room), :] = tail
    pl.semaphore_wait(barrier, n_lat - 1 + 2)

    @pl.loop(1, n_lat)
    def _(step):
        index_move(step).start()

    for j in range(2):
        @pl.when(can_up)
        def _():
            z_move(lat, j, True).start()

        @pl.when(can_down)
        def _():
            z_move(lat, j, False).start()

        x_move(lat, j).start()

    def weights():
        col = lax.broadcasted_iota(jnp.int32, (8, DEPTH), 1)
        beside = col >= CX * WINDOW
        rest = jnp.where(beside, col - CX * WINDOW, col)
        xl = lax.shift_right_logical(rest * 1639, 16)
        zc = rest - WINDOW * xl
        place = jnp.where(beside, jnp.where(xl < HW, xl + CX, xl - CX), xl)
        sub = lax.broadcasted_iota(jnp.int32, (8, DEPTH), 0)
        sigma = 1.0 + 0.75 * jnp.full((8, DEPTH), width_ref[0], jnp.int32).astype(jnp.float32)
        twice = 2.0 * sigma * sigma

        def bell(d, reach, scale):
            square = (d * d).astype(jnp.float32)
            return jnp.where(jnp.abs(d) <= reach, jnp.exp(-square / scale), 0.0)

        norm = jnp.zeros((8, DEPTH), jnp.float32)
        for d in range(-HW, HW + 1):
            at = lat * CX + sub + d
            norm += jnp.where((at >= 0) & (at < CX * n_lat), jnp.exp(-float(d * d) / twice), 0.0)
        wx = bell(place - sub, HW, twice) / norm
        for zv in range(CZ // 8):
            norm = jnp.zeros((8, DEPTH), jnp.float32)
            zz = sub + 8 * zv
            for d in range(-HZ, HZ + 1):
                at = rad * CZ + zz + d
                norm += jnp.where((at >= 0) & (at < CZ * n_rad), float(np.exp(-d * d / 4.5)), 0.0)
            kern_w[zv * 8 : zv * 8 + 8, :] = bell(zc - HZ - zz, HZ, 4.5) / norm
        for xx in range(CX):
            both = kern_w[...] * wx[xx : xx + 1, :]
            high = both.astype(jnp.bfloat16)
            whi_ref[xx * CZ : xx * CZ + CZ, :] = high
            wlo_ref[xx * CZ : xx * CZ + CZ, :] = (both - high.astype(jnp.float32)).astype(jnp.bfloat16)

    kern_w = compact_ref.at[pl.ds(0, CZ)]
    weights()

    def lists():
        @pl.loop(1, n_lat)
        def _(step):
            index_take(step).wait_recv()

        elements = index_ref.shape[2]
        shape = (n_lat, elements)
        rel = index_ref[:, 0, :] - lat
        x0 = index_ref[:, 1, :]
        zq = index_ref[:, 2, :] - rad * CZ + HZ + 8
        y0 = index_ref[:, 3, :]
        keep = (rel >= -1) & (rel <= 1) & (zq >= 4) & (zq < WINDOW + 8)
        before = lax.broadcasted_iota(jnp.int32, (elements, elements), 0) < lax.broadcasted_iota(jnp.int32, (elements, elements), 1)
        flags = jnp.where(keep, 1.0, 0.0)
        rank = jnp.dot(flags.astype(jnp.bfloat16), jnp.where(before, 1.0, 0.0).astype(jnp.bfloat16), preferred_element_type=jnp.float32)
        total = jnp.sum(flags, axis=1, keepdims=True).astype(jnp.int32)
        rank = jnp.where(keep, rank, -1.0)
        low = jnp.maximum(x0, jnp.where(rel < 0, HW, 0))
        high = jnp.minimum(x0 + 4, jnp.where(rel > 0, HW - 1, CX - 1))
        code = low + 8 * (high - low + 1)
        lane = lax.broadcasted_iota(jnp.int32, shape, 1)
        fields = [lane, zq, y0, x0, code, jnp.where(rel == 0, 0, 1)]
        fields = [jnp.where(keep, f, 0).astype(jnp.float32) for f in fields]
        slot = lax.broadcasted_iota(jnp.int32, (elements, elements), 0).astype(jnp.float32)
        zero = jnp.zeros((1, elements), jnp.float32)
        for i in range(n_lat):
            stack = jnp.concatenate([f[i : i + 1] for f in fields] + [zero, zero], axis=0).astype(jnp.bfloat16)
            pick = jnp.where(rank[i : i + 1] == slot, 1.0, 0.0).astype(jnp.bfloat16)
            compact_ref[8 * i : 8 * i + 8, :elements] = lax.dot_general(
                stack, pick, (((1,), (1,)), ((), ())), preferred_element_type=jnp.float32)

        def field(f):
            return jnp.concatenate([compact_ref[8 * i + f : 8 * i + f + 1, :elements] for i in range(n_lat)], axis=0).astype(jnp.int32)

        e, zq, y0, x0, code, beside = [field(f) for f in range(6)]
        start = e * NGLL
        row = lax.broadcasted_iota(jnp.int32, shape, 0) * block + 3 * lax.shift_right_logical(start, 7)
        off = start & (LANES - 1)
        words = row | (off << 16) | (((off - 25 * x0) & (LANES - 1)) << 23)
        words_ref[0] = jnp.where(lane == elements - 1, total, words)
        zb = jnp.maximum(lax.shift_right_logical(zq, 2) - 1, 0)
        at = ((beside * Z_BINS + zb) * Y_TILES + lax.shift_right_logical(y0, 4)) * 8
        words_ref[1] = at | ((zq & 7) << 16) | ((y0 & 15) << 20) | (code << 24)

    def when_there(d, up, body):
        zi = z - d if up else z + d

        @pl.when((zi >= 0) & (zi < levels))
        def _():
            body(2 * zi)

    def line(d, up, j):
        def body(i):
            i = i + x
            z_move(i, j, up).wait_recv()

            @pl.when(can_up if up else can_down)
            def _():
                z_move(i, j, up).start()

            x_move(i, j).start()
            if j == 0:
                y_move(i, "send").start()
            k_move(i, j, spans).start()

        when_there(d, up, body)

    def cross(d, up, j):
        def body(i):
            i = i + 1 - x
            x_move(i, j).wait_recv()
            if j == 0:
                y_move(i, "send").start()
            k_move(i, j, spans).start()

        when_there(d, up, body)

    def y_done(d, up, column):
        def body(i):
            i = i + column
            y_move(i, "take").wait_recv()
            k_move(i, 2, spans).start()

        when_there(d, up, body)

    ways = lambda d: (True, False) if d else (True,)
    for d in range(1, levels + 2):
        for j in range(2):
            if d < levels:
                for up in ways(d):
                    line(d, up, j)
            if d - 1 < levels:
                for up in ways(d - 1):
                    cross(d - 1, up, j)
            if j == 0 and d == 1:
                lists()
            if j == 0 and 1 <= d - 1 < levels:
                for up in ways(d - 1):
                    y_done(d - 1, up, x)
            if j == 0 and 0 <= d - 2 < levels:
                for up in ways(d - 2):
                    y_done(d - 2, up, 1 - x)

    @pl.loop(1, n_lat)
    def _(step):
        index_move(step).wait_send()

    @pl.loop(0, n_lat)
    def _(i):
        @pl.when(i != lat)
        def _():
            for j in range(3):
                k_move(i, j, other).wait_recv()
                k_move(i, j, spans).wait_send()
            y_move(i, "send").wait_send()

    @pl.loop(0, levels)
    def _(zi):
        i = 2 * zi + x
        for j in range(2):
            x_move(i, j).wait_send()

            @pl.when(can_up & (zi <= z))
            def _():
                z_move(i, j, True).wait_send()

            @pl.when(can_down & (zi >= z))
            def _():
                z_move(i, j, False).wait_send()


def grid_kernel(n_lat, words_ref, data_ref, whi_ref, wlo_ref, ghi_hbm, glo_hbm, out_hbm, acc0, acc1, acc2, field, result, words, ghi_ref, glo_ref, sem, smooth_sem, out_sem):
    accs = (acc0, acc1, acc2)
    smooth = [pltpu.make_async_copy(ghi_hbm, ghi_ref, smooth_sem.at[0]), pltpu.make_async_copy(glo_hbm, glo_ref, smooth_sem.at[1])]
    bring = pltpu.make_async_copy(words_ref, words, sem)
    bring.start()
    for copy in smooth:
        copy.start()
    rows = acc0.shape[0]

    @pl.loop(0, rows // 8, unroll=11)
    def _(r):
        for acc in accs:
            acc[pl.ds(pl.multiple_of(r * 8, 8), 8), :] = jnp.zeros((8, LANES), jnp.float32)

    bring.wait()
    lane = lax.broadcasted_iota(jnp.int32, (8, LANES), 1)
    sub = lax.broadcasted_iota(jnp.int32, (8, LANES), 0)
    across = lane & 15
    along = lax.shift_right_logical(lane, 4)
    ramp = 25 * along
    elements = words.shape[2]

    @pl.loop(0, n_lat)
    def _(i):
        count = words[0, i, elements - 1]

        @pl.loop(0, lax.div(count + SUM_WAYS - 1, SUM_WAYS))
        def _(step):
            for u in range(SUM_WAYS):
                p = step * SUM_WAYS + u
                w0, w1 = words[0, i, p], words[1, i, p]
                row = w0 & 0xFFFF
                off = lax.shift_right_logical(w0, 16) & 127
                shift = lax.shift_right_logical(w0, 23)
                at = pl.multiple_of(w1 & 0xFFFF, 8)
                zq = lax.shift_right_logical(w1, 16) & 7
                yl = lax.shift_right_logical(w1, 20) & 15
                low = lax.shift_right_logical(w1, 24) & 7
                wide = lax.shift_right_logical(w1, 27)
                tz = (sub - zq) & 7
                ty = (lane - yl) & 15
                tx = along - low
                index = (ramp + shift + 5 * tz + ty) & (LANES - 1)
                good = (tz < 5) & (ty < 5) & (tx >= 0) & (tx < wide)
                first = across >= yl
                here, there = good & first, good & jnp.logical_not(first)
                head = lane >= off
                for c in range(3):
                    a = jnp.broadcast_to(data_ref[pl.ds(row + c, 1), :], (8, LANES))
                    b = jnp.broadcast_to(data_ref[pl.ds(row + 3 + c, 1), :], (8, LANES))
                    v = jnp.take_along_axis(jnp.where(head, a, b), index, axis=1, mode="promise_in_bounds")
                    accs[c][pl.ds(at, 8), :] += jnp.where(here, v, 0.0)
                    accs[c][pl.ds(at + 8, 8), :] += jnp.where(there, v, 0.0)

    low_half = sub < 4
    for copy in smooth:
        copy.wait()
    for c in range(3):
        acc = accs[c]

        @pl.loop(0, 2)
        def _(g):
            @pl.loop(0, WINDOW // 8)
            def _(h):
                for side in range(2):
                    v = []
                    for t in range(8):
                        def bins(n):
                            r = ((g * Z_BINS + 2 * h + n) * Y_TILES + side * 8 + t) * 8
                            return acc[pl.ds(pl.multiple_of(r, 8), 8), :]

                        v.append(bins(1) + jnp.where(low_half, bins(0), bins(2)))
                    for bit in (4, 2, 1):
                        straight = (along & bit) == 0
                        w = list(v)
                        for r in range(8):
                            if r & bit:
                                continue
                            a, b = v[r], v[r + bit]
                            if bit == 4:
                                turned = pltpu.roll(jnp.where(straight, b, a), 64, 1)
                                w[r] = jnp.where(straight, a, turned)
                                w[r + bit] = jnp.where(straight, turned, b)
                            else:
                                w[r] = jnp.where(straight, a, pltpu.roll(b, 16 * bit, 1))
                                w[r + bit] = jnp.where(straight, pltpu.roll(a, LANES - 16 * bit, 1), b)
                        v = w
                    for xl in range(8):
                        r = pl.multiple_of(g * (CX * WINDOW) + xl * WINDOW + h * 8, 8)
                        field[pl.ds(r, 8), side * LANES : (side + 1) * LANES] = v[xl]

        def split(a):
            high = a.astype(jnp.bfloat16)
            return high, (a - high.astype(jnp.float32)).astype(jnp.bfloat16)

        def dot(a, b):
            return jnp.dot(a, b, preferred_element_type=jnp.float32)

        high, low = split(field[...])
        whi = whi_ref[...]
        mixed = dot(whi, high) + dot(wlo_ref[...], high) + dot(whi, low)
        high, low = split(mixed)
        ghi = ghi_ref[...]
        done = dot(high, ghi) + dot(low, ghi) + dot(high, glo_ref[...])
        result[c] = done.reshape(CX, CZ, NY)
        pltpu.make_async_copy(result.at[c], out_hbm.at[c], out_sem.at[c]).start()
    for c in range(3):
        pltpu.make_async_copy(result.at[c], out_hbm.at[c], out_sem.at[c]).wait()


def on_device_whole(n_lat, n_rad, kernels, cells, tiles, width_class):
    elements = tiles.shape[0]
    block = -(-kernels.shape[1] // LANES * 3 // 16) * 16
    smem = pl.BlockSpec(memory_space=pltpu.SMEM)
    vmem = pl.BlockSpec(memory_space=pltpu.VMEM)
    hbm = pl.BlockSpec(memory_space=pltpu.HBM)
    dma = pltpu.SemaphoreType.DMA
    data, words, whi, wlo = pl.pallas_call(
        functools.partial(gather_kernel, n_lat, n_rad, block),
        out_shape=[
            jax.ShapeDtypeStruct((n_lat * block + 8, LANES), jnp.float32),
            jax.ShapeDtypeStruct((2, n_lat, elements), jnp.int32),
            jax.ShapeDtypeStruct((CX * CZ, DEPTH), jnp.bfloat16),
            jax.ShapeDtypeStruct((CX * CZ, DEPTH), jnp.bfloat16),
        ],
        in_specs=[smem, hbm, hbm, hbm],
        out_specs=[vmem] * 4,
        scratch_shapes=[
            pltpu.VMEM(kernels.shape, jnp.float32),
            pltpu.VMEM((1, elements), jnp.int32),
            pltpu.VMEM(cells.shape, jnp.int32),
            pltpu.VMEM((n_lat, 8, elements), jnp.int32),
            pltpu.VMEM((8 * n_lat, DEPTH), jnp.float32),
            dma((3,)), dma((n_lat,)), dma((n_lat,)),
            dma((n_lat, 4)), dma((n_lat, 2)), dma((n_lat, 2)), dma((n_lat, 2)),
            dma((n_lat,)), dma((n_lat,)), dma((n_lat, 3)), dma((n_lat, 3)),
        ],
        compiler_params=pltpu.CompilerParams(
            vmem_limit_bytes=VMEM_LIMIT, collective_id=0, has_side_effects=True
        ),
    )(width_class, tiles.reshape(1, elements), cells, kernels)
    smooth = band_matrix(NY, 2.5, HY).T.astype(np.float32)
    high = smooth.astype(jnp.bfloat16)
    low = (smooth - high.astype(np.float32)).astype(jnp.bfloat16)
    rows = 2 * Z_BINS * Y_TILES * 8
    return pl.pallas_call(
        functools.partial(grid_kernel, n_lat),
        out_shape=jax.ShapeDtypeStruct((3, CX, CZ, NY), jnp.float32),
        in_specs=[vmem] * 4 + [hbm] * 2,
        out_specs=hbm,
        scratch_shapes=[
            pltpu.VMEM((rows, LANES), jnp.float32),
            pltpu.VMEM((rows, LANES), jnp.float32),
            pltpu.VMEM((rows, LANES), jnp.float32),
            pltpu.VMEM((DEPTH, NY), jnp.float32),
            pltpu.VMEM((3, CX, CZ, NY), jnp.float32),
            pltpu.SMEM((2, n_lat, elements), jnp.int32),
            pltpu.VMEM((NY, NY), jnp.bfloat16),
            pltpu.VMEM((NY, NY), jnp.bfloat16),
            dma, dma((2,)), dma((3,)),
        ],
        compiler_params=pltpu.CompilerParams(vmem_limit_bytes=VMEM_LIMIT),
    )(words, data, whi, wlo, jnp.asarray(high), jnp.asarray(low))


def solution(mesh):
    n_lat, n_rad = mesh.shape["lat"], mesh.shape["rad"]
    whole = n_lat <= 8 and n_lat % 2 == 0 and n_rad == 4
    return jax.shard_map(
        functools.partial(on_device_whole if whole else on_device, n_lat, n_rad),
        mesh=mesh,
        in_specs=(P(None, "lat"), P(None, "lat"), P("lat", None), P("lat")),
        out_specs=P(None, "lat", "rad", None),
        check_vma=False,
    )
```

```python
import functools

import jax
import jax.numpy as jnp
import numpy as np
from jax import lax
from jax.experimental import pallas as pl
from jax.experimental.pallas import tpu as pltpu
from jax.sharding import PartitionSpec as P

CX = 8
NY = 256
CZ = 32
NGLL = 125
HW = 4
HY = 8
HZ = 4
ZP = CZ + 4 * HZ
LANES = 128
TAPS = 2 * HZ + 1
PADX = CX + 2 * HW
PACK_UNROLL = 4
SUM_UNROLL = 4
VMEM_LIMIT = 48 * 2**20
MESH = pl.DeviceIdType.MESH


def band_matrix(count, sigma, half):
    place = np.arange(count)
    gap = place[None, :] - place[:, None]
    gauss = np.where(np.abs(gap) <= half, np.exp(-(gap**2) / (2.0 * sigma**2)), 0.0)
    return gauss / gauss.sum(axis=1, keepdims=True)


def z_taps(n_rad):
    full = np.pad(band_matrix(CZ * n_rad, 1.5, HZ), ((0, 0), (HZ, HZ)))
    return np.stack([full[z, z : z + TAPS] for z in range(CZ * n_rad)]).astype(np.float32)


def pack_kernel(
    n_lat, n_rad, share, elements, tiles_ref, cells_hbm, kern_hbm, out_ref, count, todo, place, cells_ref, kern_ref, sems
):
    slab = lax.axis_index("rad")
    rows = elements * NGLL // LANES
    bring_cells = pltpu.make_async_copy(cells_hbm, cells_ref, sems.at[0])
    bring_kern = pltpu.make_async_copy(kern_hbm, kern_ref, sems.at[1])
    bring_cells.start()
    bring_kern.start()
    out_ref[...] = jnp.full(out_ref.shape, -1000.0, jnp.float32)
    lane = lax.broadcasted_iota(jnp.int32, (3, LANES), 1)

    @pl.loop(0, n_lat)
    def _(t):
        count[t] = 0

    def listed(e, n):
        t = tiles_ref[e]
        rank = count[t]
        count[t] = rank + 1
        slot = lax.div(rank, n_rad)
        todo[n] = e
        place[n] = t * share + slot
        return n + jnp.where(rank - slot * n_rad == slab, 1, 0)

    n = lax.fori_loop(0, elements, listed, 0, unroll=4)
    for more in range(PACK_UNROLL):
        todo[n + more] = 0
        place[n + more] = n_lat * share
    bring_cells.wait()
    bring_kern.wait()

    def packed(step, _):
        for u in range(PACK_UNROLL):
            e = todo[step * PACK_UNROLL + u]
            at = place[step * PACK_UNROLL + u]
            start = e * NGLL
            row = lax.shift_right_logical(start, 7)
            off = start & (LANES - 1)
            after = jnp.minimum(row + 1, rows - 1)
            a = kern_ref[:, pl.ds(pl.multiple_of(row * LANES, LANES), LANES)]
            b = kern_ref[:, pl.ds(pl.multiple_of(after * LANES, LANES), LANES)]
            v = pltpu.roll(jnp.where(lane >= off, a, b), (LANES - off) & (LANES - 1), 1)
            v = jnp.where(lane == NGLL, cells_ref[0, e].astype(jnp.float32), v)
            v = jnp.where(lane == NGLL + 1, cells_ref[1, e].astype(jnp.float32), v)
            v = jnp.where(lane == NGLL + 2, cells_ref[2, e].astype(jnp.float32), v)
            t = lax.div(at, share)
            slot = at - t * share
            for c in range(3):
                out_ref[t, pl.ds(c * share + slot, 1), :] = v[c : c + 1]
        return 0

    lax.fori_loop(0, lax.div(n + PACK_UNROLL - 1, PACK_UNROLL), packed, 0)


def exchange_kernel(n_lat, n_rad, send_ref, recv_ref, own_sem, send_sem, recv_sem, fwd_sem, got_sem):
    tile, slab = lax.axis_index("lat"), lax.axis_index("rad")
    barrier = pltpu.get_barrier_semaphore()

    @pl.loop(1, n_lat)
    def _(k):
        pl.semaphore_signal(barrier, inc=1, device_id=(lax.rem(tile + k, n_lat), slab), device_id_type=MESH)

    pair = slab + 1 - 2 * lax.rem(slab, 2)
    other = slab + 2 - 4 * lax.div(slab, 2)
    for peer in (pair, other):
        pl.semaphore_signal(barrier, inc=1, device_id=(tile, peer), device_id_type=MESH)
    pl.semaphore_wait(barrier, n_lat - 1 + 2)

    def across(k):
        to = lax.rem(tile + k, n_lat)
        return pltpu.make_async_remote_copy(
            src_ref=send_ref.at[to],
            dst_ref=recv_ref.at[slab, tile],
            send_sem=send_sem.at[k],
            recv_sem=recv_sem.at[k],
            device_id=(to, slab),
            device_id_type=MESH,
        )

    def share(k, of, to, way):
        block = recv_ref.at[of, lax.rem(tile + n_lat - k, n_lat)]
        return pltpu.make_async_remote_copy(
            src_ref=block,
            dst_ref=block,
            send_sem=fwd_sem.at[way, k],
            recv_sem=got_sem.at[way, k],
            device_id=(tile, to),
            device_id_type=MESH,
        )

    def forward(k):
        share(k, slab, other, 0).start()
        share(k, slab, pair, 1).start()

    def relay(k):
        share(k, other, other, 0).wait_recv()
        share(k, other, pair, 2).start()

    @pl.loop(1, n_lat)
    def _(k):
        across(k).start()

    own = pltpu.make_async_copy(send_ref.at[tile], recv_ref.at[slab, tile], own_sem)
    own.start()
    own.wait()
    forward(0)

    @pl.loop(1, n_lat)
    def _(k):
        across(k).wait_recv()
        forward(k)

    @pl.loop(0, n_lat)
    def _(k):
        relay(k)

    @pl.loop(0, n_lat)
    def _(k):
        share(k, pair, pair, 1).wait_recv()
        share(k, other + pair - slab, pair, 2).wait_recv()

    @pl.loop(1, n_lat)
    def _(k):
        across(k).wait_send()

    @pl.loop(0, n_lat)
    def _(k):
        share(k, slab, other, 0).wait_send()
        share(k, slab, pair, 1).wait_send()
        share(k, other, pair, 2).wait_send()


def sum_kernel(blocks, share, meta_ref, recv_ref, acc, todo):
    slab = lax.axis_index("rad")
    slots = blocks * share
    acc[...] = jnp.zeros(acc.shape, jnp.float32)
    lane = lax.broadcasted_iota(jnp.int32, (8, LANES), 1)
    sub = lax.broadcasted_iota(jnp.int32, (8, LANES), 0)
    ramp = 25 * sub + lane
    low = slab * CZ - 2 * HZ

    def listed(s, n):
        zb = meta_ref[slots + s] - low
        todo[n] = s
        return n + jnp.where((zb >= 0) & (zb < CZ + 3 * HZ), 1, 0)

    n = lax.fori_loop(0, slots, listed, 0, unroll=8)
    for more in range(SUM_UNROLL):
        todo[n + more] = 0

    def place(at, values, index, mask):
        for j in range(5):
            picked = jnp.where(mask, index + 5 * j, NGLL)
            for c in range(3):
                piece = jnp.take_along_axis(values[c], picked, axis=1, mode="promise_in_bounds")
                acc[pl.ds(pl.multiple_of(at + (3 * j + c) * 8, 8), 8), :] += piece

    def summed(step, _):
        later = []
        for u in range(SUM_UNROLL):
            s = todo[step * SUM_UNROLL + u]
            good = step * SUM_UNROLL + u < n
            x0 = jnp.clip(meta_ref[s], 0, CX - 5)
            zb = jnp.clip(meta_ref[slots + s] - low, 0, CZ + 3 * HZ - 1)
            y0 = jnp.clip(meta_ref[2 * slots + s], 0, NY - 5)
            block = lax.div(s, share)
            slot = s - block * share
            values = []
            for c in range(3):
                row = jnp.broadcast_to(recv_ref[block, pl.ds(c * share + slot, 1), :], (8, LANES))
                values.append(jnp.where(lane < NGLL, row, 0.0))
            half = lax.shift_right_logical(y0, 7)
            yl = y0 & (LANES - 1)
            index = ramp - (25 * x0 + yl)
            rows = (sub >= x0) & (sub < jnp.where(good, x0 + 5, 0))
            at = (half * ZP + zb) * 24
            place(at, values, index, rows & (lane >= yl) & (lane < yl + 5))
            later.append((at, values, index, rows, yl))
        widest = functools.reduce(jnp.maximum, [entry[4] for entry in later])

        @pl.when(widest > LANES - 5)
        def _():
            for at, values, index, rows, yl in later:
                over = rows & (lane < yl + 5 - LANES)

                @pl.when(yl > LANES - 5)
                def _():
                    place(at + ZP * 24, values, index + LANES, over)

        return 0

    lax.fori_loop(0, lax.div(n + SUM_UNROLL - 1, SUM_UNROLL), summed, 0)


def finish_kernel(n_lat, taps_ref, wx_ref, acc, wy_ref, out_ref, planes, rows_ref, send_sem, recv_sem):
    tile, slab = lax.axis_index("lat"), lax.axis_index("rad")
    barrier = pltpu.get_barrier_semaphore()
    has_prev, has_next = tile > 0, tile < n_lat - 1
    halo = HW * CZ

    @pl.when(has_prev)
    def _():
        pl.semaphore_signal(barrier, inc=1, device_id=(tile - 1, slab), device_id_type=MESH)

    @pl.when(has_next)
    def _():
        pl.semaphore_signal(barrier, inc=1, device_id=(tile + 1, slab), device_id_type=MESH)

    def at(c, row, count):
        return rows_ref.at[:, pl.ds(c * PADX * CZ + row, count), :]

    def to_next(c):
        return pltpu.make_async_remote_copy(
            src_ref=at(c, CX * CZ, halo),
            dst_ref=at(c, 0, halo),
            send_sem=send_sem.at[0, c],
            recv_sem=recv_sem.at[0, c],
            device_id=(tile + 1, slab),
            device_id_type=MESH,
        )

    def to_prev(c):
        return pltpu.make_async_remote_copy(
            src_ref=at(c, halo, halo),
            dst_ref=at(c, halo + CX * CZ, halo),
            send_sem=send_sem.at[1, c],
            recv_sem=recv_sem.at[1, c],
            device_id=(tile - 1, slab),
            device_id_type=MESH,
        )

    for c in range(3):

        @pl.loop(0, CZ, unroll=4)
        def _(z):
            for half in range(NY // LANES):
                total = jnp.zeros((CX, LANES), jnp.float32)
                for d in range(TAPS):
                    weight = taps_ref[(slab * CZ + z) * TAPS + d]
                    row = pl.multiple_of(((half * ZP + z + HZ + d) * 3 + c) * CX, 8)
                    total = total + weight * acc[pl.ds(row, CX), :]
                cols = slice(half * LANES, (half + 1) * LANES)
                planes[pl.ds(pl.multiple_of(z * CX, 8), CX), cols] = total

        product = jnp.dot(planes[...], wy_ref[...], precision=lax.Precision.HIGHEST)
        for z in range(CZ):
            for half in range(NY // LANES):
                piece = product[z * CX : (z + 1) * CX, half * LANES : (half + 1) * LANES]
                rows_ref[half, pl.ds(c * PADX * CZ + halo + z, CX, stride=CZ), :] = piece

        if c == 0:
            beside = jnp.minimum(tile, 1) + jnp.minimum(n_lat - 1 - tile, 1)
            pl.semaphore_wait(barrier, beside)

        @pl.when(has_next)
        def _():
            to_next(c).start()

        @pl.when(has_prev)
        def _():
            to_prev(c).start()

        zeros = jnp.zeros((NY // LANES, halo, LANES), jnp.float32)

        @pl.when(tile == 0)
        def _():
            rows_ref[:, c * PADX * CZ : c * PADX * CZ + halo, :] = zeros

        @pl.when(tile == n_lat - 1)
        def _():
            rows_ref[:, c * PADX * CZ + halo + CX * CZ : (c + 1) * PADX * CZ, :] = zeros

    for c in range(3):

        @pl.when(has_prev)
        def _():
            to_next(c).wait_recv()

        @pl.when(has_next)
        def _():
            to_prev(c).wait_recv()

        @pl.loop(0, CX)
        def _(x):
            for half in range(NY // LANES):
                total = jnp.zeros((CZ, LANES), jnp.float32)
                for d in range(2 * HW + 1):
                    row = pl.multiple_of(c * PADX * CZ + (x + d) * CZ, 8)
                    total = total + wx_ref[x * (2 * HW + 1) + d] * rows_ref[half, pl.ds(row, CZ), :]
                out_ref[c, x, :, half * LANES : (half + 1) * LANES] = total

    for c in range(3):

        @pl.when(has_next)
        def _():
            to_next(c).wait_send()

        @pl.when(has_prev)
        def _():
            to_prev(c).wait_send()


def x_weights(width_class, n_lat):
    rows = lax.axis_index("lat") * CX + jnp.arange(CX)
    sigma = 1.0 + 0.75 * width_class[0].astype(jnp.float32)
    offsets = jnp.arange(-HW, HW + 1)
    target = rows[:, None] + offsets[None, :]
    valid = (target >= 0) & (target < CX * n_lat)
    gauss = jnp.exp(-(offsets[None, :].astype(jnp.float32) ** 2) / (2.0 * sigma**2))
    gauss = jnp.where(valid, gauss, 0.0)
    return gauss / jnp.sum(gauss, axis=1, keepdims=True)


def on_device(n_lat, n_rad, kernels, cells, tiles, width_class):
    elements = tiles.shape[0]
    cap = max(2, 2 * elements // n_lat)
    share = -(-cap // n_rad)
    blocks = n_rad * n_lat
    slots = blocks * share
    params = pltpu.CompilerParams(vmem_limit_bytes=VMEM_LIMIT)
    smem = pl.BlockSpec(memory_space=pltpu.SMEM)
    vmem = pl.BlockSpec(memory_space=pltpu.VMEM)
    hbm = pl.BlockSpec(memory_space=pl.ANY)
    send = pl.pallas_call(
        functools.partial(pack_kernel, n_lat, n_rad, share, elements),
        out_shape=jax.ShapeDtypeStruct((n_lat + 1, 3 * share, LANES), jnp.float32),
        in_specs=[smem, hbm, hbm],
        out_specs=vmem,
        scratch_shapes=[
            pltpu.SMEM((n_lat,), jnp.int32),
            pltpu.SMEM((elements + PACK_UNROLL,), jnp.int32),
            pltpu.SMEM((elements + PACK_UNROLL,), jnp.int32),
            pltpu.SMEM(cells.shape, jnp.int32),
            pltpu.VMEM(kernels.shape, jnp.float32),
            pltpu.SemaphoreType.DMA((2,)),
        ],
        compiler_params=params,
    )(tiles.reshape(-1), cells, kernels)
    recv = pl.pallas_call(
        functools.partial(exchange_kernel, n_lat, n_rad),
        out_shape=jax.ShapeDtypeStruct((n_rad, n_lat, 3 * share, LANES), jnp.float32),
        in_specs=[vmem],
        out_specs=vmem,
        scratch_shapes=[
            pltpu.SemaphoreType.DMA,
            pltpu.SemaphoreType.DMA((n_lat,)),
            pltpu.SemaphoreType.DMA((n_lat,)),
            pltpu.SemaphoreType.DMA((3, n_lat)),
            pltpu.SemaphoreType.DMA((3, n_lat)),
        ],
        compiler_params=pltpu.CompilerParams(
            vmem_limit_bytes=VMEM_LIMIT, collective_id=0, has_side_effects=True
        ),
    )(send)
    recv = recv.reshape(blocks, 3 * share, LANES)
    meta = recv[:, :share, NGLL:].transpose(2, 0, 1).reshape(-1).astype(jnp.int32)
    grid_rows = NY // LANES * ZP * 24
    summed = pl.pallas_call(
        functools.partial(sum_kernel, blocks, share),
        out_shape=jax.ShapeDtypeStruct((grid_rows, LANES), jnp.float32),
        in_specs=[smem, vmem],
        out_specs=vmem,
        scratch_shapes=[pltpu.SMEM((slots + SUM_UNROLL,), jnp.int32)],
        compiler_params=params,
    )(meta, recv)
    return pl.pallas_call(
        functools.partial(finish_kernel, n_lat),
        out_shape=jax.ShapeDtypeStruct((3, CX, CZ, NY), jnp.float32),
        in_specs=[smem, smem, vmem, vmem],
        out_specs=vmem,
        scratch_shapes=[
            pltpu.VMEM((CZ * CX, NY), jnp.float32),
            pltpu.VMEM((NY // LANES, 3 * PADX * CZ, LANES), jnp.float32),
            pltpu.SemaphoreType.DMA((2, 3)),
            pltpu.SemaphoreType.DMA((2, 3)),
        ],
        compiler_params=pltpu.CompilerParams(
            vmem_limit_bytes=VMEM_LIMIT, collective_id=1, has_side_effects=True
        ),
    )(
        jnp.asarray(z_taps(n_rad).reshape(-1)),
        x_weights(width_class, n_lat).reshape(-1),
        summed,
        jnp.asarray(band_matrix(NY, 2.5, HY).T.astype(np.float32)),
    )

ROW_TILES = 3
Z_BINS = 11
Y_TILES = 17
WINDOW = CZ + 2 * HZ
DEPTH = 2 * CX * WINDOW
SUM_WAYS = 16


def gather_kernel(n_lat, n_rad, block, width_ref, tiles_hbm, cells_hbm, kern_hbm, data_ref, words_ref, whi_ref, wlo_ref,
                  kern_ref, tiles_ref, cells_ref, index_ref, compact_ref, in_sem, is_sem, ir_sem, zs, zr, xs, xr, ys, yr, bs, br):
    lat, rad = lax.axis_index("lat"), lax.axis_index("rad")
    levels = n_lat // 2
    z, x = lax.div(lat, 2), lax.rem(lat, 2)
    y, k = lax.div(rad, 2), lax.rem(rad, 2)
    across_x, across_y, across_k = lat + 1 - 2 * x, rad + 2 - 4 * y, rad + 1 - 2 * k
    barrier = pltpu.get_barrier_semaphore()

    @pl.loop(1, n_lat)
    def _(step):
        pl.semaphore_signal(barrier, inc=1, device_id=(lax.rem(lat + step, n_lat), rad), device_id_type=MESH)

    for peer in (across_y, across_k):
        pl.semaphore_signal(barrier, inc=1, device_id=(lat, peer), device_id_type=MESH)
    brought = [
        pltpu.make_async_copy(kern_hbm, kern_ref, in_sem.at[0]),
        pltpu.make_async_copy(tiles_hbm, tiles_ref, in_sem.at[1]),
        pltpu.make_async_copy(cells_hbm, cells_ref, in_sem.at[2]),
    ]
    for copy in brought:
        copy.start()

    half = block // 2
    edge = half // 8 // 3 * 8 + 8
    inner = half - 2 * edge
    mine = k * half
    spans = {"send": (mine + y * (edge + inner), edge), "inner": (mine + edge, inner), "take": (mine + (1 - y) * (edge + inner), edge)}
    theirs = (1 - k) * half
    other = {"send": (theirs + y * (edge + inner), edge), "inner": (theirs + edge, inner), "take": (theirs + (1 - y) * (edge + inner), edge)}
    parts = ("send", "inner")

    def piece(i, span):
        return data_ref.at[pl.ds(pl.multiple_of(i * block + span[0], 8), span[1])]

    def move(i, span, send_sem, recv_sem, device):
        return pltpu.make_async_remote_copy(
            src_ref=piece(i, span), dst_ref=piece(i, span), send_sem=send_sem, recv_sem=recv_sem,
            device_id=device, device_id_type=MESH)

    def z_move(i, j, up):
        return move(i, spans[parts[j]], zs.at[i, 2 * j + (0 if up else 1)], zr.at[i, j], (lat + (2 if up else -2), rad))

    def x_move(i, j):
        return move(i, spans[parts[j]], xs.at[i, j], xr.at[i, j], (across_x, rad))

    def y_move(i, name):
        return move(i, spans[name], ys.at[i], yr.at[i], (lat, across_y))

    def k_move(i, j, of):
        return move(i, of[("send", "inner", "take")[j]], bs.at[i, j], br.at[i, j], (lat, across_k))

    def index_move(step):
        to = lax.rem(lat + step, n_lat)
        return pltpu.make_async_remote_copy(
            src_ref=index_ref.at[lat], dst_ref=index_ref.at[lat], send_sem=is_sem.at[step], recv_sem=ir_sem.at[step],
            device_id=(to, rad), device_id_type=MESH)

    def index_take(step):
        whose = index_ref.at[lax.rem(lat + n_lat - step, n_lat)]
        return pltpu.make_async_remote_copy(
            src_ref=whose, dst_ref=whose, send_sem=is_sem.at[step], recv_sem=ir_sem.at[step],
            device_id=(lax.rem(lat + step, n_lat), rad), device_id_type=MESH)

    can_up, can_down = z < levels - 1, z > 0
    brought[1].wait()
    brought[2].wait()
    index_ref[lat] = jnp.concatenate([tiles_ref[...], cells_ref[...], jnp.zeros((4, tiles_ref.shape[1]), jnp.int32)], axis=0)
    brought[0].wait()
    base = pl.multiple_of(lat * block, 8)
    lane_tiles = kern_ref.shape[1] // LANES
    groups = lane_tiles // 8

    def packed(at, row, count):
        rows = [kern_ref[:, pl.ds(pl.multiple_of(at + u * LANES, LANES), LANES)] for u in range(count)]
        return jnp.concatenate(rows, axis=0)

    @pl.loop(0, groups, unroll=4)
    def _(g):
        data_ref[pl.ds(base + pl.multiple_of(g * 24, 8), 24), :] = packed(g * 8 * LANES, 0, 8)

    left = lane_tiles - groups * 8
    if left:
        tail = packed(groups * 8 * LANES, 0, left)
        room = block - groups * 24
        tail = jnp.concatenate([tail, jnp.zeros((room - 3 * left, LANES), jnp.float32)], axis=0)
        data_ref[pl.ds(base + groups * 24, room), :] = tail
    pl.semaphore_wait(barrier, n_lat - 1 + 2)

    @pl.loop(1, n_lat)
    def _(step):
        index_move(step).start()

    for j in range(2):
        @pl.when(can_up)
        def _():
            z_move(lat, j, True).start()

        @pl.when(can_down)
        def _():
            z_move(lat, j, False).start()

        x_move(lat, j).start()

    def weights():
        col = lax.broadcasted_iota(jnp.int32, (8, DEPTH), 1)
        beside = col >= CX * WINDOW
        rest = jnp.where(beside, col - CX * WINDOW, col)
        xl = lax.shift_right_logical(rest * 1639, 16)
        zc = rest - WINDOW * xl
        place = jnp.where(beside, jnp.where(xl < HW, xl + CX, xl - CX), xl)
        sub = lax.broadcasted_iota(jnp.int32, (8, DEPTH), 0)
        sigma = 1.0 + 0.75 * jnp.full((8, DEPTH), width_ref[0], jnp.int32).astype(jnp.float32)
        twice = 2.0 * sigma * sigma

        def bell(d, reach, scale):
            square = (d * d).astype(jnp.float32)
            return jnp.where(jnp.abs(d) <= reach, jnp.exp(-square / scale), 0.0)

        norm = jnp.zeros((8, DEPTH), jnp.float32)
        for d in range(-HW, HW + 1):
            at = lat * CX + sub + d
            norm += jnp.where((at >= 0) & (at < CX * n_lat), jnp.exp(-float(d * d) / twice), 0.0)
        wx = bell(place - sub, HW, twice) / norm
        for zv in range(CZ // 8):
            norm = jnp.zeros((8, DEPTH), jnp.float32)
            zz = sub + 8 * zv
            for d in range(-HZ, HZ + 1):
                at = rad * CZ + zz + d
                norm += jnp.where((at >= 0) & (at < CZ * n_rad), float(np.exp(-d * d / 4.5)), 0.0)
            kern_w[zv * 8 : zv * 8 + 8, :] = bell(zc - HZ - zz, HZ, 4.5) / norm
        for xx in range(CX):
            both = kern_w[...] * wx[xx : xx + 1, :]
            high = both.astype(jnp.bfloat16)
            whi_ref[xx * CZ : xx * CZ + CZ, :] = high
            wlo_ref[xx * CZ : xx * CZ + CZ, :] = (both - high.astype(jnp.float32)).astype(jnp.bfloat16)

    kern_w = compact_ref.at[pl.ds(0, CZ)]
    weights()

    def lists():
        @pl.loop(1, n_lat)
        def _(step):
            index_take(step).wait_recv()

        elements = index_ref.shape[2]
        shape = (n_lat, elements)
        rel = index_ref[:, 0, :] - lat
        x0 = index_ref[:, 1, :]
        zq = index_ref[:, 2, :] - rad * CZ + HZ + 8
        y0 = index_ref[:, 3, :]
        keep = (rel >= -1) & (rel <= 1) & (zq >= 4) & (zq < WINDOW + 8)
        before = lax.broadcasted_iota(jnp.int32, (elements, elements), 0) < lax.broadcasted_iota(jnp.int32, (elements, elements), 1)
        flags = jnp.where(keep, 1.0, 0.0)
        rank = jnp.dot(flags.astype(jnp.bfloat16), jnp.where(before, 1.0, 0.0).astype(jnp.bfloat16), preferred_element_type=jnp.float32)
        total = jnp.sum(flags, axis=1, keepdims=True).astype(jnp.int32)
        rank = jnp.where(keep, rank, -1.0)
        low = jnp.maximum(x0, jnp.where(rel < 0, HW, 0))
        high = jnp.minimum(x0 + 4, jnp.where(rel > 0, HW - 1, CX - 1))
        code = low + 8 * (high - low + 1)
        lane = lax.broadcasted_iota(jnp.int32, shape, 1)
        fields = [lane, zq, y0, x0, code, jnp.where(rel == 0, 0, 1)]
        fields = [jnp.where(keep, f, 0).astype(jnp.float32) for f in fields]
        slot = lax.broadcasted_iota(jnp.int32, (elements, elements), 0).astype(jnp.float32)
        zero = jnp.zeros((1, elements), jnp.float32)
        for i in range(n_lat):
            stack = jnp.concatenate([f[i : i + 1] for f in fields] + [zero, zero], axis=0).astype(jnp.bfloat16)
            pick = jnp.where(rank[i : i + 1] == slot, 1.0, 0.0).astype(jnp.bfloat16)
            compact_ref[8 * i : 8 * i + 8, :elements] = lax.dot_general(
                stack, pick, (((1,), (1,)), ((), ())), preferred_element_type=jnp.float32)

        def field(f):
            return jnp.concatenate([compact_ref[8 * i + f : 8 * i + f + 1, :elements] for i in range(n_lat)], axis=0).astype(jnp.int32)

        e, zq, y0, x0, code, beside = [field(f) for f in range(6)]
        start = e * NGLL
        row = lax.broadcasted_iota(jnp.int32, shape, 0) * block + 3 * lax.shift_right_logical(start, 7)
        off = start & (LANES - 1)
        words = row | (off << 16) | (((off - 25 * x0) & (LANES - 1)) << 23)
        words_ref[0] = jnp.where(lane == elements - 1, total, words)
        zb = jnp.maximum(lax.shift_right_logical(zq, 2) - 1, 0)
        at = ((beside * Z_BINS + zb) * Y_TILES + lax.shift_right_logical(y0, 4)) * 8
        words_ref[1] = at | ((zq & 7) << 16) | ((y0 & 15) << 20) | (code << 24)

    def when_there(d, up, body):
        zi = z - d if up else z + d

        @pl.when((zi >= 0) & (zi < levels))
        def _():
            body(2 * zi)

    def line(d, up, j):
        def body(i):
            i = i + x
            z_move(i, j, up).wait_recv()

            @pl.when(can_up if up else can_down)
            def _():
                z_move(i, j, up).start()

            x_move(i, j).start()
            if j == 0:
                y_move(i, "send").start()
            k_move(i, j, spans).start()

        when_there(d, up, body)

    def cross(d, up, j):
        def body(i):
            i = i + 1 - x
            x_move(i, j).wait_recv()
            if j == 0:
                y_move(i, "send").start()
            k_move(i, j, spans).start()

        when_there(d, up, body)

    def y_done(d, up, column):
        def body(i):
            i = i + column
            y_move(i, "take").wait_recv()
            k_move(i, 2, spans).start()

        when_there(d, up, body)

    ways = lambda d: (True, False) if d else (True,)
    for d in range(1, levels + 2):
        for j in range(2):
            if d < levels:
                for up in ways(d):
                    line(d, up, j)
            if d - 1 < levels:
                for up in ways(d - 1):
                    cross(d - 1, up, j)
            if j == 0 and d == 1:
                lists()
            if j == 0 and 1 <= d - 1 < levels:
                for up in ways(d - 1):
                    y_done(d - 1, up, x)
            if j == 0 and 0 <= d - 2 < levels:
                for up in ways(d - 2):
                    y_done(d - 2, up, 1 - x)

    @pl.loop(1, n_lat)
    def _(step):
        index_move(step).wait_send()

    @pl.loop(0, n_lat)
    def _(i):
        @pl.when(i != lat)
        def _():
            for j in range(3):
                k_move(i, j, other).wait_recv()
                k_move(i, j, spans).wait_send()
            y_move(i, "send").wait_send()

    @pl.loop(0, levels)
    def _(zi):
        i = 2 * zi + x
        for j in range(2):
            x_move(i, j).wait_send()

            @pl.when(can_up & (zi <= z))
            def _():
                z_move(i, j, True).wait_send()

            @pl.when(can_down & (zi >= z))
            def _():
                z_move(i, j, False).wait_send()


def grid_kernel(n_lat, words_ref, data_ref, whi_ref, wlo_ref, ghi_hbm, glo_hbm, out_hbm, acc0, acc1, acc2, field, result, words, ghi_ref, glo_ref, sem, smooth_sem, out_sem):
    accs = (acc0, acc1, acc2)
    smooth = [pltpu.make_async_copy(ghi_hbm, ghi_ref, smooth_sem.at[0]), pltpu.make_async_copy(glo_hbm, glo_ref, smooth_sem.at[1])]
    bring = pltpu.make_async_copy(words_ref, words, sem)
    bring.start()
    for copy in smooth:
        copy.start()
    rows = acc0.shape[0]

    @pl.loop(0, rows // 8, unroll=11)
    def _(r):
        for acc in accs:
            acc[pl.ds(pl.multiple_of(r * 8, 8), 8), :] = jnp.zeros((8, LANES), jnp.float32)

    bring.wait()
    lane = lax.broadcasted_iota(jnp.int32, (8, LANES), 1)
    sub = lax.broadcasted_iota(jnp.int32, (8, LANES), 0)
    across = lane & 15
    along = lax.shift_right_logical(lane, 4)
    ramp = 25 * along
    elements = words.shape[2]

    @pl.loop(0, n_lat)
    def _(i):
        count = words[0, i, elements - 1]

        @pl.loop(0, lax.div(count + SUM_WAYS - 1, SUM_WAYS))
        def _(step):
            for u in range(SUM_WAYS):
                p = step * SUM_WAYS + u
                w0, w1 = words[0, i, p], words[1, i, p]
                row = w0 & 0xFFFF
                off = lax.shift_right_logical(w0, 16) & 127
                shift = lax.shift_right_logical(w0, 23)
                at = pl.multiple_of(w1 & 0xFFFF, 8)
                zq = lax.shift_right_logical(w1, 16) & 7
                yl = lax.shift_right_logical(w1, 20) & 15
                low = lax.shift_right_logical(w1, 24) & 7
                wide = lax.shift_right_logical(w1, 27)
                tz = (sub - zq) & 7
                ty = (lane - yl) & 15
                tx = along - low
                index = (ramp + shift + 5 * tz + ty) & (LANES - 1)
                good = (tz < 5) & (ty < 5) & (tx >= 0) & (tx < wide)
                first = across >= yl
                here, there = good & first, good & jnp.logical_not(first)
                head = lane >= off
                for c in range(3):
                    a = jnp.broadcast_to(data_ref[pl.ds(row + c, 1), :], (8, LANES))
                    b = jnp.broadcast_to(data_ref[pl.ds(row + 3 + c, 1), :], (8, LANES))
                    v = jnp.take_along_axis(jnp.where(head, a, b), index, axis=1, mode="promise_in_bounds")
                    accs[c][pl.ds(at, 8), :] += jnp.where(here, v, 0.0)
                    accs[c][pl.ds(at + 8, 8), :] += jnp.where(there, v, 0.0)

    low_half = sub < 4
    for copy in smooth:
        copy.wait()
    for c in range(3):
        acc = accs[c]

        @pl.loop(0, 2, unroll=2)
        def _(g):
            @pl.loop(0, WINDOW // 8, unroll=WINDOW // 8)
            def _(h):
                for side in range(2):
                    v = []
                    for t in range(8):
                        def bins(n):
                            r = ((g * Z_BINS + 2 * h + n) * Y_TILES + side * 8 + t) * 8
                            return acc[pl.ds(pl.multiple_of(r, 8), 8), :]

                        v.append(bins(1) + jnp.where(low_half, bins(0), bins(2)))
                    for bit in (4, 2, 1):
                        straight = (along & bit) == 0
                        w = list(v)
                        for r in range(8):
                            if r & bit:
                                continue
                            a, b = v[r], v[r + bit]
                            if bit == 4:
                                turned = pltpu.roll(jnp.where(straight, b, a), 64, 1)
                                w[r] = jnp.where(straight, a, turned)
                                w[r + bit] = jnp.where(straight, turned, b)
                            else:
                                w[r] = jnp.where(straight, a, pltpu.roll(b, 16 * bit, 1))
                                w[r + bit] = jnp.where(straight, pltpu.roll(a, LANES - 16 * bit, 1), b)
                        v = w
                    for xl in range(8):
                        r = pl.multiple_of(g * (CX * WINDOW) + xl * WINDOW + h * 8, 8)
                        field[pl.ds(r, 8), side * LANES : (side + 1) * LANES] = v[xl]

        def split(a):
            high = a.astype(jnp.bfloat16)
            return high, (a - high.astype(jnp.float32)).astype(jnp.bfloat16)

        def dot(a, b):
            return jnp.dot(a, b, preferred_element_type=jnp.float32)

        high, low = split(field[...])
        whi = whi_ref[...]
        mixed = dot(whi, high) + dot(wlo_ref[...], high) + dot(whi, low)
        high, low = split(mixed)
        ghi = ghi_ref[...]
        done = dot(high, ghi) + dot(low, ghi) + dot(high, glo_ref[...])
        result[c] = done.reshape(CX, CZ, NY)
        pltpu.make_async_copy(result.at[c], out_hbm.at[c], out_sem.at[c]).start()
    for c in range(3):
        pltpu.make_async_copy(result.at[c], out_hbm.at[c], out_sem.at[c]).wait()


def on_device_whole(n_lat, n_rad, kernels, cells, tiles, width_class):
    elements = tiles.shape[0]
    block = -(-kernels.shape[1] // LANES * 3 // 16) * 16
    smem = pl.BlockSpec(memory_space=pltpu.SMEM)
    vmem = pl.BlockSpec(memory_space=pltpu.VMEM)
    hbm = pl.BlockSpec(memory_space=pltpu.HBM)
    dma = pltpu.SemaphoreType.DMA
    data, words, whi, wlo = pl.pallas_call(
        functools.partial(gather_kernel, n_lat, n_rad, block),
        out_shape=[
            jax.ShapeDtypeStruct((n_lat * block + 8, LANES), jnp.float32),
            jax.ShapeDtypeStruct((2, n_lat, elements), jnp.int32),
            jax.ShapeDtypeStruct((CX * CZ, DEPTH), jnp.bfloat16),
            jax.ShapeDtypeStruct((CX * CZ, DEPTH), jnp.bfloat16),
        ],
        in_specs=[smem, hbm, hbm, hbm],
        out_specs=[vmem] * 4,
        scratch_shapes=[
            pltpu.VMEM(kernels.shape, jnp.float32),
            pltpu.VMEM((1, elements), jnp.int32),
            pltpu.VMEM(cells.shape, jnp.int32),
            pltpu.VMEM((n_lat, 8, elements), jnp.int32),
            pltpu.VMEM((8 * n_lat, DEPTH), jnp.float32),
            dma((3,)), dma((n_lat,)), dma((n_lat,)),
            dma((n_lat, 4)), dma((n_lat, 2)), dma((n_lat, 2)), dma((n_lat, 2)),
            dma((n_lat,)), dma((n_lat,)), dma((n_lat, 3)), dma((n_lat, 3)),
        ],
        compiler_params=pltpu.CompilerParams(
            vmem_limit_bytes=VMEM_LIMIT, collective_id=0, has_side_effects=True
        ),
    )(width_class, tiles.reshape(1, elements), cells, kernels)
    smooth = band_matrix(NY, 2.5, HY).T.astype(np.float32)
    high = smooth.astype(jnp.bfloat16)
    low = (smooth - high.astype(np.float32)).astype(jnp.bfloat16)
    rows = 2 * Z_BINS * Y_TILES * 8
    return pl.pallas_call(
        functools.partial(grid_kernel, n_lat),
        out_shape=jax.ShapeDtypeStruct((3, CX, CZ, NY), jnp.float32),
        in_specs=[vmem] * 4 + [hbm] * 2,
        out_specs=hbm,
        scratch_shapes=[
            pltpu.VMEM((rows, LANES), jnp.float32),
            pltpu.VMEM((rows, LANES), jnp.float32),
            pltpu.VMEM((rows, LANES), jnp.float32),
            pltpu.VMEM((DEPTH, NY), jnp.float32),
            pltpu.VMEM((3, CX, CZ, NY), jnp.float32),
            pltpu.SMEM((2, n_lat, elements), jnp.int32),
            pltpu.VMEM((NY, NY), jnp.bfloat16),
            pltpu.VMEM((NY, NY), jnp.bfloat16),
            dma, dma((2,)), dma((3,)),
        ],
        compiler_params=pltpu.CompilerParams(vmem_limit_bytes=VMEM_LIMIT),
    )(words, data, whi, wlo, jnp.asarray(high), jnp.asarray(low))


def solution(mesh):
    n_lat, n_rad = mesh.shape["lat"], mesh.shape["rad"]
    whole = n_lat <= 8 and n_lat % 2 == 0 and n_rad == 4
    return jax.shard_map(
        functools.partial(on_device_whole if whole else on_device, n_lat, n_rad),
        mesh=mesh,
        in_specs=(P(None, "lat"), P(None, "lat"), P("lat", None), P("lat")),
        out_specs=P(None, "lat", "rad", None),
        check_vma=False,
    )
```

```python
import functools

import jax
import jax.numpy as jnp
import numpy as np
from jax import lax
from jax.experimental import pallas as pl
from jax.experimental.pallas import tpu as pltpu
from jax.sharding import PartitionSpec as P

CX = 8
NY = 256
CZ = 32
NGLL = 125
HW = 4
HY = 8
HZ = 4
ZP = CZ + 4 * HZ
LANES = 128
TAPS = 2 * HZ + 1
PADX = CX + 2 * HW
PACK_UNROLL = 4
SUM_UNROLL = 4
VMEM_LIMIT = 48 * 2**20
MESH = pl.DeviceIdType.MESH


def band_matrix(count, sigma, half):
    place = np.arange(count)
    gap = place[None, :] - place[:, None]
    gauss = np.where(np.abs(gap) <= half, np.exp(-(gap**2) / (2.0 * sigma**2)), 0.0)
    return gauss / gauss.sum(axis=1, keepdims=True)


def z_taps(n_rad):
    full = np.pad(band_matrix(CZ * n_rad, 1.5, HZ), ((0, 0), (HZ, HZ)))
    return np.stack([full[z, z : z + TAPS] for z in range(CZ * n_rad)]).astype(np.float32)


def pack_kernel(
    n_lat, n_rad, share, elements, tiles_ref, cells_hbm, kern_hbm, out_ref, count, todo, place, cells_ref, kern_ref, sems
):
    slab = lax.axis_index("rad")
    rows = elements * NGLL // LANES
    bring_cells = pltpu.make_async_copy(cells_hbm, cells_ref, sems.at[0])
    bring_kern = pltpu.make_async_copy(kern_hbm, kern_ref, sems.at[1])
    bring_cells.start()
    bring_kern.start()
    out_ref[...] = jnp.full(out_ref.shape, -1000.0, jnp.float32)
    lane = lax.broadcasted_iota(jnp.int32, (3, LANES), 1)

    @pl.loop(0, n_lat)
    def _(t):
        count[t] = 0

    def listed(e, n):
        t = tiles_ref[e]
        rank = count[t]
        count[t] = rank + 1
        slot = lax.div(rank, n_rad)
        todo[n] = e
        place[n] = t * share + slot
        return n + jnp.where(rank - slot * n_rad == slab, 1, 0)

    n = lax.fori_loop(0, elements, listed, 0, unroll=4)
    for more in range(PACK_UNROLL):
        todo[n + more] = 0
        place[n + more] = n_lat * share
    bring_cells.wait()
    bring_kern.wait()

    def packed(step, _):
        for u in range(PACK_UNROLL):
            e = todo[step * PACK_UNROLL + u]
            at = place[step * PACK_UNROLL + u]
            start = e * NGLL
            row = lax.shift_right_logical(start, 7)
            off = start & (LANES - 1)
            after = jnp.minimum(row + 1, rows - 1)
            a = kern_ref[:, pl.ds(pl.multiple_of(row * LANES, LANES), LANES)]
            b = kern_ref[:, pl.ds(pl.multiple_of(after * LANES, LANES), LANES)]
            v = pltpu.roll(jnp.where(lane >= off, a, b), (LANES - off) & (LANES - 1), 1)
            v = jnp.where(lane == NGLL, cells_ref[0, e].astype(jnp.float32), v)
            v = jnp.where(lane == NGLL + 1, cells_ref[1, e].astype(jnp.float32), v)
            v = jnp.where(lane == NGLL + 2, cells_ref[2, e].astype(jnp.float32), v)
            t = lax.div(at, share)
            slot = at - t * share
            for c in range(3):
                out_ref[t, pl.ds(c * share + slot, 1), :] = v[c : c + 1]
        return 0

    lax.fori_loop(0, lax.div(n + PACK_UNROLL - 1, PACK_UNROLL), packed, 0)


def exchange_kernel(n_lat, n_rad, send_ref, recv_ref, own_sem, send_sem, recv_sem, fwd_sem, got_sem):
    tile, slab = lax.axis_index("lat"), lax.axis_index("rad")
    barrier = pltpu.get_barrier_semaphore()

    @pl.loop(1, n_lat)
    def _(k):
        pl.semaphore_signal(barrier, inc=1, device_id=(lax.rem(tile + k, n_lat), slab), device_id_type=MESH)

    pair = slab + 1 - 2 * lax.rem(slab, 2)
    other = slab + 2 - 4 * lax.div(slab, 2)
    for peer in (pair, other):
        pl.semaphore_signal(barrier, inc=1, device_id=(tile, peer), device_id_type=MESH)
    pl.semaphore_wait(barrier, n_lat - 1 + 2)

    def across(k):
        to = lax.rem(tile + k, n_lat)
        return pltpu.make_async_remote_copy(
            src_ref=send_ref.at[to],
            dst_ref=recv_ref.at[slab, tile],
            send_sem=send_sem.at[k],
            recv_sem=recv_sem.at[k],
            device_id=(to, slab),
            device_id_type=MESH,
        )

    def share(k, of, to, way):
        block = recv_ref.at[of, lax.rem(tile + n_lat - k, n_lat)]
        return pltpu.make_async_remote_copy(
            src_ref=block,
            dst_ref=block,
            send_sem=fwd_sem.at[way, k],
            recv_sem=got_sem.at[way, k],
            device_id=(tile, to),
            device_id_type=MESH,
        )

    def forward(k):
        share(k, slab, other, 0).start()
        share(k, slab, pair, 1).start()

    def relay(k):
        share(k, other, other, 0).wait_recv()
        share(k, other, pair, 2).start()

    @pl.loop(1, n_lat)
    def _(k):
        across(k).start()

    own = pltpu.make_async_copy(send_ref.at[tile], recv_ref.at[slab, tile], own_sem)
    own.start()
    own.wait()
    forward(0)

    @pl.loop(1, n_lat)
    def _(k):
        across(k).wait_recv()
        forward(k)

    @pl.loop(0, n_lat)
    def _(k):
        relay(k)

    @pl.loop(0, n_lat)
    def _(k):
        share(k, pair, pair, 1).wait_recv()
        share(k, other + pair - slab, pair, 2).wait_recv()

    @pl.loop(1, n_lat)
    def _(k):
        across(k).wait_send()

    @pl.loop(0, n_lat)
    def _(k):
        share(k, slab, other, 0).wait_send()
        share(k, slab, pair, 1).wait_send()
        share(k, other, pair, 2).wait_send()


def sum_kernel(blocks, share, meta_ref, recv_ref, acc, todo):
    slab = lax.axis_index("rad")
    slots = blocks * share
    acc[...] = jnp.zeros(acc.shape, jnp.float32)
    lane = lax.broadcasted_iota(jnp.int32, (8, LANES), 1)
    sub = lax.broadcasted_iota(jnp.int32, (8, LANES), 0)
    ramp = 25 * sub + lane
    low = slab * CZ - 2 * HZ

    def listed(s, n):
        zb = meta_ref[slots + s] - low
        todo[n] = s
        return n + jnp.where((zb >= 0) & (zb < CZ + 3 * HZ), 1, 0)

    n = lax.fori_loop(0, slots, listed, 0, unroll=8)
    for more in range(SUM_UNROLL):
        todo[n + more] = 0

    def place(at, values, index, mask):
        for j in range(5):
            picked = jnp.where(mask, index + 5 * j, NGLL)
            for c in range(3):
                piece = jnp.take_along_axis(values[c], picked, axis=1, mode="promise_in_bounds")
                acc[pl.ds(pl.multiple_of(at + (3 * j + c) * 8, 8), 8), :] += piece

    def summed(step, _):
        later = []
        for u in range(SUM_UNROLL):
            s = todo[step * SUM_UNROLL + u]
            good = step * SUM_UNROLL + u < n
            x0 = jnp.clip(meta_ref[s], 0, CX - 5)
            zb = jnp.clip(meta_ref[slots + s] - low, 0, CZ + 3 * HZ - 1)
            y0 = jnp.clip(meta_ref[2 * slots + s], 0, NY - 5)
            block = lax.div(s, share)
            slot = s - block * share
            values = []
            for c in range(3):
                row = jnp.broadcast_to(recv_ref[block, pl.ds(c * share + slot, 1), :], (8, LANES))
                values.append(jnp.where(lane < NGLL, row, 0.0))
            half = lax.shift_right_logical(y0, 7)
            yl = y0 & (LANES - 1)
            index = ramp - (25 * x0 + yl)
            rows = (sub >= x0) & (sub < jnp.where(good, x0 + 5, 0))
            at = (half * ZP + zb) * 24
            place(at, values, index, rows & (lane >= yl) & (lane < yl + 5))
            later.append((at, values, index, rows, yl))
        widest = functools.reduce(jnp.maximum, [entry[4] for entry in later])

        @pl.when(widest > LANES - 5)
        def _():
            for at, values, index, rows, yl in later:
                over = rows & (lane < yl + 5 - LANES)

                @pl.when(yl > LANES - 5)
                def _():
                    place(at + ZP * 24, values, index + LANES, over)

        return 0

    lax.fori_loop(0, lax.div(n + SUM_UNROLL - 1, SUM_UNROLL), summed, 0)


def finish_kernel(n_lat, taps_ref, wx_ref, acc, wy_ref, out_ref, planes, rows_ref, send_sem, recv_sem):
    tile, slab = lax.axis_index("lat"), lax.axis_index("rad")
    barrier = pltpu.get_barrier_semaphore()
    has_prev, has_next = tile > 0, tile < n_lat - 1
    halo = HW * CZ

    @pl.when(has_prev)
    def _():
        pl.semaphore_signal(barrier, inc=1, device_id=(tile - 1, slab), device_id_type=MESH)

    @pl.when(has_next)
    def _():
        pl.semaphore_signal(barrier, inc=1, device_id=(tile + 1, slab), device_id_type=MESH)

    def at(c, row, count):
        return rows_ref.at[:, pl.ds(c * PADX * CZ + row, count), :]

    def to_next(c):
        return pltpu.make_async_remote_copy(
            src_ref=at(c, CX * CZ, halo),
            dst_ref=at(c, 0, halo),
            send_sem=send_sem.at[0, c],
            recv_sem=recv_sem.at[0, c],
            device_id=(tile + 1, slab),
            device_id_type=MESH,
        )

    def to_prev(c):
        return pltpu.make_async_remote_copy(
            src_ref=at(c, halo, halo),
            dst_ref=at(c, halo + CX * CZ, halo),
            send_sem=send_sem.at[1, c],
            recv_sem=recv_sem.at[1, c],
            device_id=(tile - 1, slab),
            device_id_type=MESH,
        )

    for c in range(3):

        @pl.loop(0, CZ, unroll=4)
        def _(z):
            for half in range(NY // LANES):
                total = jnp.zeros((CX, LANES), jnp.float32)
                for d in range(TAPS):
                    weight = taps_ref[(slab * CZ + z) * TAPS + d]
                    row = pl.multiple_of(((half * ZP + z + HZ + d) * 3 + c) * CX, 8)
                    total = total + weight * acc[pl.ds(row, CX), :]
                cols = slice(half * LANES, (half + 1) * LANES)
                planes[pl.ds(pl.multiple_of(z * CX, 8), CX), cols] = total

        product = jnp.dot(planes[...], wy_ref[...], precision=lax.Precision.HIGHEST)
        for z in range(CZ):
            for half in range(NY // LANES):
                piece = product[z * CX : (z + 1) * CX, half * LANES : (half + 1) * LANES]
                rows_ref[half, pl.ds(c * PADX * CZ + halo + z, CX, stride=CZ), :] = piece

        if c == 0:
            beside = jnp.minimum(tile, 1) + jnp.minimum(n_lat - 1 - tile, 1)
            pl.semaphore_wait(barrier, beside)

        @pl.when(has_next)
        def _():
            to_next(c).start()

        @pl.when(has_prev)
        def _():
            to_prev(c).start()

        zeros = jnp.zeros((NY // LANES, halo, LANES), jnp.float32)

        @pl.when(tile == 0)
        def _():
            rows_ref[:, c * PADX * CZ : c * PADX * CZ + halo, :] = zeros

        @pl.when(tile == n_lat - 1)
        def _():
            rows_ref[:, c * PADX * CZ + halo + CX * CZ : (c + 1) * PADX * CZ, :] = zeros

    for c in range(3):

        @pl.when(has_prev)
        def _():
            to_next(c).wait_recv()

        @pl.when(has_next)
        def _():
            to_prev(c).wait_recv()

        @pl.loop(0, CX)
        def _(x):
            for half in range(NY // LANES):
                total = jnp.zeros((CZ, LANES), jnp.float32)
                for d in range(2 * HW + 1):
                    row = pl.multiple_of(c * PADX * CZ + (x + d) * CZ, 8)
                    total = total + wx_ref[x * (2 * HW + 1) + d] * rows_ref[half, pl.ds(row, CZ), :]
                out_ref[c, x, :, half * LANES : (half + 1) * LANES] = total

    for c in range(3):

        @pl.when(has_next)
        def _():
            to_next(c).wait_send()

        @pl.when(has_prev)
        def _():
            to_prev(c).wait_send()


def x_weights(width_class, n_lat):
    rows = lax.axis_index("lat") * CX + jnp.arange(CX)
    sigma = 1.0 + 0.75 * width_class[0].astype(jnp.float32)
    offsets = jnp.arange(-HW, HW + 1)
    target = rows[:, None] + offsets[None, :]
    valid = (target >= 0) & (target < CX * n_lat)
    gauss = jnp.exp(-(offsets[None, :].astype(jnp.float32) ** 2) / (2.0 * sigma**2))
    gauss = jnp.where(valid, gauss, 0.0)
    return gauss / jnp.sum(gauss, axis=1, keepdims=True)


def on_device(n_lat, n_rad, kernels, cells, tiles, width_class):
    elements = tiles.shape[0]
    cap = max(2, 2 * elements // n_lat)
    share = -(-cap // n_rad)
    blocks = n_rad * n_lat
    slots = blocks * share
    params = pltpu.CompilerParams(vmem_limit_bytes=VMEM_LIMIT)
    smem = pl.BlockSpec(memory_space=pltpu.SMEM)
    vmem = pl.BlockSpec(memory_space=pltpu.VMEM)
    hbm = pl.BlockSpec(memory_space=pl.ANY)
    send = pl.pallas_call(
        functools.partial(pack_kernel, n_lat, n_rad, share, elements),
        out_shape=jax.ShapeDtypeStruct((n_lat + 1, 3 * share, LANES), jnp.float32),
        in_specs=[smem, hbm, hbm],
        out_specs=vmem,
        scratch_shapes=[
            pltpu.SMEM((n_lat,), jnp.int32),
            pltpu.SMEM((elements + PACK_UNROLL,), jnp.int32),
            pltpu.SMEM((elements + PACK_UNROLL,), jnp.int32),
            pltpu.SMEM(cells.shape, jnp.int32),
            pltpu.VMEM(kernels.shape, jnp.float32),
            pltpu.SemaphoreType.DMA((2,)),
        ],
        compiler_params=params,
    )(tiles.reshape(-1), cells, kernels)
    recv = pl.pallas_call(
        functools.partial(exchange_kernel, n_lat, n_rad),
        out_shape=jax.ShapeDtypeStruct((n_rad, n_lat, 3 * share, LANES), jnp.float32),
        in_specs=[vmem],
        out_specs=vmem,
        scratch_shapes=[
            pltpu.SemaphoreType.DMA,
            pltpu.SemaphoreType.DMA((n_lat,)),
            pltpu.SemaphoreType.DMA((n_lat,)),
            pltpu.SemaphoreType.DMA((3, n_lat)),
            pltpu.SemaphoreType.DMA((3, n_lat)),
        ],
        compiler_params=pltpu.CompilerParams(
            vmem_limit_bytes=VMEM_LIMIT, collective_id=0, has_side_effects=True
        ),
    )(send)
    recv = recv.reshape(blocks, 3 * share, LANES)
    meta = recv[:, :share, NGLL:].transpose(2, 0, 1).reshape(-1).astype(jnp.int32)
    grid_rows = NY // LANES * ZP * 24
    summed = pl.pallas_call(
        functools.partial(sum_kernel, blocks, share),
        out_shape=jax.ShapeDtypeStruct((grid_rows, LANES), jnp.float32),
        in_specs=[smem, vmem],
        out_specs=vmem,
        scratch_shapes=[pltpu.SMEM((slots + SUM_UNROLL,), jnp.int32)],
        compiler_params=params,
    )(meta, recv)
    return pl.pallas_call(
        functools.partial(finish_kernel, n_lat),
        out_shape=jax.ShapeDtypeStruct((3, CX, CZ, NY), jnp.float32),
        in_specs=[smem, smem, vmem, vmem],
        out_specs=vmem,
        scratch_shapes=[
            pltpu.VMEM((CZ * CX, NY), jnp.float32),
            pltpu.VMEM((NY // LANES, 3 * PADX * CZ, LANES), jnp.float32),
            pltpu.SemaphoreType.DMA((2, 3)),
            pltpu.SemaphoreType.DMA((2, 3)),
        ],
        compiler_params=pltpu.CompilerParams(
            vmem_limit_bytes=VMEM_LIMIT, collective_id=1, has_side_effects=True
        ),
    )(
        jnp.asarray(z_taps(n_rad).reshape(-1)),
        x_weights(width_class, n_lat).reshape(-1),
        summed,
        jnp.asarray(band_matrix(NY, 2.5, HY).T.astype(np.float32)),
    )

ROW_TILES = 3
Z_BINS = 11
Y_TILES = 17
WINDOW = CZ + 2 * HZ
DEPTH = 2 * CX * WINDOW
SUM_WAYS = 16


def gather_kernel(n_lat, n_rad, block, width_ref, tiles_hbm, cells_hbm, kern_hbm, data_ref, words_ref, whi_ref, wlo_ref,
                  kern_ref, tiles_ref, cells_ref, index_ref, compact_ref, in_sem, is_sem, ir_sem, zs, zr, xs, xr, ys, yr, bs, br):
    lat, rad = lax.axis_index("lat"), lax.axis_index("rad")
    levels = n_lat // 2
    z, x = lax.div(lat, 2), lax.rem(lat, 2)
    y, k = lax.div(rad, 2), lax.rem(rad, 2)
    across_x, across_y, across_k = lat + 1 - 2 * x, rad + 2 - 4 * y, rad + 1 - 2 * k
    barrier = pltpu.get_barrier_semaphore()

    @pl.loop(1, n_lat)
    def _(step):
        pl.semaphore_signal(barrier, inc=1, device_id=(lax.rem(lat + step, n_lat), rad), device_id_type=MESH)

    for peer in (across_y, across_k):
        pl.semaphore_signal(barrier, inc=1, device_id=(lat, peer), device_id_type=MESH)
    brought = [
        pltpu.make_async_copy(kern_hbm, kern_ref, in_sem.at[0]),
        pltpu.make_async_copy(tiles_hbm, tiles_ref, in_sem.at[1]),
        pltpu.make_async_copy(cells_hbm, cells_ref, in_sem.at[2]),
    ]
    for copy in brought:
        copy.start()

    half = block // 2
    edge = half // 8 // 3 * 8 + 8
    inner = half - 2 * edge
    mine = k * half
    spans = {"send": (mine + y * (edge + inner), edge), "inner": (mine + edge, inner), "take": (mine + (1 - y) * (edge + inner), edge)}
    parts = ("send", "inner")

    def piece(i, span):
        return data_ref.at[pl.ds(pl.multiple_of(i * block + span[0], 8), span[1])]

    def move(i, span, send_sem, recv_sem, device):
        return pltpu.make_async_remote_copy(
            src_ref=piece(i, span), dst_ref=piece(i, span), send_sem=send_sem, recv_sem=recv_sem,
            device_id=device, device_id_type=MESH)

    def z_move(i, j, up):
        return move(i, spans[parts[j]], zs.at[i, 0 if up else 1], zr.at[i, j], (lat + (2 if up else -2), rad))

    def x_move(i, j):
        return move(i, spans[parts[j]], xs.at[j], xr.at[i, j], (across_x, rad))

    def y_move(i, name):
        return move(i, spans[name], ys, yr.at[i], (lat, across_y))

    def k_move(i, j):
        return move(i, spans[("send", "inner", "take")[j]], bs, br, (lat, across_k))

    def sized(rows, send_sem, recv_sem, device):
        return move(0, (0, rows), send_sem, recv_sem, device)

    def index_move(step):
        to = lax.rem(lat + step, n_lat)
        return pltpu.make_async_remote_copy(
            src_ref=index_ref.at[lat], dst_ref=index_ref.at[lat], send_sem=is_sem, recv_sem=ir_sem,
            device_id=(to, rad), device_id_type=MESH)

    def index_all():
        others = index_ref.at[pl.ds(0, n_lat - 1)]
        return pltpu.make_async_remote_copy(
            src_ref=others, dst_ref=others, send_sem=is_sem, recv_sem=ir_sem,
            device_id=(across_x, rad), device_id_type=MESH)

    can_up, can_down = z < levels - 1, z > 0
    brought[1].wait()
    brought[2].wait()
    index_ref[lat] = jnp.concatenate([tiles_ref[...], cells_ref[...], jnp.zeros((4, tiles_ref.shape[1]), jnp.int32)], axis=0)
    brought[0].wait()
    base = pl.multiple_of(lat * block, 8)
    lane_tiles = kern_ref.shape[1] // LANES
    groups = lane_tiles // 8

    def packed(at, row, count):
        rows = [kern_ref[:, pl.ds(pl.multiple_of(at + u * LANES, LANES), LANES)] for u in range(count)]
        return jnp.concatenate(rows, axis=0)

    @pl.loop(0, groups, unroll=4)
    def _(g):
        data_ref[pl.ds(base + pl.multiple_of(g * 24, 8), 24), :] = packed(g * 8 * LANES, 0, 8)

    left = lane_tiles - groups * 8
    if left:
        tail = packed(groups * 8 * LANES, 0, left)
        room = block - groups * 24
        tail = jnp.concatenate([tail, jnp.zeros((room - 3 * left, LANES), jnp.float32)], axis=0)
        data_ref[pl.ds(base + groups * 24, room), :] = tail
    pl.semaphore_wait(barrier, n_lat - 1 + 2)

    @pl.loop(1, n_lat)
    def _(step):
        index_move(step).start()

    for j in range(2):
        @pl.when(can_up)
        def _():
            z_move(lat, j, True).start()

        @pl.when(can_down)
        def _():
            z_move(lat, j, False).start()

        x_move(lat, j).start()

    def weights():
        col = lax.broadcasted_iota(jnp.int32, (8, DEPTH), 1)
        beside = col >= CX * WINDOW
        rest = jnp.where(beside, col - CX * WINDOW, col)
        xl = lax.shift_right_logical(rest * 1639, 16)
        zc = rest - WINDOW * xl
        place = jnp.where(beside, jnp.where(xl < HW, xl + CX, xl - CX), xl)
        sub = lax.broadcasted_iota(jnp.int32, (8, DEPTH), 0)
        sigma = 1.0 + 0.75 * jnp.full((8, DEPTH), width_ref[0], jnp.int32).astype(jnp.float32)
        twice = 2.0 * sigma * sigma

        def bell(d, reach, scale):
            square = (d * d).astype(jnp.float32)
            return jnp.where(jnp.abs(d) <= reach, jnp.exp(-square / scale), 0.0)

        norm = jnp.zeros((8, DEPTH), jnp.float32)
        for d in range(-HW, HW + 1):
            at = lat * CX + sub + d
            norm += jnp.where((at >= 0) & (at < CX * n_lat), jnp.exp(-float(d * d) / twice), 0.0)
        wx = bell(place - sub, HW, twice) / norm
        for zv in range(CZ // 8):
            norm = jnp.zeros((8, DEPTH), jnp.float32)
            zz = sub + 8 * zv
            for d in range(-HZ, HZ + 1):
                at = rad * CZ + zz + d
                norm += jnp.where((at >= 0) & (at < CZ * n_rad), float(np.exp(-d * d / 4.5)), 0.0)
            kern_w[zv * 8 : zv * 8 + 8, :] = bell(zc - HZ - zz, HZ, 4.5) / norm
        for xx in range(CX):
            both = kern_w[...] * wx[xx : xx + 1, :]
            high = both.astype(jnp.bfloat16)
            whi_ref[xx * CZ : xx * CZ + CZ, :] = high
            wlo_ref[xx * CZ : xx * CZ + CZ, :] = (both - high.astype(jnp.float32)).astype(jnp.bfloat16)

    kern_w = compact_ref.at[pl.ds(0, CZ)]
    weights()

    def lists():
        index_all().wait_recv()
        elements = index_ref.shape[2]
        shape = (n_lat, elements)
        rel = index_ref[:, 0, :] - lat
        x0 = index_ref[:, 1, :]
        zq = index_ref[:, 2, :] - rad * CZ + HZ + 8
        y0 = index_ref[:, 3, :]
        keep = (rel >= -1) & (rel <= 1) & (zq >= 4) & (zq < WINDOW + 8)
        before = lax.broadcasted_iota(jnp.int32, (elements, elements), 0) < lax.broadcasted_iota(jnp.int32, (elements, elements), 1)
        flags = jnp.where(keep, 1.0, 0.0)
        rank = jnp.dot(flags.astype(jnp.bfloat16), jnp.where(before, 1.0, 0.0).astype(jnp.bfloat16), preferred_element_type=jnp.float32)
        total = jnp.sum(flags, axis=1, keepdims=True).astype(jnp.int32)
        rank = jnp.where(keep, rank, -1.0)
        low = jnp.maximum(x0, jnp.where(rel < 0, HW, 0))
        high = jnp.minimum(x0 + 4, jnp.where(rel > 0, HW - 1, CX - 1))
        code = low + 8 * (high - low + 1)
        lane = lax.broadcasted_iota(jnp.int32, shape, 1)
        fields = [lane, zq, y0, x0, code, jnp.where(rel == 0, 0, 1)]
        fields = [jnp.where(keep, f, 0).astype(jnp.float32) for f in fields]
        slot = lax.broadcasted_iota(jnp.int32, (elements, elements), 0).astype(jnp.float32)
        zero = jnp.zeros((1, elements), jnp.float32)
        for i in range(n_lat):
            stack = jnp.concatenate([f[i : i + 1] for f in fields] + [zero, zero], axis=0).astype(jnp.bfloat16)
            pick = jnp.where(rank[i : i + 1] == slot, 1.0, 0.0).astype(jnp.bfloat16)
            compact_ref[8 * i : 8 * i + 8, :elements] = lax.dot_general(
                stack, pick, (((1,), (1,)), ((), ())), preferred_element_type=jnp.float32)

        def field(f):
            return jnp.concatenate([compact_ref[8 * i + f : 8 * i + f + 1, :elements] for i in range(n_lat)], axis=0).astype(jnp.int32)

        e, zq, y0, x0, code, beside = [field(f) for f in range(6)]
        start = e * NGLL
        row = lax.broadcasted_iota(jnp.int32, shape, 0) * block + 3 * lax.shift_right_logical(start, 7)
        off = start & (LANES - 1)
        words = row | (off << 16) | (((off - 25 * x0) & (LANES - 1)) << 23)
        words_ref[0] = jnp.where(lane == elements - 1, total, words)
        zb = jnp.maximum(lax.shift_right_logical(zq, 2) - 1, 0)
        at = ((beside * Z_BINS + zb) * Y_TILES + lax.shift_right_logical(y0, 4)) * 8
        words_ref[1] = at | ((zq & 7) << 16) | ((y0 & 15) << 20) | (code << 24)

    def when_there(d, up, body):
        zi = z - d if up else z + d

        @pl.when((zi >= 0) & (zi < levels))
        def _():
            body(2 * zi)

    def from_end(d, up):
        return (z - d == 0) if up else (z + d == levels - 1)

    def further(i, j, up):
        @pl.when(can_up if up else can_down)
        def _():
            z_move(i, j, up).start()

    def line(d, up, j):
        def body(i):
            i = i + x
            z_move(i, j, up).wait_recv()
            further(i, j, up)
            if j == 0:
                x_move(i, j).start()
                y_move(i, "send").start()
            else:
                @pl.when(jnp.logical_not(from_end(d, up)))
                def _():
                    x_move(i, j).start()

            k_move(i, j).start()

        when_there(d, up, body)

    def cross(d, up, j):
        def body(i):
            i = i + 1 - x
            if j == 0:
                x_move(i, j).wait_recv()
                y_move(i, "send").start()
            elif d == 0:
                x_move(i, j).wait_recv()

                @pl.when(z == 0)
                def _():
                    z_move(i, j, True).start()

                @pl.when(z == levels - 1)
                def _():
                    z_move(i, j, False).start()
            else:
                @pl.when(from_end(d, up))
                def _():
                    z_move(i, j, up).wait_recv()
                    further(i, j, up)

                @pl.when(jnp.logical_not(from_end(d, up)))
                def _():
                    x_move(i, j).wait_recv()

            k_move(i, j).start()

        when_there(d, up, body)

    def y_done(d, up, column):
        def body(i):
            i = i + column
            y_move(i, "take").wait_recv()
            k_move(i, 2).start()

        when_there(d, up, body)

    ways = lambda d: (True, False) if d else (True,)
    for d in range(1, levels + 2):
        for j in range(2):
            if d < levels:
                for up in ways(d):
                    line(d, up, j)
            if d - 1 < levels:
                for up in ways(d - 1):
                    cross(d - 1, up, j)
            if j == 0 and d == 1:
                lists()
            if j == 0 and 1 <= d - 1 < levels:
                for up in ways(d - 1):
                    y_done(d - 1, up, x)
            if j == 0 and 0 <= d - 2 < levels:
                for up in ways(d - 2):
                    y_done(d - 2, up, 1 - x)

    index_all().wait_send()
    sized(levels * edge, xs.at[0], xr.at[0, 0], (across_x, rad)).wait_send()
    at_end = (z == 0) | (z == levels - 1)
    lines = levels - 1 if levels > 1 else 1

    @pl.when(at_end)
    def _():
        sized(lines * inner, xs.at[1], xr.at[0, 1], (across_x, rad)).wait_send()

    if levels > 2:
        @pl.when(jnp.logical_not(at_end))
        def _():
            sized((levels - 2) * inner, xs.at[1], xr.at[0, 1], (across_x, rad)).wait_send()

    for up in (True, False):
        able, way = (can_up, 0) if up else (can_down, 1)
        peer = (lat + (2 if up else -2), rad)

        @pl.when(able)
        def _():
            @pl.loop(0, levels)
            def _(zi):
                @pl.when((zi <= z) if up else (zi >= z))
                def _():
                    sized(edge + inner, zs.at[2 * zi + x, way], zr.at[0, 0], peer).wait_send()

            end = 0 if up else levels - 1
            sized(inner, zs.at[2 * end + 1 - x, way], zr.at[0, 0], peer).wait_send()

    sized((n_lat - 1) * edge, ys, yr.at[0], (lat, across_y)).wait_send()
    everything = sized((n_lat - 1) * half, bs, br, (lat, across_k))
    everything.wait_send()
    everything.wait_recv()


def grid_kernel(n_lat, words_ref, data_ref, whi_ref, wlo_ref, ghi_hbm, glo_hbm, out_hbm, acc0, acc1, acc2, field, result, words, ghi_ref, glo_ref, sem, smooth_sem, out_sem):
    accs = (acc0, acc1, acc2)
    smooth = [pltpu.make_async_copy(ghi_hbm, ghi_ref, smooth_sem.at[0]), pltpu.make_async_copy(glo_hbm, glo_ref, smooth_sem.at[1])]
    bring = pltpu.make_async_copy(words_ref, words, sem)
    bring.start()
    for copy in smooth:
        copy.start()
    rows = acc0.shape[0]

    @pl.loop(0, rows // 8, unroll=11)
    def _(r):
        for acc in accs:
            acc[pl.ds(pl.multiple_of(r * 8, 8), 8), :] = jnp.zeros((8, LANES), jnp.float32)

    bring.wait()
    lane = lax.broadcasted_iota(jnp.int32, (8, LANES), 1)
    sub = lax.broadcasted_iota(jnp.int32, (8, LANES), 0)
    across = lane & 15
    along = lax.shift_right_logical(lane, 4)
    ramp = 25 * along
    elements = words.shape[2]

    @pl.loop(0, n_lat)
    def _(i):
        count = words[0, i, elements - 1]

        @pl.loop(0, lax.div(count + SUM_WAYS - 1, SUM_WAYS))
        def _(step):
            for u in range(SUM_WAYS):
                p = step * SUM_WAYS + u
                w0, w1 = words[0, i, p], words[1, i, p]
                row = w0 & 0xFFFF
                off = lax.shift_right_logical(w0, 16) & 127
                shift = lax.shift_right_logical(w0, 23)
                at = pl.multiple_of(w1 & 0xFFFF, 8)
                zq = lax.shift_right_logical(w1, 16) & 7
                yl = lax.shift_right_logical(w1, 20) & 15
                low = lax.shift_right_logical(w1, 24) & 7
                wide = lax.shift_right_logical(w1, 27)
                tz = (sub - zq) & 7
                ty = (lane - yl) & 15
                tx = along - low
                index = (ramp + shift + 5 * tz + ty) & (LANES - 1)
                good = (tz < 5) & (ty < 5) & (tx >= 0) & (tx < wide)
                first = across >= yl
                here, there = good & first, good & jnp.logical_not(first)
                head = lane >= off
                for c in range(3):
                    a = jnp.broadcast_to(data_ref[pl.ds(row + c, 1), :], (8, LANES))
                    b = jnp.broadcast_to(data_ref[pl.ds(row + 3 + c, 1), :], (8, LANES))
                    v = jnp.take_along_axis(jnp.where(head, a, b), index, axis=1, mode="promise_in_bounds")
                    accs[c][pl.ds(at, 8), :] += jnp.where(here, v, 0.0)
                    accs[c][pl.ds(at + 8, 8), :] += jnp.where(there, v, 0.0)

    low_half = sub < 4
    for copy in smooth:
        copy.wait()
    for c in range(3):
        acc = accs[c]

        @pl.loop(0, 2, unroll=2)
        def _(g):
            @pl.loop(0, WINDOW // 8, unroll=WINDOW // 8)
            def _(h):
                for side in range(2):
                    v = []
                    for t in range(8):
                        def bins(n):
                            r = ((g * Z_BINS + 2 * h + n) * Y_TILES + side * 8 + t) * 8
                            return acc[pl.ds(pl.multiple_of(r, 8), 8), :]

                        v.append(bins(1) + jnp.where(low_half, bins(0), bins(2)))
                    for bit in (4, 2, 1):
                        straight = (along & bit) == 0
                        w = list(v)
                        for r in range(8):
                            if r & bit:
                                continue
                            a, b = v[r], v[r + bit]
                            if bit == 4:
                                turned = pltpu.roll(jnp.where(straight, b, a), 64, 1)
                                w[r] = jnp.where(straight, a, turned)
                                w[r + bit] = jnp.where(straight, turned, b)
                            else:
                                w[r] = jnp.where(straight, a, pltpu.roll(b, 16 * bit, 1))
                                w[r + bit] = jnp.where(straight, pltpu.roll(a, LANES - 16 * bit, 1), b)
                        v = w
                    for xl in range(8):
                        r = pl.multiple_of(g * (CX * WINDOW) + xl * WINDOW + h * 8, 8)
                        field[pl.ds(r, 8), side * LANES : (side + 1) * LANES] = v[xl]

        def split(a):
            high = a.astype(jnp.bfloat16)
            return high, (a - high.astype(jnp.float32)).astype(jnp.bfloat16)

        def dot(a, b):
            return jnp.dot(a, b, preferred_element_type=jnp.float32)

        high, low = split(field[...])
        whi = whi_ref[...]
        mixed = dot(whi, high) + dot(wlo_ref[...], high) + dot(whi, low)
        high, low = split(mixed)
        ghi = ghi_ref[...]
        done = dot(high, ghi) + dot(low, ghi) + dot(high, glo_ref[...])
        result[c] = done.reshape(CX, CZ, NY)
        pltpu.make_async_copy(result.at[c], out_hbm.at[c], out_sem.at[c]).start()
    for c in range(3):
        pltpu.make_async_copy(result.at[c], out_hbm.at[c], out_sem.at[c]).wait()


def on_device_whole(n_lat, n_rad, kernels, cells, tiles, width_class):
    elements = tiles.shape[0]
    block = -(-kernels.shape[1] // LANES * 3 // 16) * 16
    smem = pl.BlockSpec(memory_space=pltpu.SMEM)
    vmem = pl.BlockSpec(memory_space=pltpu.VMEM)
    hbm = pl.BlockSpec(memory_space=pltpu.HBM)
    dma = pltpu.SemaphoreType.DMA
    stay = functools.partial(pltpu.with_memory_space_constraint, memory_space=pltpu.HBM)
    data, words, whi, wlo = pl.pallas_call(
        functools.partial(gather_kernel, n_lat, n_rad, block),
        out_shape=[
            jax.ShapeDtypeStruct((n_lat * block + 8, LANES), jnp.float32),
            jax.ShapeDtypeStruct((2, n_lat, elements), jnp.int32),
            jax.ShapeDtypeStruct((CX * CZ, DEPTH), jnp.bfloat16),
            jax.ShapeDtypeStruct((CX * CZ, DEPTH), jnp.bfloat16),
        ],
        in_specs=[smem, hbm, hbm, hbm],
        out_specs=[vmem] * 4,
        scratch_shapes=[
            pltpu.VMEM(kernels.shape, jnp.float32),
            pltpu.VMEM((1, elements), jnp.int32),
            pltpu.VMEM(cells.shape, jnp.int32),
            pltpu.VMEM((n_lat, 8, elements), jnp.int32),
            pltpu.VMEM((8 * n_lat, DEPTH), jnp.float32),
            dma((3,)), dma, dma,
            dma((n_lat, 2)), dma((n_lat, 2)), dma((2,)), dma((n_lat, 2)),
            dma, dma((n_lat,)), dma, dma,
        ],
        compiler_params=pltpu.CompilerParams(
            vmem_limit_bytes=VMEM_LIMIT, collective_id=0, has_side_effects=True
        ),
    )(width_class, *map(stay, (tiles.reshape(1, elements), cells, kernels)))
    smooth = band_matrix(NY, 2.5, HY).T.astype(np.float32)
    high = smooth.astype(jnp.bfloat16)
    low = (smooth - high.astype(np.float32)).astype(jnp.bfloat16)
    rows = 2 * Z_BINS * Y_TILES * 8
    return pl.pallas_call(
        functools.partial(grid_kernel, n_lat),
        out_shape=jax.ShapeDtypeStruct((3, CX, CZ, NY), jnp.float32),
        in_specs=[vmem] * 4 + [hbm] * 2,
        out_specs=hbm,
        scratch_shapes=[
            pltpu.VMEM((rows, LANES), jnp.float32),
            pltpu.VMEM((rows, LANES), jnp.float32),
            pltpu.VMEM((rows, LANES), jnp.float32),
            pltpu.VMEM((DEPTH, NY), jnp.float32),
            pltpu.VMEM((3, CX, CZ, NY), jnp.float32),
            pltpu.SMEM((2, n_lat, elements), jnp.int32),
            pltpu.VMEM((NY, NY), jnp.bfloat16),
            pltpu.VMEM((NY, NY), jnp.bfloat16),
            dma, dma((2,)), dma((3,)),
        ],
        compiler_params=pltpu.CompilerParams(vmem_limit_bytes=VMEM_LIMIT),
    )(words, data, whi, wlo, stay(jnp.asarray(high)), stay(jnp.asarray(low)))


def solution(mesh):
    n_lat, n_rad = mesh.shape["lat"], mesh.shape["rad"]
    whole = n_lat <= 8 and n_lat % 2 == 0 and n_rad == 4
    return jax.shard_map(
        functools.partial(on_device_whole if whole else on_device, n_lat, n_rad),
        mesh=mesh,
        in_specs=(P(None, "lat"), P(None, "lat"), P("lat", None), P("lat")),
        out_specs=P(None, "lat", "rad", None),
        check_vma=False,
    )
```

```python
import functools

import jax
import jax.numpy as jnp
import numpy as np
from jax import lax
from jax.experimental import pallas as pl
from jax.experimental.pallas import tpu as pltpu
from jax.sharding import PartitionSpec as P

CX = 8
NY = 256
CZ = 32
NGLL = 125
HW = 4
HY = 8
HZ = 4
ZP = CZ + 4 * HZ
LANES = 128
TAPS = 2 * HZ + 1
PADX = CX + 2 * HW
PACK_UNROLL = 4
SUM_UNROLL = 4
VMEM_LIMIT = 48 * 2**20
MESH = pl.DeviceIdType.MESH


def band_matrix(count, sigma, half):
    place = np.arange(count)
    gap = place[None, :] - place[:, None]
    gauss = np.where(np.abs(gap) <= half, np.exp(-(gap**2) / (2.0 * sigma**2)), 0.0)
    return gauss / gauss.sum(axis=1, keepdims=True)


def z_taps(n_rad):
    full = np.pad(band_matrix(CZ * n_rad, 1.5, HZ), ((0, 0), (HZ, HZ)))
    return np.stack([full[z, z : z + TAPS] for z in range(CZ * n_rad)]).astype(np.float32)


def pack_kernel(
    n_lat, n_rad, share, elements, tiles_ref, cells_hbm, kern_hbm, out_ref, count, todo, place, cells_ref, kern_ref, sems
):
    slab = lax.axis_index("rad")
    rows = elements * NGLL // LANES
    bring_cells = pltpu.make_async_copy(cells_hbm, cells_ref, sems.at[0])
    bring_kern = pltpu.make_async_copy(kern_hbm, kern_ref, sems.at[1])
    bring_cells.start()
    bring_kern.start()
    out_ref[...] = jnp.full(out_ref.shape, -1000.0, jnp.float32)
    lane = lax.broadcasted_iota(jnp.int32, (3, LANES), 1)

    @pl.loop(0, n_lat)
    def _(t):
        count[t] = 0

    def listed(e, n):
        t = tiles_ref[e]
        rank = count[t]
        count[t] = rank + 1
        slot = lax.div(rank, n_rad)
        todo[n] = e
        place[n] = t * share + slot
        return n + jnp.where(rank - slot * n_rad == slab, 1, 0)

    n = lax.fori_loop(0, elements, listed, 0, unroll=4)
    for more in range(PACK_UNROLL):
        todo[n + more] = 0
        place[n + more] = n_lat * share
    bring_cells.wait()
    bring_kern.wait()

    def packed(step, _):
        for u in range(PACK_UNROLL):
            e = todo[step * PACK_UNROLL + u]
            at = place[step * PACK_UNROLL + u]
            start = e * NGLL
            row = lax.shift_right_logical(start, 7)
            off = start & (LANES - 1)
            after = jnp.minimum(row + 1, rows - 1)
            a = kern_ref[:, pl.ds(pl.multiple_of(row * LANES, LANES), LANES)]
            b = kern_ref[:, pl.ds(pl.multiple_of(after * LANES, LANES), LANES)]
            v = pltpu.roll(jnp.where(lane >= off, a, b), (LANES - off) & (LANES - 1), 1)
            v = jnp.where(lane == NGLL, cells_ref[0, e].astype(jnp.float32), v)
            v = jnp.where(lane == NGLL + 1, cells_ref[1, e].astype(jnp.float32), v)
            v = jnp.where(lane == NGLL + 2, cells_ref[2, e].astype(jnp.float32), v)
            t = lax.div(at, share)
            slot = at - t * share
            for c in range(3):
                out_ref[t, pl.ds(c * share + slot, 1), :] = v[c : c + 1]
        return 0

    lax.fori_loop(0, lax.div(n + PACK_UNROLL - 1, PACK_UNROLL), packed, 0)


def exchange_kernel(n_lat, n_rad, send_ref, recv_ref, own_sem, send_sem, recv_sem, fwd_sem, got_sem):
    tile, slab = lax.axis_index("lat"), lax.axis_index("rad")
    barrier = pltpu.get_barrier_semaphore()

    @pl.loop(1, n_lat)
    def _(k):
        pl.semaphore_signal(barrier, inc=1, device_id=(lax.rem(tile + k, n_lat), slab), device_id_type=MESH)

    pair = slab + 1 - 2 * lax.rem(slab, 2)
    other = slab + 2 - 4 * lax.div(slab, 2)
    for peer in (pair, other):
        pl.semaphore_signal(barrier, inc=1, device_id=(tile, peer), device_id_type=MESH)
    pl.semaphore_wait(barrier, n_lat - 1 + 2)

    def across(k):
        to = lax.rem(tile + k, n_lat)
        return pltpu.make_async_remote_copy(
            src_ref=send_ref.at[to],
            dst_ref=recv_ref.at[slab, tile],
            send_sem=send_sem.at[k],
            recv_sem=recv_sem.at[k],
            device_id=(to, slab),
            device_id_type=MESH,
        )

    def share(k, of, to, way):
        block = recv_ref.at[of, lax.rem(tile + n_lat - k, n_lat)]
        return pltpu.make_async_remote_copy(
            src_ref=block,
            dst_ref=block,
            send_sem=fwd_sem.at[way, k],
            recv_sem=got_sem.at[way, k],
            device_id=(tile, to),
            device_id_type=MESH,
        )

    def forward(k):
        share(k, slab, other, 0).start()
        share(k, slab, pair, 1).start()

    def relay(k):
        share(k, other, other, 0).wait_recv()
        share(k, other, pair, 2).start()

    @pl.loop(1, n_lat)
    def _(k):
        across(k).start()

    own = pltpu.make_async_copy(send_ref.at[tile], recv_ref.at[slab, tile], own_sem)
    own.start()
    own.wait()
    forward(0)

    @pl.loop(1, n_lat)
    def _(k):
        across(k).wait_recv()
        forward(k)

    @pl.loop(0, n_lat)
    def _(k):
        relay(k)

    @pl.loop(0, n_lat)
    def _(k):
        share(k, pair, pair, 1).wait_recv()
        share(k, other + pair - slab, pair, 2).wait_recv()

    @pl.loop(1, n_lat)
    def _(k):
        across(k).wait_send()

    @pl.loop(0, n_lat)
    def _(k):
        share(k, slab, other, 0).wait_send()
        share(k, slab, pair, 1).wait_send()
        share(k, other, pair, 2).wait_send()


def sum_kernel(blocks, share, meta_ref, recv_ref, acc, todo):
    slab = lax.axis_index("rad")
    slots = blocks * share
    acc[...] = jnp.zeros(acc.shape, jnp.float32)
    lane = lax.broadcasted_iota(jnp.int32, (8, LANES), 1)
    sub = lax.broadcasted_iota(jnp.int32, (8, LANES), 0)
    ramp = 25 * sub + lane
    low = slab * CZ - 2 * HZ

    def listed(s, n):
        zb = meta_ref[slots + s] - low
        todo[n] = s
        return n + jnp.where((zb >= 0) & (zb < CZ + 3 * HZ), 1, 0)

    n = lax.fori_loop(0, slots, listed, 0, unroll=8)
    for more in range(SUM_UNROLL):
        todo[n + more] = 0

    def place(at, values, index, mask):
        for j in range(5):
            picked = jnp.where(mask, index + 5 * j, NGLL)
            for c in range(3):
                piece = jnp.take_along_axis(values[c], picked, axis=1, mode="promise_in_bounds")
                acc[pl.ds(pl.multiple_of(at + (3 * j + c) * 8, 8), 8), :] += piece

    def summed(step, _):
        later = []
        for u in range(SUM_UNROLL):
            s = todo[step * SUM_UNROLL + u]
            good = step * SUM_UNROLL + u < n
            x0 = jnp.clip(meta_ref[s], 0, CX - 5)
            zb = jnp.clip(meta_ref[slots + s] - low, 0, CZ + 3 * HZ - 1)
            y0 = jnp.clip(meta_ref[2 * slots + s], 0, NY - 5)
            block = lax.div(s, share)
            slot = s - block * share
            values = []
            for c in range(3):
                row = jnp.broadcast_to(recv_ref[block, pl.ds(c * share + slot, 1), :], (8, LANES))
                values.append(jnp.where(lane < NGLL, row, 0.0))
            half = lax.shift_right_logical(y0, 7)
            yl = y0 & (LANES - 1)
            index = ramp - (25 * x0 + yl)
            rows = (sub >= x0) & (sub < jnp.where(good, x0 + 5, 0))
            at = (half * ZP + zb) * 24
            place(at, values, index, rows & (lane >= yl) & (lane < yl + 5))
            later.append((at, values, index, rows, yl))
        widest = functools.reduce(jnp.maximum, [entry[4] for entry in later])

        @pl.when(widest > LANES - 5)
        def _():
            for at, values, index, rows, yl in later:
                over = rows & (lane < yl + 5 - LANES)

                @pl.when(yl > LANES - 5)
                def _():
                    place(at + ZP * 24, values, index + LANES, over)

        return 0

    lax.fori_loop(0, lax.div(n + SUM_UNROLL - 1, SUM_UNROLL), summed, 0)


def finish_kernel(n_lat, taps_ref, wx_ref, acc, wy_ref, out_ref, planes, rows_ref, send_sem, recv_sem):
    tile, slab = lax.axis_index("lat"), lax.axis_index("rad")
    barrier = pltpu.get_barrier_semaphore()
    has_prev, has_next = tile > 0, tile < n_lat - 1
    halo = HW * CZ

    @pl.when(has_prev)
    def _():
        pl.semaphore_signal(barrier, inc=1, device_id=(tile - 1, slab), device_id_type=MESH)

    @pl.when(has_next)
    def _():
        pl.semaphore_signal(barrier, inc=1, device_id=(tile + 1, slab), device_id_type=MESH)

    def at(c, row, count):
        return rows_ref.at[:, pl.ds(c * PADX * CZ + row, count), :]

    def to_next(c):
        return pltpu.make_async_remote_copy(
            src_ref=at(c, CX * CZ, halo),
            dst_ref=at(c, 0, halo),
            send_sem=send_sem.at[0, c],
            recv_sem=recv_sem.at[0, c],
            device_id=(tile + 1, slab),
            device_id_type=MESH,
        )

    def to_prev(c):
        return pltpu.make_async_remote_copy(
            src_ref=at(c, halo, halo),
            dst_ref=at(c, halo + CX * CZ, halo),
            send_sem=send_sem.at[1, c],
            recv_sem=recv_sem.at[1, c],
            device_id=(tile - 1, slab),
            device_id_type=MESH,
        )

    for c in range(3):

        @pl.loop(0, CZ, unroll=4)
        def _(z):
            for half in range(NY // LANES):
                total = jnp.zeros((CX, LANES), jnp.float32)
                for d in range(TAPS):
                    weight = taps_ref[(slab * CZ + z) * TAPS + d]
                    row = pl.multiple_of(((half * ZP + z + HZ + d) * 3 + c) * CX, 8)
                    total = total + weight * acc[pl.ds(row, CX), :]
                cols = slice(half * LANES, (half + 1) * LANES)
                planes[pl.ds(pl.multiple_of(z * CX, 8), CX), cols] = total

        product = jnp.dot(planes[...], wy_ref[...], precision=lax.Precision.HIGHEST)
        for z in range(CZ):
            for half in range(NY // LANES):
                piece = product[z * CX : (z + 1) * CX, half * LANES : (half + 1) * LANES]
                rows_ref[half, pl.ds(c * PADX * CZ + halo + z, CX, stride=CZ), :] = piece

        if c == 0:
            beside = jnp.minimum(tile, 1) + jnp.minimum(n_lat - 1 - tile, 1)
            pl.semaphore_wait(barrier, beside)

        @pl.when(has_next)
        def _():
            to_next(c).start()

        @pl.when(has_prev)
        def _():
            to_prev(c).start()

        zeros = jnp.zeros((NY // LANES, halo, LANES), jnp.float32)

        @pl.when(tile == 0)
        def _():
            rows_ref[:, c * PADX * CZ : c * PADX * CZ + halo, :] = zeros

        @pl.when(tile == n_lat - 1)
        def _():
            rows_ref[:, c * PADX * CZ + halo + CX * CZ : (c + 1) * PADX * CZ, :] = zeros

    for c in range(3):

        @pl.when(has_prev)
        def _():
            to_next(c).wait_recv()

        @pl.when(has_next)
        def _():
            to_prev(c).wait_recv()

        @pl.loop(0, CX)
        def _(x):
            for half in range(NY // LANES):
                total = jnp.zeros((CZ, LANES), jnp.float32)
                for d in range(2 * HW + 1):
                    row = pl.multiple_of(c * PADX * CZ + (x + d) * CZ, 8)
                    total = total + wx_ref[x * (2 * HW + 1) + d] * rows_ref[half, pl.ds(row, CZ), :]
                out_ref[c, x, :, half * LANES : (half + 1) * LANES] = total

    for c in range(3):

        @pl.when(has_next)
        def _():
            to_next(c).wait_send()

        @pl.when(has_prev)
        def _():
            to_prev(c).wait_send()


def x_weights(width_class, n_lat):
    rows = lax.axis_index("lat") * CX + jnp.arange(CX)
    sigma = 1.0 + 0.75 * width_class[0].astype(jnp.float32)
    offsets = jnp.arange(-HW, HW + 1)
    target = rows[:, None] + offsets[None, :]
    valid = (target >= 0) & (target < CX * n_lat)
    gauss = jnp.exp(-(offsets[None, :].astype(jnp.float32) ** 2) / (2.0 * sigma**2))
    gauss = jnp.where(valid, gauss, 0.0)
    return gauss / jnp.sum(gauss, axis=1, keepdims=True)


def on_device(n_lat, n_rad, kernels, cells, tiles, width_class):
    elements = tiles.shape[0]
    cap = max(2, 2 * elements // n_lat)
    share = -(-cap // n_rad)
    blocks = n_rad * n_lat
    slots = blocks * share
    params = pltpu.CompilerParams(vmem_limit_bytes=VMEM_LIMIT)
    smem = pl.BlockSpec(memory_space=pltpu.SMEM)
    vmem = pl.BlockSpec(memory_space=pltpu.VMEM)
    hbm = pl.BlockSpec(memory_space=pl.ANY)
    send = pl.pallas_call(
        functools.partial(pack_kernel, n_lat, n_rad, share, elements),
        out_shape=jax.ShapeDtypeStruct((n_lat + 1, 3 * share, LANES), jnp.float32),
        in_specs=[smem, hbm, hbm],
        out_specs=vmem,
        scratch_shapes=[
            pltpu.SMEM((n_lat,), jnp.int32),
            pltpu.SMEM((elements + PACK_UNROLL,), jnp.int32),
            pltpu.SMEM((elements + PACK_UNROLL,), jnp.int32),
            pltpu.SMEM(cells.shape, jnp.int32),
            pltpu.VMEM(kernels.shape, jnp.float32),
            pltpu.SemaphoreType.DMA((2,)),
        ],
        compiler_params=params,
    )(tiles.reshape(-1), cells, kernels)
    recv = pl.pallas_call(
        functools.partial(exchange_kernel, n_lat, n_rad),
        out_shape=jax.ShapeDtypeStruct((n_rad, n_lat, 3 * share, LANES), jnp.float32),
        in_specs=[vmem],
        out_specs=vmem,
        scratch_shapes=[
            pltpu.SemaphoreType.DMA,
            pltpu.SemaphoreType.DMA((n_lat,)),
            pltpu.SemaphoreType.DMA((n_lat,)),
            pltpu.SemaphoreType.DMA((3, n_lat)),
            pltpu.SemaphoreType.DMA((3, n_lat)),
        ],
        compiler_params=pltpu.CompilerParams(
            vmem_limit_bytes=VMEM_LIMIT, collective_id=0, has_side_effects=True
        ),
    )(send)
    recv = recv.reshape(blocks, 3 * share, LANES)
    meta = recv[:, :share, NGLL:].transpose(2, 0, 1).reshape(-1).astype(jnp.int32)
    grid_rows = NY // LANES * ZP * 24
    summed = pl.pallas_call(
        functools.partial(sum_kernel, blocks, share),
        out_shape=jax.ShapeDtypeStruct((grid_rows, LANES), jnp.float32),
        in_specs=[smem, vmem],
        out_specs=vmem,
        scratch_shapes=[pltpu.SMEM((slots + SUM_UNROLL,), jnp.int32)],
        compiler_params=params,
    )(meta, recv)
    return pl.pallas_call(
        functools.partial(finish_kernel, n_lat),
        out_shape=jax.ShapeDtypeStruct((3, CX, CZ, NY), jnp.float32),
        in_specs=[smem, smem, vmem, vmem],
        out_specs=vmem,
        scratch_shapes=[
            pltpu.VMEM((CZ * CX, NY), jnp.float32),
            pltpu.VMEM((NY // LANES, 3 * PADX * CZ, LANES), jnp.float32),
            pltpu.SemaphoreType.DMA((2, 3)),
            pltpu.SemaphoreType.DMA((2, 3)),
        ],
        compiler_params=pltpu.CompilerParams(
            vmem_limit_bytes=VMEM_LIMIT, collective_id=1, has_side_effects=True
        ),
    )(
        jnp.asarray(z_taps(n_rad).reshape(-1)),
        x_weights(width_class, n_lat).reshape(-1),
        summed,
        jnp.asarray(band_matrix(NY, 2.5, HY).T.astype(np.float32)),
    )

ROW_TILES = 3
Z_BINS = 11
Y_TILES = 17
WINDOW = CZ + 2 * HZ
DEPTH = 2 * CX * WINDOW
SUM_WAYS = 16
SUM_GROUP = 4
CUTS = 2


def gather_kernel(n_lat, n_rad, block, width_ref, tiles_hbm, cells_hbm, kern_hbm, data_ref, words_ref, whi_ref, wlo_ref,
                  kern_ref, tiles_ref, cells_ref, index_ref, compact_ref, in_sem, is_sem, ir_sem, zs, zr, xs, xr, ys, yr, bs, br):
    lat, rad = lax.axis_index("lat"), lax.axis_index("rad")
    levels = n_lat // 2
    z, x = lax.div(lat, 2), lax.rem(lat, 2)
    y, k = lax.div(rad, 2), lax.rem(rad, 2)
    across_x, across_y, across_k = lat + 1 - 2 * x, rad + 2 - 4 * y, rad + 1 - 2 * k
    barrier = pltpu.get_barrier_semaphore()

    @pl.loop(1, n_lat)
    def _(step):
        pl.semaphore_signal(barrier, inc=1, device_id=(lax.rem(lat + step, n_lat), rad), device_id_type=MESH)

    for peer in (across_y, across_k):
        pl.semaphore_signal(barrier, inc=1, device_id=(lat, peer), device_id_type=MESH)
    brought = [
        pltpu.make_async_copy(kern_hbm, kern_ref, in_sem.at[0]),
        pltpu.make_async_copy(tiles_hbm, tiles_ref, in_sem.at[1]),
        pltpu.make_async_copy(cells_hbm, cells_ref, in_sem.at[2]),
    ]
    for copy in brought:
        copy.start()

    half = block // 2
    part = half // 2
    mine = k * half
    piece = part // CUTS
    starts = [mine + (y if j < CUTS else 1 - y) * part + j % CUTS * piece for j in range(2 * CUTS)]

    def move(row, count, send_sem, recv_sem, device):
        rows = data_ref.at[pl.ds(pl.multiple_of(row, 8), count)]
        return pltpu.make_async_remote_copy(
            src_ref=rows, dst_ref=rows, send_sem=send_sem, recv_sem=recv_sem,
            device_id=device, device_id_type=MESH)

    def z_move(i, j, up):
        way = 0 if up else 1
        return move(i * block + starts[j], piece, zs.at[i, way], zr.at[i, j], (lat + (2 if up else -2), rad))

    def x_move(i, j):
        return move(i * block + starts[j], piece, xs.at[j // CUTS], xr.at[i, j], (across_x, rad))

    def y_move(i, j):
        return move(i * block + starts[j], piece, ys, yr.at[i, j % CUTS], (lat, across_y))

    def k_move(i):
        return move(i * block + mine, half, bs, br, (lat, across_k))

    def sized(rows, send_sem, recv_sem, device):
        return move(0, rows, send_sem, recv_sem, device)

    def index_move(step):
        to = lax.rem(lat + step, n_lat)
        return pltpu.make_async_remote_copy(
            src_ref=index_ref.at[lat], dst_ref=index_ref.at[lat], send_sem=is_sem, recv_sem=ir_sem,
            device_id=(to, rad), device_id_type=MESH)

    def index_all():
        others = index_ref.at[pl.ds(0, n_lat - 1)]
        return pltpu.make_async_remote_copy(
            src_ref=others, dst_ref=others, send_sem=is_sem, recv_sem=ir_sem,
            device_id=(across_x, rad), device_id_type=MESH)

    can_up, can_down = z < levels - 1, z > 0
    at_end = (z == 0) | (z == levels - 1)
    long_up, long_down = z < levels - 2, z > 1
    brought[1].wait()
    brought[2].wait()
    index_ref[lat] = jnp.concatenate([tiles_ref[...], cells_ref[...], jnp.zeros((4, tiles_ref.shape[1]), jnp.int32)], axis=0)
    brought[0].wait()
    base = pl.multiple_of(lat * block, 8)
    lane_tiles = kern_ref.shape[1] // LANES
    groups = lane_tiles // 8

    def packed(at, row, count):
        rows = [kern_ref[:, pl.ds(pl.multiple_of(at + u * LANES, LANES), LANES)] for u in range(count)]
        return jnp.concatenate(rows, axis=0)

    @pl.loop(0, groups, unroll=4)
    def _(g):
        data_ref[pl.ds(base + pl.multiple_of(g * 24, 8), 24), :] = packed(g * 8 * LANES, 0, 8)

    left = lane_tiles - groups * 8
    if left:
        tail = packed(groups * 8 * LANES, 0, left)
        room = block - groups * 24
        tail = jnp.concatenate([tail, jnp.zeros((room - 3 * left, LANES), jnp.float32)], axis=0)
        data_ref[pl.ds(base + groups * 24, room), :] = tail
    pl.semaphore_wait(barrier, n_lat - 1 + 2)

    def own_z(j, up):
        able = (long_up if up else long_down) if j >= CUTS else (can_up if up else can_down)

        @pl.when(able)
        def _():
            z_move(lat, j, up).start()

    for j in range(2 * CUTS):
        own_z(j, True)
        own_z(j, False)
        if j < CUTS:
            x_move(lat, j).start()

    @pl.loop(1, n_lat)
    def _(step):
        index_move(step).start()

    def weights():
        col = lax.broadcasted_iota(jnp.int32, (8, DEPTH), 1)
        beside = col >= CX * WINDOW
        rest = jnp.where(beside, col - CX * WINDOW, col)
        xl = lax.shift_right_logical(rest * 1639, 16)
        zc = rest - WINDOW * xl
        place = jnp.where(beside, jnp.where(xl < HW, xl + CX, xl - CX), xl)
        sub = lax.broadcasted_iota(jnp.int32, (8, DEPTH), 0)
        sigma = 1.0 + 0.75 * jnp.full((8, DEPTH), width_ref[0], jnp.int32).astype(jnp.float32)
        twice = 2.0 * sigma * sigma

        def bell(d, reach, scale):
            square = (d * d).astype(jnp.float32)
            return jnp.where(jnp.abs(d) <= reach, jnp.exp(-square / scale), 0.0)

        norm = jnp.zeros((8, DEPTH), jnp.float32)
        for d in range(-HW, HW + 1):
            at = lat * CX + sub + d
            norm += jnp.where((at >= 0) & (at < CX * n_lat), jnp.exp(-float(d * d) / twice), 0.0)
        wx = bell(place - sub, HW, twice) / norm
        for zv in range(CZ // 8):
            norm = jnp.zeros((8, DEPTH), jnp.float32)
            zz = sub + 8 * zv
            for d in range(-HZ, HZ + 1):
                at = rad * CZ + zz + d
                norm += jnp.where((at >= 0) & (at < CZ * n_rad), float(np.exp(-d * d / 4.5)), 0.0)
            kern_w[zv * 8 : zv * 8 + 8, :] = bell(zc - HZ - zz, HZ, 4.5) / norm
        for xx in range(CX):
            both = kern_w[...] * wx[xx : xx + 1, :]
            high = both.astype(jnp.bfloat16)
            whi_ref[xx * CZ : xx * CZ + CZ, :] = high
            wlo_ref[xx * CZ : xx * CZ + CZ, :] = (both - high.astype(jnp.float32)).astype(jnp.bfloat16)

    kern_w = compact_ref.at[pl.ds(0, CZ)]
    weights()

    def lists():
        index_all().wait_recv()
        elements = index_ref.shape[2]
        shape = (n_lat, elements)
        rel = index_ref[:, 0, :] - lat
        x0 = index_ref[:, 1, :]
        zq = index_ref[:, 2, :] - rad * CZ + HZ + 8
        y0 = index_ref[:, 3, :]
        keep = (rel >= -1) & (rel <= 1) & (zq >= 4) & (zq < WINDOW + 8)
        before = lax.broadcasted_iota(jnp.int32, (elements, elements), 0) < lax.broadcasted_iota(jnp.int32, (elements, elements), 1)
        flags = jnp.where(keep, 1.0, 0.0)
        rank = jnp.dot(flags.astype(jnp.bfloat16), jnp.where(before, 1.0, 0.0).astype(jnp.bfloat16), preferred_element_type=jnp.float32)
        total = jnp.sum(flags, axis=1, keepdims=True).astype(jnp.int32)
        rank = jnp.where(keep, rank, -1.0)
        low = jnp.maximum(x0, jnp.where(rel < 0, HW, 0))
        high = jnp.minimum(x0 + 4, jnp.where(rel > 0, HW - 1, CX - 1))
        code = low + 8 * (high - low + 1)
        lane = lax.broadcasted_iota(jnp.int32, shape, 1)
        fields = [lane, zq, y0, x0, code, jnp.where(rel == 0, 0, 1)]
        fields = [jnp.where(keep, f, 0).astype(jnp.float32) for f in fields]
        slot = lax.broadcasted_iota(jnp.int32, (elements, elements), 0).astype(jnp.float32)
        zero = jnp.zeros((1, elements), jnp.float32)
        for i in range(n_lat):
            stack = jnp.concatenate([f[i : i + 1] for f in fields] + [zero, zero], axis=0).astype(jnp.bfloat16)
            pick = jnp.where(rank[i : i + 1] == slot, 1.0, 0.0).astype(jnp.bfloat16)
            compact_ref[8 * i : 8 * i + 8, :elements] = lax.dot_general(
                stack, pick, (((1,), (1,)), ((), ())), preferred_element_type=jnp.float32)

        def field(f):
            return jnp.concatenate([compact_ref[8 * i + f : 8 * i + f + 1, :elements] for i in range(n_lat)], axis=0).astype(jnp.int32)

        e, zq, y0, x0, code, beside = [field(f) for f in range(6)]
        start = e * NGLL
        row = lax.broadcasted_iota(jnp.int32, shape, 0) * block + 3 * lax.shift_right_logical(start, 7)
        off = start & (LANES - 1)
        words = row | (off << 16) | (((off - 25 * x0) & (LANES - 1)) << 23)
        words_ref[0] = jnp.where(lane == elements - 1, total, words)
        zb = jnp.maximum(lax.shift_right_logical(zq, 2) - 1, 0)
        at = ((beside * Z_BINS + zb) * Y_TILES + lax.shift_right_logical(y0, 4)) * 8
        words_ref[1] = at | ((zq & 7) << 16) | ((y0 & 15) << 20) | (code << 24)

    def when_there(d, up, body):
        zi = z - d if up else z + d

        @pl.when((zi >= 0) & (zi < levels))
        def _():
            body(2 * zi)

    def line(d, up, j):
        more = can_up if up else can_down

        def body(i):
            i = i + x
            if j < CUTS:
                z_move(i, j, up).wait_recv()

                @pl.when(more)
                def _():
                    z_move(i, j, up).start()

                x_move(i, j).start()
                if d == 1:
                    @pl.when(jnp.logical_not(more))
                    def _():
                        y_move(i, j).start()
            elif d > 1:
                z_move(i, j, up).wait_recv()

                @pl.when(more)
                def _():
                    z_move(i, j, up).start()

                if d == levels - 1:
                    x_move(i, j).start()
                if j == 2 * CUTS - 1:
                    k_move(i).start()
            else:
                @pl.when(more)
                def _():
                    z_move(i, j, up).wait_recv()
                    z_move(i, j, up).start()
                    if j == 2 * CUTS - 1:
                        k_move(i).start()

        when_there(d, up, body)

    def cross(d, up, j):
        def body(i):
            i = i + 1 - x
            if j < CUTS:
                x_move(i, j).wait_recv()
                if d < levels - 1:
                    y_move(i, j).start()
            elif d == levels - 1:
                x_move(i, j).wait_recv()
                if j == 2 * CUTS - 1:
                    k_move(i).start()

        when_there(d, up, body)

    def y_done(d, up, own_column):
        def body(i):
            i = i + (x if own_column else 1 - x)

            def finish():
                for j in range(CUTS):
                    y_move(i, CUTS + j).wait_recv()
                k_move(i).start()

            if own_column:
                pl.when(jnp.logical_not(can_up if up else can_down))(finish)
            else:
                finish()

        when_there(d, up, body)

    ways = lambda d: (True, False) if d else (True,)
    for d in range(1, levels + 1):
        for j in range(CUTS):
            if d < levels:
                for up in ways(d):
                    line(d, up, j)
            for up in ways(d - 1):
                cross(d - 1, up, j)
        if d < levels:
            for j in range(CUTS, 2 * CUTS):
                for up in ways(d):
                    line(d, up, j)
        if d == 3:
            lists()
        if d == levels:
            for j in range(CUTS, 2 * CUTS):
                for up in ways(d - 1):
                    cross(d - 1, up, j)
        if d == 2:
            for up in ways(1):
                y_done(1, up, True)
        if 2 <= d <= levels:
            for up in ways(d - 2):
                y_done(d - 2, up, False)

    index_all().wait_send()
    sized(levels * part, xs.at[0], xr.at[0, 0], (across_x, rad)).wait_send()

    @pl.when(at_end)
    def _():
        sized(part, xs.at[1], xr.at[0, 1], (across_x, rad)).wait_send()

    for up in (True, False):
        way = 0 if up else 1
        peer = (lat + (2 if up else -2), rad)

        @pl.when(can_up if up else can_down)
        def _():
            for zi in range(levels):
                passed = (zi <= z) if up else (zi >= z)
                both = zi < levels - 2 if up else zi > 1

                @pl.when(passed)
                def _():
                    sized(2 * part if both else part, zs.at[2 * zi + x, way], zr.at[0, 0], peer).wait_send()

    sized(levels * part, ys, yr.at[0, 0], (lat, across_y)).wait_send()
    everything = sized((n_lat - 1) * half, bs, br, (lat, across_k))
    everything.wait_send()
    everything.wait_recv()


def grid_kernel(n_lat, words_ref, data_ref, whi_ref, wlo_ref, ghi_hbm, glo_hbm, out_hbm, acc0, acc1, acc2, fields, result, words, todo, ghi_ref, glo_ref, sem, smooth_sem, out_sem):
    accs = (acc0, acc1, acc2)
    smooth = [pltpu.make_async_copy(ghi_hbm, ghi_ref, smooth_sem.at[0]), pltpu.make_async_copy(glo_hbm, glo_ref, smooth_sem.at[1])]
    bring = pltpu.make_async_copy(words_ref, words.at[:, pl.ds(0, n_lat), :], sem)
    bring.start()
    for copy in smooth:
        copy.start()
    rows = acc0.shape[0]

    @pl.loop(0, rows // 8, unroll=11)
    def _(r):
        for acc in accs:
            acc[pl.ds(pl.multiple_of(r * 8, 8), 8), :] = jnp.zeros((8, LANES), jnp.float32)

    bring.wait()
    lane = lax.broadcasted_iota(jnp.int32, (8, LANES), 1)
    sub = lax.broadcasted_iota(jnp.int32, (8, LANES), 0)
    across = lane & 15
    along = lax.shift_right_logical(lane, 4)
    ramp = 25 * along
    elements = words.shape[2]

    for u in range(SUM_GROUP):
        words[0, n_lat, u] = 0
        words[1, n_lat, u] = 0

    def listed(i, n):
        many = lax.div(words[0, i, elements - 1] + SUM_GROUP - 1, SUM_GROUP)

        @pl.loop(0, lax.div(many + 7, 8))
        def _(t):
            for u in range(8):
                todo[n + t * 8 + u] = (i << 16) + (t * 8 + u) * SUM_GROUP

        return n + many

    groups = lax.fori_loop(0, n_lat, listed, 0)
    batch = SUM_WAYS // SUM_GROUP
    for u in range(batch):
        todo[groups + u] = n_lat << 16

    @pl.loop(0, lax.div(groups + batch - 1, batch))
    def _(step):
        for g in range(batch):
            first_slot = todo[step * batch + g]
            i = lax.shift_right_logical(first_slot, 16)
            p0 = first_slot & 0xFFFF
            for u in range(SUM_GROUP):
                w0, w1 = words[0, i, p0 + u], words[1, i, p0 + u]
                row = w0 & 0xFFFF
                off = lax.shift_right_logical(w0, 16) & 127
                shift = lax.shift_right_logical(w0, 23)
                at = pl.multiple_of(w1 & 0xFFFF, 8)
                zq = lax.shift_right_logical(w1, 16) & 7
                yl = lax.shift_right_logical(w1, 20) & 15
                low = lax.shift_right_logical(w1, 24) & 7
                wide = lax.shift_right_logical(w1, 27)
                tz = (sub - zq) & 7
                ty = (lane - yl) & 15
                tx = along - low
                index = (ramp + shift + 5 * tz + ty) & (LANES - 1)
                good = (tz < 5) & (ty < 5) & (tx >= 0) & (tx < wide)
                first = across >= yl
                here, there = good & first, good & jnp.logical_not(first)
                head = lane >= off
                for c in range(3):
                    a = jnp.broadcast_to(data_ref[pl.ds(row + c, 1), :], (8, LANES))
                    b = jnp.broadcast_to(data_ref[pl.ds(row + 3 + c, 1), :], (8, LANES))
                    v = jnp.take_along_axis(jnp.where(head, a, b), index, axis=1, mode="promise_in_bounds")
                    accs[c][pl.ds(at, 8), :] += jnp.where(here, v, 0.0)
                    accs[c][pl.ds(at + 8, 8), :] += jnp.where(there, v, 0.0)

    low_half = sub < 4
    for copy in smooth:
        copy.wait()
    for c in range(3):
        acc, field = accs[c], fields.at[c]

        @pl.loop(0, 2, unroll=2)
        def _(g):
            @pl.loop(0, WINDOW // 8, unroll=WINDOW // 8)
            def _(h):
                for side in range(2):
                    v = []
                    for t in range(8):
                        def bins(n):
                            r = ((g * Z_BINS + 2 * h + n) * Y_TILES + side * 8 + t) * 8
                            return acc[pl.ds(pl.multiple_of(r, 8), 8), :]

                        v.append(bins(1) + jnp.where(low_half, bins(0), bins(2)))
                    for bit in (4, 2, 1):
                        straight = (along & bit) == 0
                        w = list(v)
                        for r in range(8):
                            if r & bit:
                                continue
                            a, b = v[r], v[r + bit]
                            if bit == 4:
                                turned = pltpu.roll(jnp.where(straight, b, a), 64, 1)
                                w[r] = jnp.where(straight, a, turned)
                                w[r + bit] = jnp.where(straight, turned, b)
                            else:
                                w[r] = jnp.where(straight, a, pltpu.roll(b, 16 * bit, 1))
                                w[r + bit] = jnp.where(straight, pltpu.roll(a, LANES - 16 * bit, 1), b)
                        v = w
                    for xl in range(8):
                        r = pl.multiple_of(g * (CX * WINDOW) + xl * WINDOW + h * 8, 8)
                        field[pl.ds(r, 8), side * LANES : (side + 1) * LANES] = v[xl]

        def split(a):
            high = a.astype(jnp.bfloat16)
            return high, (a - high.astype(jnp.float32)).astype(jnp.bfloat16)

        def dot(a, b):
            return jnp.dot(a, b, preferred_element_type=jnp.float32)

        high, low = split(field[...])
        whi = whi_ref[...]
        mixed = dot(whi, high) + dot(wlo_ref[...], high) + dot(whi, low)
        high, low = split(mixed)
        ghi = ghi_ref[...]
        done = dot(high, ghi) + dot(low, ghi) + dot(high, glo_ref[...])
        result[c] = done.reshape(CX, CZ, NY)
        pltpu.make_async_copy(result.at[c], out_hbm.at[c], out_sem.at[c]).start()
    for c in range(3):
        pltpu.make_async_copy(result.at[c], out_hbm.at[c], out_sem.at[c]).wait()


def on_device_whole(n_lat, n_rad, kernels, cells, tiles, width_class):
    elements = tiles.shape[0]
    block = -(-kernels.shape[1] // LANES * 3 // 32) * 32
    smem = pl.BlockSpec(memory_space=pltpu.SMEM)
    vmem = pl.BlockSpec(memory_space=pltpu.VMEM)
    hbm = pl.BlockSpec(memory_space=pltpu.HBM)
    dma = pltpu.SemaphoreType.DMA
    stay = functools.partial(pltpu.with_memory_space_constraint, memory_space=pltpu.HBM)
    data, words, whi, wlo = pl.pallas_call(
        functools.partial(gather_kernel, n_lat, n_rad, block),
        out_shape=[
            jax.ShapeDtypeStruct((n_lat * block + 8, LANES), jnp.float32),
            jax.ShapeDtypeStruct((2, n_lat, elements), jnp.int32),
            jax.ShapeDtypeStruct((CX * CZ, DEPTH), jnp.bfloat16),
            jax.ShapeDtypeStruct((CX * CZ, DEPTH), jnp.bfloat16),
        ],
        in_specs=[smem, hbm, hbm, hbm],
        out_specs=[vmem] * 4,
        scratch_shapes=[
            pltpu.VMEM(kernels.shape, jnp.float32),
            pltpu.VMEM((1, elements), jnp.int32),
            pltpu.VMEM(cells.shape, jnp.int32),
            pltpu.VMEM((n_lat, 8, elements), jnp.int32),
            pltpu.VMEM((8 * n_lat, DEPTH), jnp.float32),
            dma((3,)), dma, dma,
            dma((n_lat, 2)), dma((n_lat, 2 * CUTS)), dma((2,)), dma((n_lat, 2 * CUTS)),
            dma, dma((n_lat, CUTS)), dma, dma,
        ],
        compiler_params=pltpu.CompilerParams(
            vmem_limit_bytes=VMEM_LIMIT, collective_id=0, has_side_effects=True
        ),
    )(width_class, *map(stay, (tiles.reshape(1, elements), cells, kernels)))
    smooth = band_matrix(NY, 2.5, HY).T.astype(np.float32)
    high = smooth.astype(jnp.bfloat16)
    low = (smooth - high.astype(np.float32)).astype(jnp.bfloat16)
    rows = 2 * Z_BINS * Y_TILES * 8
    return pl.pallas_call(
        functools.partial(grid_kernel, n_lat),
        out_shape=jax.ShapeDtypeStruct((3, CX, CZ, NY), jnp.float32),
        in_specs=[vmem] * 4 + [hbm] * 2,
        out_specs=hbm,
        scratch_shapes=[
            pltpu.VMEM((rows, LANES), jnp.float32),
            pltpu.VMEM((rows, LANES), jnp.float32),
            pltpu.VMEM((rows, LANES), jnp.float32),
            pltpu.VMEM((3, DEPTH, NY), jnp.float32),
            pltpu.VMEM((3, CX, CZ, NY), jnp.float32),
            pltpu.SMEM((2, n_lat + 1, elements), jnp.int32),
            pltpu.SMEM((n_lat * elements // SUM_GROUP + 16,), jnp.int32),
            pltpu.VMEM((NY, NY), jnp.bfloat16),
            pltpu.VMEM((NY, NY), jnp.bfloat16),
            dma, dma((2,)), dma((3,)),
        ],
        compiler_params=pltpu.CompilerParams(vmem_limit_bytes=VMEM_LIMIT),
    )(words, data, whi, wlo, stay(jnp.asarray(high)), stay(jnp.asarray(low)))


def solution(mesh):
    n_lat, n_rad = mesh.shape["lat"], mesh.shape["rad"]
    whole = n_lat == 8 and n_rad == 4
    return jax.shard_map(
        functools.partial(on_device_whole if whole else on_device, n_lat, n_rad),
        mesh=mesh,
        in_specs=(P(None, "lat"), P(None, "lat"), P("lat", None), P("lat")),
        out_specs=P(None, "lat", "rad", None),
        check_vma=False,
    )
```

```python
import functools

import jax
import jax.numpy as jnp
import numpy as np
from jax import lax
from jax.experimental import pallas as pl
from jax.experimental.pallas import tpu as pltpu
from jax.sharding import PartitionSpec as P

CX = 8
NY = 256
CZ = 32
NGLL = 125
HW = 4
HY = 8
HZ = 4
ZP = CZ + 4 * HZ
LANES = 128
TAPS = 2 * HZ + 1
PADX = CX + 2 * HW
PACK_UNROLL = 4
SUM_UNROLL = 4
VMEM_LIMIT = 48 * 2**20
MESH = pl.DeviceIdType.MESH


def band_matrix(count, sigma, half):
    place = np.arange(count)
    gap = place[None, :] - place[:, None]
    gauss = np.where(np.abs(gap) <= half, np.exp(-(gap**2) / (2.0 * sigma**2)), 0.0)
    return gauss / gauss.sum(axis=1, keepdims=True)


def z_taps(n_rad):
    full = np.pad(band_matrix(CZ * n_rad, 1.5, HZ), ((0, 0), (HZ, HZ)))
    return np.stack([full[z, z : z + TAPS] for z in range(CZ * n_rad)]).astype(np.float32)


def pack_kernel(
    n_lat, n_rad, share, elements, tiles_ref, cells_hbm, kern_hbm, out_ref, count, todo, place, cells_ref, kern_ref, sems
):
    slab = lax.axis_index("rad")
    rows = elements * NGLL // LANES
    bring_cells = pltpu.make_async_copy(cells_hbm, cells_ref, sems.at[0])
    bring_kern = pltpu.make_async_copy(kern_hbm, kern_ref, sems.at[1])
    bring_cells.start()
    bring_kern.start()
    out_ref[...] = jnp.full(out_ref.shape, -1000.0, jnp.float32)
    lane = lax.broadcasted_iota(jnp.int32, (3, LANES), 1)

    @pl.loop(0, n_lat)
    def _(t):
        count[t] = 0

    def listed(e, n):
        t = tiles_ref[e]
        rank = count[t]
        count[t] = rank + 1
        slot = lax.div(rank, n_rad)
        todo[n] = e
        place[n] = t * share + slot
        return n + jnp.where(rank - slot * n_rad == slab, 1, 0)

    n = lax.fori_loop(0, elements, listed, 0, unroll=4)
    for more in range(PACK_UNROLL):
        todo[n + more] = 0
        place[n + more] = n_lat * share
    bring_cells.wait()
    bring_kern.wait()

    def packed(step, _):
        for u in range(PACK_UNROLL):
            e = todo[step * PACK_UNROLL + u]
            at = place[step * PACK_UNROLL + u]
            start = e * NGLL
            row = lax.shift_right_logical(start, 7)
            off = start & (LANES - 1)
            after = jnp.minimum(row + 1, rows - 1)
            a = kern_ref[:, pl.ds(pl.multiple_of(row * LANES, LANES), LANES)]
            b = kern_ref[:, pl.ds(pl.multiple_of(after * LANES, LANES), LANES)]
            v = pltpu.roll(jnp.where(lane >= off, a, b), (LANES - off) & (LANES - 1), 1)
            v = jnp.where(lane == NGLL, cells_ref[0, e].astype(jnp.float32), v)
            v = jnp.where(lane == NGLL + 1, cells_ref[1, e].astype(jnp.float32), v)
            v = jnp.where(lane == NGLL + 2, cells_ref[2, e].astype(jnp.float32), v)
            t = lax.div(at, share)
            slot = at - t * share
            for c in range(3):
                out_ref[t, pl.ds(c * share + slot, 1), :] = v[c : c + 1]
        return 0

    lax.fori_loop(0, lax.div(n + PACK_UNROLL - 1, PACK_UNROLL), packed, 0)


def exchange_kernel(n_lat, n_rad, send_ref, recv_ref, own_sem, send_sem, recv_sem, fwd_sem, got_sem):
    tile, slab = lax.axis_index("lat"), lax.axis_index("rad")
    barrier = pltpu.get_barrier_semaphore()

    @pl.loop(1, n_lat)
    def _(k):
        pl.semaphore_signal(barrier, inc=1, device_id=(lax.rem(tile + k, n_lat), slab), device_id_type=MESH)

    pair = slab + 1 - 2 * lax.rem(slab, 2)
    other = slab + 2 - 4 * lax.div(slab, 2)
    for peer in (pair, other):
        pl.semaphore_signal(barrier, inc=1, device_id=(tile, peer), device_id_type=MESH)
    pl.semaphore_wait(barrier, n_lat - 1 + 2)

    def across(k):
        to = lax.rem(tile + k, n_lat)
        return pltpu.make_async_remote_copy(
            src_ref=send_ref.at[to],
            dst_ref=recv_ref.at[slab, tile],
            send_sem=send_sem.at[k],
            recv_sem=recv_sem.at[k],
            device_id=(to, slab),
            device_id_type=MESH,
        )

    def share(k, of, to, way):
        block = recv_ref.at[of, lax.rem(tile + n_lat - k, n_lat)]
        return pltpu.make_async_remote_copy(
            src_ref=block,
            dst_ref=block,
            send_sem=fwd_sem.at[way, k],
            recv_sem=got_sem.at[way, k],
            device_id=(tile, to),
            device_id_type=MESH,
        )

    def forward(k):
        share(k, slab, other, 0).start()
        share(k, slab, pair, 1).start()

    def relay(k):
        share(k, other, other, 0).wait_recv()
        share(k, other, pair, 2).start()

    @pl.loop(1, n_lat)
    def _(k):
        across(k).start()

    own = pltpu.make_async_copy(send_ref.at[tile], recv_ref.at[slab, tile], own_sem)
    own.start()
    own.wait()
    forward(0)

    @pl.loop(1, n_lat)
    def _(k):
        across(k).wait_recv()
        forward(k)

    @pl.loop(0, n_lat)
    def _(k):
        relay(k)

    @pl.loop(0, n_lat)
    def _(k):
        share(k, pair, pair, 1).wait_recv()
        share(k, other + pair - slab, pair, 2).wait_recv()

    @pl.loop(1, n_lat)
    def _(k):
        across(k).wait_send()

    @pl.loop(0, n_lat)
    def _(k):
        share(k, slab, other, 0).wait_send()
        share(k, slab, pair, 1).wait_send()
        share(k, other, pair, 2).wait_send()


def sum_kernel(blocks, share, meta_ref, recv_ref, acc, todo):
    slab = lax.axis_index("rad")
    slots = blocks * share
    acc[...] = jnp.zeros(acc.shape, jnp.float32)
    lane = lax.broadcasted_iota(jnp.int32, (8, LANES), 1)
    sub = lax.broadcasted_iota(jnp.int32, (8, LANES), 0)
    ramp = 25 * sub + lane
    low = slab * CZ - 2 * HZ

    def listed(s, n):
        zb = meta_ref[slots + s] - low
        todo[n] = s
        return n + jnp.where((zb >= 0) & (zb < CZ + 3 * HZ), 1, 0)

    n = lax.fori_loop(0, slots, listed, 0, unroll=8)
    for more in range(SUM_UNROLL):
        todo[n + more] = 0

    def place(at, values, index, mask):
        for j in range(5):
            picked = jnp.where(mask, index + 5 * j, NGLL)
            for c in range(3):
                piece = jnp.take_along_axis(values[c], picked, axis=1, mode="promise_in_bounds")
                acc[pl.ds(pl.multiple_of(at + (3 * j + c) * 8, 8), 8), :] += piece

    def summed(step, _):
        later = []
        for u in range(SUM_UNROLL):
            s = todo[step * SUM_UNROLL + u]
            good = step * SUM_UNROLL + u < n
            x0 = jnp.clip(meta_ref[s], 0, CX - 5)
            zb = jnp.clip(meta_ref[slots + s] - low, 0, CZ + 3 * HZ - 1)
            y0 = jnp.clip(meta_ref[2 * slots + s], 0, NY - 5)
            block = lax.div(s, share)
            slot = s - block * share
            values = []
            for c in range(3):
                row = jnp.broadcast_to(recv_ref[block, pl.ds(c * share + slot, 1), :], (8, LANES))
                values.append(jnp.where(lane < NGLL, row, 0.0))
            half = lax.shift_right_logical(y0, 7)
            yl = y0 & (LANES - 1)
            index = ramp - (25 * x0 + yl)
            rows = (sub >= x0) & (sub < jnp.where(good, x0 + 5, 0))
            at = (half * ZP + zb) * 24
            place(at, values, index, rows & (lane >= yl) & (lane < yl + 5))
            later.append((at, values, index, rows, yl))
        widest = functools.reduce(jnp.maximum, [entry[4] for entry in later])

        @pl.when(widest > LANES - 5)
        def _():
            for at, values, index, rows, yl in later:
                over = rows & (lane < yl + 5 - LANES)

                @pl.when(yl > LANES - 5)
                def _():
                    place(at + ZP * 24, values, index + LANES, over)

        return 0

    lax.fori_loop(0, lax.div(n + SUM_UNROLL - 1, SUM_UNROLL), summed, 0)


def finish_kernel(n_lat, taps_ref, wx_ref, acc, wy_ref, out_ref, planes, rows_ref, send_sem, recv_sem):
    tile, slab = lax.axis_index("lat"), lax.axis_index("rad")
    barrier = pltpu.get_barrier_semaphore()
    has_prev, has_next = tile > 0, tile < n_lat - 1
    halo = HW * CZ

    @pl.when(has_prev)
    def _():
        pl.semaphore_signal(barrier, inc=1, device_id=(tile - 1, slab), device_id_type=MESH)

    @pl.when(has_next)
    def _():
        pl.semaphore_signal(barrier, inc=1, device_id=(tile + 1, slab), device_id_type=MESH)

    def at(c, row, count):
        return rows_ref.at[:, pl.ds(c * PADX * CZ + row, count), :]

    def to_next(c):
        return pltpu.make_async_remote_copy(
            src_ref=at(c, CX * CZ, halo),
            dst_ref=at(c, 0, halo),
            send_sem=send_sem.at[0, c],
            recv_sem=recv_sem.at[0, c],
            device_id=(tile + 1, slab),
            device_id_type=MESH,
        )

    def to_prev(c):
        return pltpu.make_async_remote_copy(
            src_ref=at(c, halo, halo),
            dst_ref=at(c, halo + CX * CZ, halo),
            send_sem=send_sem.at[1, c],
            recv_sem=recv_sem.at[1, c],
            device_id=(tile - 1, slab),
            device_id_type=MESH,
        )

    for c in range(3):

        @pl.loop(0, CZ, unroll=4)
        def _(z):
            for half in range(NY // LANES):
                total = jnp.zeros((CX, LANES), jnp.float32)
                for d in range(TAPS):
                    weight = taps_ref[(slab * CZ + z) * TAPS + d]
                    row = pl.multiple_of(((half * ZP + z + HZ + d) * 3 + c) * CX, 8)
                    total = total + weight * acc[pl.ds(row, CX), :]
                cols = slice(half * LANES, (half + 1) * LANES)
                planes[pl.ds(pl.multiple_of(z * CX, 8), CX), cols] = total

        product = jnp.dot(planes[...], wy_ref[...], precision=lax.Precision.HIGHEST)
        for z in range(CZ):
            for half in range(NY // LANES):
                piece = product[z * CX : (z + 1) * CX, half * LANES : (half + 1) * LANES]
                rows_ref[half, pl.ds(c * PADX * CZ + halo + z, CX, stride=CZ), :] = piece

        if c == 0:
            beside = jnp.minimum(tile, 1) + jnp.minimum(n_lat - 1 - tile, 1)
            pl.semaphore_wait(barrier, beside)

        @pl.when(has_next)
        def _():
            to_next(c).start()

        @pl.when(has_prev)
        def _():
            to_prev(c).start()

        zeros = jnp.zeros((NY // LANES, halo, LANES), jnp.float32)

        @pl.when(tile == 0)
        def _():
            rows_ref[:, c * PADX * CZ : c * PADX * CZ + halo, :] = zeros

        @pl.when(tile == n_lat - 1)
        def _():
            rows_ref[:, c * PADX * CZ + halo + CX * CZ : (c + 1) * PADX * CZ, :] = zeros

    for c in range(3):

        @pl.when(has_prev)
        def _():
            to_next(c).wait_recv()

        @pl.when(has_next)
        def _():
            to_prev(c).wait_recv()

        @pl.loop(0, CX)
        def _(x):
            for half in range(NY // LANES):
                total = jnp.zeros((CZ, LANES), jnp.float32)
                for d in range(2 * HW + 1):
                    row = pl.multiple_of(c * PADX * CZ + (x + d) * CZ, 8)
                    total = total + wx_ref[x * (2 * HW + 1) + d] * rows_ref[half, pl.ds(row, CZ), :]
                out_ref[c, x, :, half * LANES : (half + 1) * LANES] = total

    for c in range(3):

        @pl.when(has_next)
        def _():
            to_next(c).wait_send()

        @pl.when(has_prev)
        def _():
            to_prev(c).wait_send()


def x_weights(width_class, n_lat):
    rows = lax.axis_index("lat") * CX + jnp.arange(CX)
    sigma = 1.0 + 0.75 * width_class[0].astype(jnp.float32)
    offsets = jnp.arange(-HW, HW + 1)
    target = rows[:, None] + offsets[None, :]
    valid = (target >= 0) & (target < CX * n_lat)
    gauss = jnp.exp(-(offsets[None, :].astype(jnp.float32) ** 2) / (2.0 * sigma**2))
    gauss = jnp.where(valid, gauss, 0.0)
    return gauss / jnp.sum(gauss, axis=1, keepdims=True)


def on_device(n_lat, n_rad, kernels, cells, tiles, width_class):
    elements = tiles.shape[0]
    cap = max(2, 2 * elements // n_lat)
    share = -(-cap // n_rad)
    blocks = n_rad * n_lat
    slots = blocks * share
    params = pltpu.CompilerParams(vmem_limit_bytes=VMEM_LIMIT)
    smem = pl.BlockSpec(memory_space=pltpu.SMEM)
    vmem = pl.BlockSpec(memory_space=pltpu.VMEM)
    hbm = pl.BlockSpec(memory_space=pl.ANY)
    send = pl.pallas_call(
        functools.partial(pack_kernel, n_lat, n_rad, share, elements),
        out_shape=jax.ShapeDtypeStruct((n_lat + 1, 3 * share, LANES), jnp.float32),
        in_specs=[smem, hbm, hbm],
        out_specs=vmem,
        scratch_shapes=[
            pltpu.SMEM((n_lat,), jnp.int32),
            pltpu.SMEM((elements + PACK_UNROLL,), jnp.int32),
            pltpu.SMEM((elements + PACK_UNROLL,), jnp.int32),
            pltpu.SMEM(cells.shape, jnp.int32),
            pltpu.VMEM(kernels.shape, jnp.float32),
            pltpu.SemaphoreType.DMA((2,)),
        ],
        compiler_params=params,
    )(tiles.reshape(-1), cells, kernels)
    recv = pl.pallas_call(
        functools.partial(exchange_kernel, n_lat, n_rad),
        out_shape=jax.ShapeDtypeStruct((n_rad, n_lat, 3 * share, LANES), jnp.float32),
        in_specs=[vmem],
        out_specs=vmem,
        scratch_shapes=[
            pltpu.SemaphoreType.DMA,
            pltpu.SemaphoreType.DMA((n_lat,)),
            pltpu.SemaphoreType.DMA((n_lat,)),
            pltpu.SemaphoreType.DMA((3, n_lat)),
            pltpu.SemaphoreType.DMA((3, n_lat)),
        ],
        compiler_params=pltpu.CompilerParams(
            vmem_limit_bytes=VMEM_LIMIT, collective_id=0, has_side_effects=True
        ),
    )(send)
    recv = recv.reshape(blocks, 3 * share, LANES)
    meta = recv[:, :share, NGLL:].transpose(2, 0, 1).reshape(-1).astype(jnp.int32)
    grid_rows = NY // LANES * ZP * 24
    summed = pl.pallas_call(
        functools.partial(sum_kernel, blocks, share),
        out_shape=jax.ShapeDtypeStruct((grid_rows, LANES), jnp.float32),
        in_specs=[smem, vmem],
        out_specs=vmem,
        scratch_shapes=[pltpu.SMEM((slots + SUM_UNROLL,), jnp.int32)],
        compiler_params=params,
    )(meta, recv)
    return pl.pallas_call(
        functools.partial(finish_kernel, n_lat),
        out_shape=jax.ShapeDtypeStruct((3, CX, CZ, NY), jnp.float32),
        in_specs=[smem, smem, vmem, vmem],
        out_specs=vmem,
        scratch_shapes=[
            pltpu.VMEM((CZ * CX, NY), jnp.float32),
            pltpu.VMEM((NY // LANES, 3 * PADX * CZ, LANES), jnp.float32),
            pltpu.SemaphoreType.DMA((2, 3)),
            pltpu.SemaphoreType.DMA((2, 3)),
        ],
        compiler_params=pltpu.CompilerParams(
            vmem_limit_bytes=VMEM_LIMIT, collective_id=1, has_side_effects=True
        ),
    )(
        jnp.asarray(z_taps(n_rad).reshape(-1)),
        x_weights(width_class, n_lat).reshape(-1),
        summed,
        jnp.asarray(band_matrix(NY, 2.5, HY).T.astype(np.float32)),
    )

ROW_TILES = 3
Z_BINS = 11
Y_TILES = 17
WINDOW = CZ + 2 * HZ
DEPTH = 2 * CX * WINDOW
SUM_WAYS = 16
SUM_GROUP = 4
CUTS = 3


def gather_kernel(n_lat, n_rad, block, width_ref, tiles_hbm, cells_hbm, kern_hbm, data_ref, words_ref, whi_ref, wlo_ref,
                  kern_ref, tiles_ref, cells_ref, index_ref, compact_ref, in_sem, is_sem, ir_sem, zs, zr, xs, xr, ys, yr, bs, br):
    lat, rad = lax.axis_index("lat"), lax.axis_index("rad")
    levels = n_lat // 2
    z, x = lax.div(lat, 2), lax.rem(lat, 2)
    y, k = lax.div(rad, 2), lax.rem(rad, 2)
    across_x, across_y, across_k = lat + 1 - 2 * x, rad + 2 - 4 * y, rad + 1 - 2 * k
    barrier = pltpu.get_barrier_semaphore()

    @pl.loop(1, n_lat)
    def _(step):
        pl.semaphore_signal(barrier, inc=1, device_id=(lax.rem(lat + step, n_lat), rad), device_id_type=MESH)

    for peer in (across_y, across_k):
        pl.semaphore_signal(barrier, inc=1, device_id=(lat, peer), device_id_type=MESH)
    brought = [
        pltpu.make_async_copy(kern_hbm, kern_ref, in_sem.at[0]),
        pltpu.make_async_copy(tiles_hbm, tiles_ref, in_sem.at[1]),
        pltpu.make_async_copy(cells_hbm, cells_ref, in_sem.at[2]),
    ]
    for copy in brought:
        copy.start()

    half = block // 2
    part = half // 2
    mine = k * half
    piece = part // CUTS
    starts = [mine + (y if j < CUTS else 1 - y) * part + j % CUTS * piece for j in range(2 * CUTS)]

    def move(row, count, send_sem, recv_sem, device):
        rows = data_ref.at[pl.ds(pl.multiple_of(row, 8), count)]
        return pltpu.make_async_remote_copy(
            src_ref=rows, dst_ref=rows, send_sem=send_sem, recv_sem=recv_sem,
            device_id=device, device_id_type=MESH)

    def z_move(i, j, up):
        way = 0 if up else 1
        return move(i * block + starts[j], piece, zs.at[i, way], zr.at[i, j], (lat + (2 if up else -2), rad))

    def x_move(i, j):
        return move(i * block + starts[j], piece, xs.at[j // CUTS], xr.at[i, j], (across_x, rad))

    def y_move(i, j):
        return move(i * block + starts[j], piece, ys, yr.at[i, j % CUTS], (lat, across_y))

    def k_move(i):
        return move(i * block + mine, half, bs, br, (lat, across_k))

    def sized(rows, send_sem, recv_sem, device):
        return move(0, rows, send_sem, recv_sem, device)

    def index_move(step):
        to = lax.rem(lat + step, n_lat)
        return pltpu.make_async_remote_copy(
            src_ref=index_ref.at[lat], dst_ref=index_ref.at[lat], send_sem=is_sem, recv_sem=ir_sem,
            device_id=(to, rad), device_id_type=MESH)

    def index_all():
        others = index_ref.at[pl.ds(0, n_lat - 1)]
        return pltpu.make_async_remote_copy(
            src_ref=others, dst_ref=others, send_sem=is_sem, recv_sem=ir_sem,
            device_id=(across_x, rad), device_id_type=MESH)

    can_up, can_down = z < levels - 1, z > 0
    at_end = (z == 0) | (z == levels - 1)
    long_up, long_down = z < levels - 2, z > 1
    brought[1].wait()
    brought[2].wait()
    index_ref[lat] = jnp.concatenate([tiles_ref[...], cells_ref[...], jnp.zeros((4, tiles_ref.shape[1]), jnp.int32)], axis=0)
    brought[0].wait()
    base = pl.multiple_of(lat * block, 8)
    lane_tiles = kern_ref.shape[1] // LANES
    groups = lane_tiles // 8

    def packed(at, row, count):
        rows = [kern_ref[:, pl.ds(pl.multiple_of(at + u * LANES, LANES), LANES)] for u in range(count)]
        return jnp.concatenate(rows, axis=0)

    @pl.loop(0, groups, unroll=4)
    def _(g):
        data_ref[pl.ds(base + pl.multiple_of(g * 24, 8), 24), :] = packed(g * 8 * LANES, 0, 8)

    left = lane_tiles - groups * 8
    if left:
        tail = packed(groups * 8 * LANES, 0, left)
        room = block - groups * 24
        tail = jnp.concatenate([tail, jnp.zeros((room - 3 * left, LANES), jnp.float32)], axis=0)
        data_ref[pl.ds(base + groups * 24, room), :] = tail
    pl.semaphore_wait(barrier, n_lat - 1 + 2)

    def own_z(j, up):
        able = (long_up if up else long_down) if j >= CUTS else (can_up if up else can_down)

        @pl.when(able)
        def _():
            z_move(lat, j, up).start()

    for j in range(CUTS):
        own_z(j, True)
        own_z(j, False)
        x_move(lat, j).start()
    for j in range(CUTS, 2 * CUTS):
        for up in (True, False):
            if j == CUTS:
                own_z(j, up)
            else:
                pl.when(z == (0 if up else levels - 1))(functools.partial(own_z, j, up))

    @pl.loop(1, n_lat)
    def _(step):
        index_move(step).start()

    def weights():
        col = lax.broadcasted_iota(jnp.int32, (8, DEPTH), 1)
        beside = col >= CX * WINDOW
        rest = jnp.where(beside, col - CX * WINDOW, col)
        xl = lax.shift_right_logical(rest * 1639, 16)
        zc = rest - WINDOW * xl
        place = jnp.where(beside, jnp.where(xl < HW, xl + CX, xl - CX), xl)
        sub = lax.broadcasted_iota(jnp.int32, (8, DEPTH), 0)
        sigma = 1.0 + 0.75 * jnp.full((8, DEPTH), width_ref[0], jnp.int32).astype(jnp.float32)
        twice = 2.0 * sigma * sigma

        def bell(d, reach, scale):
            square = (d * d).astype(jnp.float32)
            return jnp.where(jnp.abs(d) <= reach, jnp.exp(-square / scale), 0.0)

        norm = jnp.zeros((8, DEPTH), jnp.float32)
        for d in range(-HW, HW + 1):
            at = lat * CX + sub + d
            norm += jnp.where((at >= 0) & (at < CX * n_lat), jnp.exp(-float(d * d) / twice), 0.0)
        wx = bell(place - sub, HW, twice) / norm
        for zv in range(CZ // 8):
            norm = jnp.zeros((8, DEPTH), jnp.float32)
            zz = sub + 8 * zv
            for d in range(-HZ, HZ + 1):
                at = rad * CZ + zz + d
                norm += jnp.where((at >= 0) & (at < CZ * n_rad), float(np.exp(-d * d / 4.5)), 0.0)
            kern_w[zv * 8 : zv * 8 + 8, :] = bell(zc - HZ - zz, HZ, 4.5) / norm
        for xx in range(CX):
            both = kern_w[...] * wx[xx : xx + 1, :]
            high = both.astype(jnp.bfloat16)
            whi_ref[xx * CZ : xx * CZ + CZ, :] = high
            wlo_ref[xx * CZ : xx * CZ + CZ, :] = (both - high.astype(jnp.float32)).astype(jnp.bfloat16)

    kern_w = compact_ref.at[pl.ds(0, CZ)]
    weights()

    def lists():
        index_all().wait_recv()
        elements = index_ref.shape[2]
        shape = (n_lat, elements)
        rel = index_ref[:, 0, :] - lat
        x0 = index_ref[:, 1, :]
        zq = index_ref[:, 2, :] - rad * CZ + HZ + 8
        y0 = index_ref[:, 3, :]
        keep = (rel >= -1) & (rel <= 1) & (zq >= 4) & (zq < WINDOW + 8)
        before = lax.broadcasted_iota(jnp.int32, (elements, elements), 0) < lax.broadcasted_iota(jnp.int32, (elements, elements), 1)
        flags = jnp.where(keep, 1.0, 0.0)
        rank = jnp.dot(flags.astype(jnp.bfloat16), jnp.where(before, 1.0, 0.0).astype(jnp.bfloat16), preferred_element_type=jnp.float32)
        total = jnp.sum(flags, axis=1, keepdims=True).astype(jnp.int32)
        rank = jnp.where(keep, rank, -1.0)
        low = jnp.maximum(x0, jnp.where(rel < 0, HW, 0))
        high = jnp.minimum(x0 + 4, jnp.where(rel > 0, HW - 1, CX - 1))
        code = low + 8 * (high - low + 1)
        lane = lax.broadcasted_iota(jnp.int32, shape, 1)
        fields = [lane, zq, y0, x0, code, jnp.where(rel == 0, 0, 1)]
        fields = [jnp.where(keep, f, 0).astype(jnp.float32) for f in fields]
        slot = lax.broadcasted_iota(jnp.int32, (elements, elements), 0).astype(jnp.float32)
        zero = jnp.zeros((1, elements), jnp.float32)
        for i in range(n_lat):
            stack = jnp.concatenate([f[i : i + 1] for f in fields] + [zero, zero], axis=0).astype(jnp.bfloat16)
            pick = jnp.where(rank[i : i + 1] == slot, 1.0, 0.0).astype(jnp.bfloat16)
            compact_ref[8 * i : 8 * i + 8, :elements] = lax.dot_general(
                stack, pick, (((1,), (1,)), ((), ())), preferred_element_type=jnp.float32)

        def field(f):
            return jnp.concatenate([compact_ref[8 * i + f : 8 * i + f + 1, :elements] for i in range(n_lat)], axis=0).astype(jnp.int32)

        e, zq, y0, x0, code, beside = [field(f) for f in range(6)]
        start = e * NGLL
        row = lax.broadcasted_iota(jnp.int32, shape, 0) * block + 3 * lax.shift_right_logical(start, 7)
        off = start & (LANES - 1)
        words = row | (off << 16) | (((off - 25 * x0) & (LANES - 1)) << 23)
        words_ref[0] = jnp.where(lane == elements - 1, total, words)
        zb = jnp.maximum(lax.shift_right_logical(zq, 2) - 1, 0)
        at = ((beside * Z_BINS + zb) * Y_TILES + lax.shift_right_logical(y0, 4)) * 8
        words_ref[1] = at | ((zq & 7) << 12) | ((y0 & 127) << 16) | (code << 24)

    def when_there(d, up, body):
        zi = z - d if up else z + d

        @pl.when((zi >= 0) & (zi < levels))
        def _():
            body(2 * zi)

    def later_own():
        for j in range(CUTS + 1, 2 * CUTS):
            for up in (True, False):
                pl.when(z != (0 if up else levels - 1))(functools.partial(own_z, j, up))

    def extra(d, up, farthest):
        end = (z == d) if up else (z == levels - 1 - d)

        @pl.when(end if farthest else jnp.logical_not(end))
        def _():
            for j in range(CUTS, 2 * CUTS):
                line(d, up, j)

    def line(d, up, j):
        more = can_up if up else can_down

        def body(i):
            i = i + x
            if j < CUTS:
                z_move(i, j, up).wait_recv()

                @pl.when(more)
                def _():
                    z_move(i, j, up).start()

                x_move(i, j).start()
                if d == 1:
                    @pl.when(jnp.logical_not(more))
                    def _():
                        y_move(i, j).start()
            elif d > 1:
                z_move(i, j, up).wait_recv()

                @pl.when(more)
                def _():
                    z_move(i, j, up).start()

                if d == levels - 1:
                    x_move(i, j).start()
                if j == 2 * CUTS - 1:
                    k_move(i).start()
            else:
                @pl.when(more)
                def _():
                    z_move(i, j, up).wait_recv()
                    z_move(i, j, up).start()
                    if j == 2 * CUTS - 1:
                        k_move(i).start()

        when_there(d, up, body)

    def cross(d, up, j):
        def body(i):
            i = i + 1 - x
            if j < CUTS:
                x_move(i, j).wait_recv()
                if d < levels - 1:
                    y_move(i, j).start()
            elif d == levels - 1:
                x_move(i, j).wait_recv()
                if j == 2 * CUTS - 1:
                    k_move(i).start()

        when_there(d, up, body)

    def y_done(d, up, own_column):
        def body(i):
            i = i + (x if own_column else 1 - x)

            def finish():
                for j in range(CUTS):
                    y_move(i, CUTS + j).wait_recv()
                k_move(i).start()

            if own_column:
                pl.when(jnp.logical_not(can_up if up else can_down))(finish)
            else:
                finish()

        when_there(d, up, body)

    ways = lambda d: (True, False) if d else (True,)
    for d in range(1, levels + 1):
        for j in range(CUTS):
            if d < levels:
                for up in ways(d):
                    line(d, up, j)
            for up in ways(d - 1):
                cross(d - 1, up, j)
            if d == 3 and j == 0:
                for up in ways(1):
                    extra(1, up, False)
        if d < levels:
            for up in ways(d):
                extra(d, up, True)
        if d == 1:
            later_own()
        if d == 3:
            for up in ways(2):
                extra(2, up, False)
            lists()
        if d == levels:
            for j in range(CUTS, 2 * CUTS):
                for up in ways(d - 1):
                    cross(d - 1, up, j)
        if d == 2:
            for up in ways(1):
                y_done(1, up, True)
        if 2 <= d <= levels:
            for up in ways(d - 2):
                y_done(d - 2, up, False)

    index_all().wait_send()
    sized(levels * part, xs.at[0], xr.at[0, 0], (across_x, rad)).wait_send()

    @pl.when(at_end)
    def _():
        sized(part, xs.at[1], xr.at[0, 1], (across_x, rad)).wait_send()

    for up in (True, False):
        way = 0 if up else 1
        peer = (lat + (2 if up else -2), rad)

        @pl.when(can_up if up else can_down)
        def _():
            for zi in range(levels):
                passed = (zi <= z) if up else (zi >= z)
                both = zi < levels - 2 if up else zi > 1

                @pl.when(passed)
                def _():
                    sized(2 * part if both else part, zs.at[2 * zi + x, way], zr.at[0, 0], peer).wait_send()

    sized(levels * part, ys, yr.at[0, 0], (lat, across_y)).wait_send()
    everything = sized((n_lat - 1) * half, bs, br, (lat, across_k))
    everything.wait_send()
    everything.wait_recv()


def grid_kernel(n_lat, words_ref, data_ref, whi_ref, wlo_ref, ghi_hbm, glo_hbm, out_hbm, acc0, acc1, acc2, fields, result, words, todo, ghi_ref, glo_ref, sem, smooth_sem, out_sem):
    accs = (acc0, acc1, acc2)
    smooth = [pltpu.make_async_copy(ghi_hbm, ghi_ref, smooth_sem.at[0]), pltpu.make_async_copy(glo_hbm, glo_ref, smooth_sem.at[1])]
    bring = pltpu.make_async_copy(words_ref, words.at[:, pl.ds(0, n_lat), :], sem)
    bring.start()
    for copy in smooth:
        copy.start()
    rows = acc0.shape[0]

    @pl.loop(0, rows // 8, unroll=11)
    def _(r):
        for acc in accs:
            acc[pl.ds(pl.multiple_of(r * 8, 8), 8), :] = jnp.zeros((8, LANES), jnp.float32)

    bring.wait()
    lane = lax.broadcasted_iota(jnp.int32, (8, LANES), 1)
    sub = lax.broadcasted_iota(jnp.int32, (8, LANES), 0)
    across = lane & 15
    along = lax.shift_right_logical(lane, 4)
    elements = words.shape[2]

    for u in range(SUM_GROUP):
        words[0, n_lat, u] = 0
        words[1, n_lat, u] = 0

    def listed(i, n):
        many = lax.div(words[0, i, elements - 1] + SUM_GROUP - 1, SUM_GROUP)

        @pl.loop(0, lax.div(many + 7, 8))
        def _(t):
            for u in range(8):
                todo[n + t * 8 + u] = (i << 16) + (t * 8 + u) * SUM_GROUP

        return n + many

    groups = lax.fori_loop(0, n_lat, listed, 0)
    batch = SUM_WAYS // SUM_GROUP
    for u in range(batch):
        todo[groups + u] = n_lat << 16

    @pl.loop(0, lax.div(groups + batch - 1, batch))
    def _(step):
        for g in range(batch):
            first_slot = todo[step * batch + g]
            i = lax.shift_right_logical(first_slot, 16)
            p0 = first_slot & 0xFFFF
            for u in range(SUM_GROUP):
                w0, w1 = words[0, i, p0 + u], words[1, i, p0 + u]
                row = w0 & 0xFFFF
                off = lax.shift_right_logical(w0, 16) & 127
                shift = lax.shift_right_logical(w0, 23)
                at = pl.multiple_of(w1 & 0xFFF, 8)
                zq = lax.shift_right_logical(w1, 12) & 7
                y0 = lax.shift_right_logical(w1, 16) & 127
                low = lax.shift_right_logical(w1, 24) & 7
                wide = lax.shift_right_logical(w1, 27)
                tz = (sub - zq) & 7
                turned = (lane - y0) & (LANES - 1)
                ty = turned & 15
                xl = lax.shift_right_logical(turned, 4)
                tx = xl - low
                index = (25 * xl + shift + 5 * tz + ty) & (LANES - 1)
                good = (tz < 5) & (ty < 5) & (tx >= 0) & (tx < wide)
                first = across >= (y0 & 15)
                here, there = good & first, good & jnp.logical_not(first)
                head = lane >= off
                for c in range(3):
                    a = jnp.broadcast_to(data_ref[pl.ds(row + c, 1), :], (8, LANES))
                    b = jnp.broadcast_to(data_ref[pl.ds(row + 3 + c, 1), :], (8, LANES))
                    v = jnp.take_along_axis(jnp.where(head, a, b), index, axis=1, mode="promise_in_bounds")
                    accs[c][pl.ds(at, 8), :] += jnp.where(here, v, 0.0)
                    accs[c][pl.ds(at + 8, 8), :] += jnp.where(there, v, 0.0)

    low_half = sub < 4
    for copy in smooth:
        copy.wait()
    for c in range(3):
        acc, field = accs[c], fields.at[c]

        @pl.loop(0, 2, unroll=2)
        def _(g):
            @pl.loop(0, WINDOW // 8, unroll=WINDOW // 8)
            def _(h):
                for side in range(2):
                    v = []
                    for t in range(8):
                        def bins(n):
                            r = ((g * Z_BINS + 2 * h + n) * Y_TILES + side * 8 + t) * 8
                            return acc[pl.ds(pl.multiple_of(r, 8), 8), :]

                        v.append(bins(1) + jnp.where(low_half, bins(0), bins(2)))
                    for bit in (1, 2, 4):
                        v = [jnp.where((along & bit) == 0, v[t], v[(t + bit) % 8]) for t in range(8)]
                    v = [v[0]] + [pltpu.roll(v[8 - xl], LANES - 16 * xl, 1) for xl in range(1, 8)]
                    for xl in range(8):
                        r = pl.multiple_of(g * (CX * WINDOW) + xl * WINDOW + h * 8, 8)
                        field[pl.ds(r, 8), side * LANES : (side + 1) * LANES] = v[xl]

        def split(a):
            high = a.astype(jnp.bfloat16)
            return high, (a - high.astype(jnp.float32)).astype(jnp.bfloat16)

        def dot(a, b):
            return jnp.dot(a, b, preferred_element_type=jnp.float32)

        high, low = split(field[...])
        whi = whi_ref[...]
        mixed = dot(whi, high) + dot(wlo_ref[...], high) + dot(whi, low)
        high, low = split(mixed)
        ghi = ghi_ref[...]
        done = dot(high, ghi) + dot(low, ghi) + dot(high, glo_ref[...])
        result[c] = done.reshape(CX, CZ, NY)
        pltpu.make_async_copy(result.at[c], out_hbm.at[c], out_sem.at[c]).start()
    for c in range(3):
        pltpu.make_async_copy(result.at[c], out_hbm.at[c], out_sem.at[c]).wait()


def on_device_whole(n_lat, n_rad, kernels, cells, tiles, width_class):
    elements = tiles.shape[0]
    block = -(-kernels.shape[1] // LANES * 3 // 32) * 32
    smem = pl.BlockSpec(memory_space=pltpu.SMEM)
    vmem = pl.BlockSpec(memory_space=pltpu.VMEM)
    hbm = pl.BlockSpec(memory_space=pltpu.HBM)
    dma = pltpu.SemaphoreType.DMA
    stay = functools.partial(pltpu.with_memory_space_constraint, memory_space=pltpu.HBM)
    data, words, whi, wlo = pl.pallas_call(
        functools.partial(gather_kernel, n_lat, n_rad, block),
        out_shape=[
            jax.ShapeDtypeStruct((n_lat * block + 8, LANES), jnp.float32),
            jax.ShapeDtypeStruct((2, n_lat, elements), jnp.int32),
            jax.ShapeDtypeStruct((CX * CZ, DEPTH), jnp.bfloat16),
            jax.ShapeDtypeStruct((CX * CZ, DEPTH), jnp.bfloat16),
        ],
        in_specs=[smem, hbm, hbm, hbm],
        out_specs=[vmem] * 4,
        scratch_shapes=[
            pltpu.VMEM(kernels.shape, jnp.float32),
            pltpu.VMEM((1, elements), jnp.int32),
            pltpu.VMEM(cells.shape, jnp.int32),
            pltpu.VMEM((n_lat, 8, elements), jnp.int32),
            pltpu.VMEM((8 * n_lat, DEPTH), jnp.float32),
            dma((3,)), dma, dma,
            dma((n_lat, 2)), dma((n_lat, 2 * CUTS)), dma((2,)), dma((n_lat, 2 * CUTS)),
            dma, dma((n_lat, CUTS)), dma, dma,
        ],
        compiler_params=pltpu.CompilerParams(
            vmem_limit_bytes=VMEM_LIMIT, collective_id=0, has_side_effects=True
        ),
    )(width_class, *map(stay, (tiles.reshape(1, elements), cells, kernels)))
    smooth = band_matrix(NY, 2.5, HY).T.astype(np.float32)
    high = smooth.astype(jnp.bfloat16)
    low = (smooth - high.astype(np.float32)).astype(jnp.bfloat16)
    rows = 2 * Z_BINS * Y_TILES * 8
    return pl.pallas_call(
        functools.partial(grid_kernel, n_lat),
        out_shape=jax.ShapeDtypeStruct((3, CX, CZ, NY), jnp.float32),
        in_specs=[vmem] * 4 + [hbm] * 2,
        out_specs=hbm,
        scratch_shapes=[
            pltpu.VMEM((rows, LANES), jnp.float32),
            pltpu.VMEM((rows, LANES), jnp.float32),
            pltpu.VMEM((rows, LANES), jnp.float32),
            pltpu.VMEM((3, DEPTH, NY), jnp.float32),
            pltpu.VMEM((3, CX, CZ, NY), jnp.float32),
            pltpu.SMEM((2, n_lat + 1, elements), jnp.int32),
            pltpu.SMEM((n_lat * elements // SUM_GROUP + 16,), jnp.int32),
            pltpu.VMEM((NY, NY), jnp.bfloat16),
            pltpu.VMEM((NY, NY), jnp.bfloat16),
            dma, dma((2,)), dma((3,)),
        ],
        compiler_params=pltpu.CompilerParams(vmem_limit_bytes=VMEM_LIMIT),
    )(words, data, whi, wlo, stay(jnp.asarray(high)), stay(jnp.asarray(low)))


def solution(mesh):
    n_lat, n_rad = mesh.shape["lat"], mesh.shape["rad"]
    whole = n_lat == 8 and n_rad == 4
    return jax.shard_map(
        functools.partial(on_device_whole if whole else on_device, n_lat, n_rad),
        mesh=mesh,
        in_specs=(P(None, "lat"), P(None, "lat"), P("lat", None), P("lat")),
        out_specs=P(None, "lat", "rad", None),
        check_vma=False,
    )
```

```python
import functools

import jax
import jax.numpy as jnp
import numpy as np
from jax import lax
from jax.experimental import pallas as pl
from jax.experimental.pallas import tpu as pltpu
from jax.sharding import PartitionSpec as P

CX = 8
NY = 256
CZ = 32
NGLL = 125
HW = 4
HY = 8
HZ = 4
ZP = CZ + 4 * HZ
LANES = 128
TAPS = 2 * HZ + 1
PADX = CX + 2 * HW
PACK_UNROLL = 4
SUM_UNROLL = 4
VMEM_LIMIT = 48 * 2**20
MESH = pl.DeviceIdType.MESH


def band_matrix(count, sigma, half):
    place = np.arange(count)
    gap = place[None, :] - place[:, None]
    gauss = np.where(np.abs(gap) <= half, np.exp(-(gap**2) / (2.0 * sigma**2)), 0.0)
    return gauss / gauss.sum(axis=1, keepdims=True)


def z_taps(n_rad):
    full = np.pad(band_matrix(CZ * n_rad, 1.5, HZ), ((0, 0), (HZ, HZ)))
    return np.stack([full[z, z : z + TAPS] for z in range(CZ * n_rad)]).astype(np.float32)


def pack_kernel(
    n_lat, n_rad, share, elements, tiles_ref, cells_hbm, kern_hbm, out_ref, count, todo, place, cells_ref, kern_ref, sems
):
    slab = lax.axis_index("rad")
    rows = elements * NGLL // LANES
    bring_cells = pltpu.make_async_copy(cells_hbm, cells_ref, sems.at[0])
    bring_kern = pltpu.make_async_copy(kern_hbm, kern_ref, sems.at[1])
    bring_cells.start()
    bring_kern.start()
    out_ref[...] = jnp.full(out_ref.shape, -1000.0, jnp.float32)
    lane = lax.broadcasted_iota(jnp.int32, (3, LANES), 1)

    @pl.loop(0, n_lat)
    def _(t):
        count[t] = 0

    def listed(e, n):
        t = tiles_ref[e]
        rank = count[t]
        count[t] = rank + 1
        slot = lax.div(rank, n_rad)
        todo[n] = e
        place[n] = t * share + slot
        return n + jnp.where(rank - slot * n_rad == slab, 1, 0)

    n = lax.fori_loop(0, elements, listed, 0, unroll=4)
    for more in range(PACK_UNROLL):
        todo[n + more] = 0
        place[n + more] = n_lat * share
    bring_cells.wait()
    bring_kern.wait()

    def packed(step, _):
        for u in range(PACK_UNROLL):
            e = todo[step * PACK_UNROLL + u]
            at = place[step * PACK_UNROLL + u]
            start = e * NGLL
            row = lax.shift_right_logical(start, 7)
            off = start & (LANES - 1)
            after = jnp.minimum(row + 1, rows - 1)
            a = kern_ref[:, pl.ds(pl.multiple_of(row * LANES, LANES), LANES)]
            b = kern_ref[:, pl.ds(pl.multiple_of(after * LANES, LANES), LANES)]
            v = pltpu.roll(jnp.where(lane >= off, a, b), (LANES - off) & (LANES - 1), 1)
            v = jnp.where(lane == NGLL, cells_ref[0, e].astype(jnp.float32), v)
            v = jnp.where(lane == NGLL + 1, cells_ref[1, e].astype(jnp.float32), v)
            v = jnp.where(lane == NGLL + 2, cells_ref[2, e].astype(jnp.float32), v)
            t = lax.div(at, share)
            slot = at - t * share
            for c in range(3):
                out_ref[t, pl.ds(c * share + slot, 1), :] = v[c : c + 1]
        return 0

    lax.fori_loop(0, lax.div(n + PACK_UNROLL - 1, PACK_UNROLL), packed, 0)


def exchange_kernel(n_lat, n_rad, send_ref, recv_ref, own_sem, send_sem, recv_sem, fwd_sem, got_sem):
    tile, slab = lax.axis_index("lat"), lax.axis_index("rad")
    barrier = pltpu.get_barrier_semaphore()

    @pl.loop(1, n_lat)
    def _(k):
        pl.semaphore_signal(barrier, inc=1, device_id=(lax.rem(tile + k, n_lat), slab), device_id_type=MESH)

    pair = slab + 1 - 2 * lax.rem(slab, 2)
    other = slab + 2 - 4 * lax.div(slab, 2)
    for peer in (pair, other):
        pl.semaphore_signal(barrier, inc=1, device_id=(tile, peer), device_id_type=MESH)
    pl.semaphore_wait(barrier, n_lat - 1 + 2)

    def across(k):
        to = lax.rem(tile + k, n_lat)
        return pltpu.make_async_remote_copy(
            src_ref=send_ref.at[to],
            dst_ref=recv_ref.at[slab, tile],
            send_sem=send_sem.at[k],
            recv_sem=recv_sem.at[k],
            device_id=(to, slab),
            device_id_type=MESH,
        )

    def share(k, of, to, way):
        block = recv_ref.at[of, lax.rem(tile + n_lat - k, n_lat)]
        return pltpu.make_async_remote_copy(
            src_ref=block,
            dst_ref=block,
            send_sem=fwd_sem.at[way, k],
            recv_sem=got_sem.at[way, k],
            device_id=(tile, to),
            device_id_type=MESH,
        )

    def forward(k):
        share(k, slab, other, 0).start()
        share(k, slab, pair, 1).start()

    def relay(k):
        share(k, other, other, 0).wait_recv()
        share(k, other, pair, 2).start()

    @pl.loop(1, n_lat)
    def _(k):
        across(k).start()

    own = pltpu.make_async_copy(send_ref.at[tile], recv_ref.at[slab, tile], own_sem)
    own.start()
    own.wait()
    forward(0)

    @pl.loop(1, n_lat)
    def _(k):
        across(k).wait_recv()
        forward(k)

    @pl.loop(0, n_lat)
    def _(k):
        relay(k)

    @pl.loop(0, n_lat)
    def _(k):
        share(k, pair, pair, 1).wait_recv()
        share(k, other + pair - slab, pair, 2).wait_recv()

    @pl.loop(1, n_lat)
    def _(k):
        across(k).wait_send()

    @pl.loop(0, n_lat)
    def _(k):
        share(k, slab, other, 0).wait_send()
        share(k, slab, pair, 1).wait_send()
        share(k, other, pair, 2).wait_send()


def sum_kernel(blocks, share, meta_ref, recv_ref, acc, todo):
    slab = lax.axis_index("rad")
    slots = blocks * share
    acc[...] = jnp.zeros(acc.shape, jnp.float32)
    lane = lax.broadcasted_iota(jnp.int32, (8, LANES), 1)
    sub = lax.broadcasted_iota(jnp.int32, (8, LANES), 0)
    ramp = 25 * sub + lane
    low = slab * CZ - 2 * HZ

    def listed(s, n):
        zb = meta_ref[slots + s] - low
        todo[n] = s
        return n + jnp.where((zb >= 0) & (zb < CZ + 3 * HZ), 1, 0)

    n = lax.fori_loop(0, slots, listed, 0, unroll=8)
    for more in range(SUM_UNROLL):
        todo[n + more] = 0

    def place(at, values, index, mask):
        for j in range(5):
            picked = jnp.where(mask, index + 5 * j, NGLL)
            for c in range(3):
                piece = jnp.take_along_axis(values[c], picked, axis=1, mode="promise_in_bounds")
                acc[pl.ds(pl.multiple_of(at + (3 * j + c) * 8, 8), 8), :] += piece

    def summed(step, _):
        later = []
        for u in range(SUM_UNROLL):
            s = todo[step * SUM_UNROLL + u]
            good = step * SUM_UNROLL + u < n
            x0 = jnp.clip(meta_ref[s], 0, CX - 5)
            zb = jnp.clip(meta_ref[slots + s] - low, 0, CZ + 3 * HZ - 1)
            y0 = jnp.clip(meta_ref[2 * slots + s], 0, NY - 5)
            block = lax.div(s, share)
            slot = s - block * share
            values = []
            for c in range(3):
                row = jnp.broadcast_to(recv_ref[block, pl.ds(c * share + slot, 1), :], (8, LANES))
                values.append(jnp.where(lane < NGLL, row, 0.0))
            half = lax.shift_right_logical(y0, 7)
            yl = y0 & (LANES - 1)
            index = ramp - (25 * x0 + yl)
            rows = (sub >= x0) & (sub < jnp.where(good, x0 + 5, 0))
            at = (half * ZP + zb) * 24
            place(at, values, index, rows & (lane >= yl) & (lane < yl + 5))
            later.append((at, values, index, rows, yl))
        widest = functools.reduce(jnp.maximum, [entry[4] for entry in later])

        @pl.when(widest > LANES - 5)
        def _():
            for at, values, index, rows, yl in later:
                over = rows & (lane < yl + 5 - LANES)

                @pl.when(yl > LANES - 5)
                def _():
                    place(at + ZP * 24, values, index + LANES, over)

        return 0

    lax.fori_loop(0, lax.div(n + SUM_UNROLL - 1, SUM_UNROLL), summed, 0)


def finish_kernel(n_lat, taps_ref, wx_ref, acc, wy_ref, out_ref, planes, rows_ref, send_sem, recv_sem):
    tile, slab = lax.axis_index("lat"), lax.axis_index("rad")
    barrier = pltpu.get_barrier_semaphore()
    has_prev, has_next = tile > 0, tile < n_lat - 1
    halo = HW * CZ

    @pl.when(has_prev)
    def _():
        pl.semaphore_signal(barrier, inc=1, device_id=(tile - 1, slab), device_id_type=MESH)

    @pl.when(has_next)
    def _():
        pl.semaphore_signal(barrier, inc=1, device_id=(tile + 1, slab), device_id_type=MESH)

    def at(c, row, count):
        return rows_ref.at[:, pl.ds(c * PADX * CZ + row, count), :]

    def to_next(c):
        return pltpu.make_async_remote_copy(
            src_ref=at(c, CX * CZ, halo),
            dst_ref=at(c, 0, halo),
            send_sem=send_sem.at[0, c],
            recv_sem=recv_sem.at[0, c],
            device_id=(tile + 1, slab),
            device_id_type=MESH,
        )

    def to_prev(c):
        return pltpu.make_async_remote_copy(
            src_ref=at(c, halo, halo),
            dst_ref=at(c, halo + CX * CZ, halo),
            send_sem=send_sem.at[1, c],
            recv_sem=recv_sem.at[1, c],
            device_id=(tile - 1, slab),
            device_id_type=MESH,
        )

    for c in range(3):

        @pl.loop(0, CZ, unroll=4)
        def _(z):
            for half in range(NY // LANES):
                total = jnp.zeros((CX, LANES), jnp.float32)
                for d in range(TAPS):
                    weight = taps_ref[(slab * CZ + z) * TAPS + d]
                    row = pl.multiple_of(((half * ZP + z + HZ + d) * 3 + c) * CX, 8)
                    total = total + weight * acc[pl.ds(row, CX), :]
                cols = slice(half * LANES, (half + 1) * LANES)
                planes[pl.ds(pl.multiple_of(z * CX, 8), CX), cols] = total

        product = jnp.dot(planes[...], wy_ref[...], precision=lax.Precision.HIGHEST)
        for z in range(CZ):
            for half in range(NY // LANES):
                piece = product[z * CX : (z + 1) * CX, half * LANES : (half + 1) * LANES]
                rows_ref[half, pl.ds(c * PADX * CZ + halo + z, CX, stride=CZ), :] = piece

        if c == 0:
            beside = jnp.minimum(tile, 1) + jnp.minimum(n_lat - 1 - tile, 1)
            pl.semaphore_wait(barrier, beside)

        @pl.when(has_next)
        def _():
            to_next(c).start()

        @pl.when(has_prev)
        def _():
            to_prev(c).start()

        zeros = jnp.zeros((NY // LANES, halo, LANES), jnp.float32)

        @pl.when(tile == 0)
        def _():
            rows_ref[:, c * PADX * CZ : c * PADX * CZ + halo, :] = zeros

        @pl.when(tile == n_lat - 1)
        def _():
            rows_ref[:, c * PADX * CZ + halo + CX * CZ : (c + 1) * PADX * CZ, :] = zeros

    for c in range(3):

        @pl.when(has_prev)
        def _():
            to_next(c).wait_recv()

        @pl.when(has_next)
        def _():
            to_prev(c).wait_recv()

        @pl.loop(0, CX)
        def _(x):
            for half in range(NY // LANES):
                total = jnp.zeros((CZ, LANES), jnp.float32)
                for d in range(2 * HW + 1):
                    row = pl.multiple_of(c * PADX * CZ + (x + d) * CZ, 8)
                    total = total + wx_ref[x * (2 * HW + 1) + d] * rows_ref[half, pl.ds(row, CZ), :]
                out_ref[c, x, :, half * LANES : (half + 1) * LANES] = total

    for c in range(3):

        @pl.when(has_next)
        def _():
            to_next(c).wait_send()

        @pl.when(has_prev)
        def _():
            to_prev(c).wait_send()


def x_weights(width_class, n_lat):
    rows = lax.axis_index("lat") * CX + jnp.arange(CX)
    sigma = 1.0 + 0.75 * width_class[0].astype(jnp.float32)
    offsets = jnp.arange(-HW, HW + 1)
    target = rows[:, None] + offsets[None, :]
    valid = (target >= 0) & (target < CX * n_lat)
    gauss = jnp.exp(-(offsets[None, :].astype(jnp.float32) ** 2) / (2.0 * sigma**2))
    gauss = jnp.where(valid, gauss, 0.0)
    return gauss / jnp.sum(gauss, axis=1, keepdims=True)


def on_device(n_lat, n_rad, kernels, cells, tiles, width_class):
    elements = tiles.shape[0]
    cap = max(2, 2 * elements // n_lat)
    share = -(-cap // n_rad)
    blocks = n_rad * n_lat
    slots = blocks * share
    params = pltpu.CompilerParams(vmem_limit_bytes=VMEM_LIMIT)
    smem = pl.BlockSpec(memory_space=pltpu.SMEM)
    vmem = pl.BlockSpec(memory_space=pltpu.VMEM)
    hbm = pl.BlockSpec(memory_space=pl.ANY)
    send = pl.pallas_call(
        functools.partial(pack_kernel, n_lat, n_rad, share, elements),
        out_shape=jax.ShapeDtypeStruct((n_lat + 1, 3 * share, LANES), jnp.float32),
        in_specs=[smem, hbm, hbm],
        out_specs=vmem,
        scratch_shapes=[
            pltpu.SMEM((n_lat,), jnp.int32),
            pltpu.SMEM((elements + PACK_UNROLL,), jnp.int32),
            pltpu.SMEM((elements + PACK_UNROLL,), jnp.int32),
            pltpu.SMEM(cells.shape, jnp.int32),
            pltpu.VMEM(kernels.shape, jnp.float32),
            pltpu.SemaphoreType.DMA((2,)),
        ],
        compiler_params=params,
    )(tiles.reshape(-1), cells, kernels)
    recv = pl.pallas_call(
        functools.partial(exchange_kernel, n_lat, n_rad),
        out_shape=jax.ShapeDtypeStruct((n_rad, n_lat, 3 * share, LANES), jnp.float32),
        in_specs=[vmem],
        out_specs=vmem,
        scratch_shapes=[
            pltpu.SemaphoreType.DMA,
            pltpu.SemaphoreType.DMA((n_lat,)),
            pltpu.SemaphoreType.DMA((n_lat,)),
            pltpu.SemaphoreType.DMA((3, n_lat)),
            pltpu.SemaphoreType.DMA((3, n_lat)),
        ],
        compiler_params=pltpu.CompilerParams(
            vmem_limit_bytes=VMEM_LIMIT, collective_id=0, has_side_effects=True
        ),
    )(send)
    recv = recv.reshape(blocks, 3 * share, LANES)
    meta = recv[:, :share, NGLL:].transpose(2, 0, 1).reshape(-1).astype(jnp.int32)
    grid_rows = NY // LANES * ZP * 24
    summed = pl.pallas_call(
        functools.partial(sum_kernel, blocks, share),
        out_shape=jax.ShapeDtypeStruct((grid_rows, LANES), jnp.float32),
        in_specs=[smem, vmem],
        out_specs=vmem,
        scratch_shapes=[pltpu.SMEM((slots + SUM_UNROLL,), jnp.int32)],
        compiler_params=params,
    )(meta, recv)
    return pl.pallas_call(
        functools.partial(finish_kernel, n_lat),
        out_shape=jax.ShapeDtypeStruct((3, CX, CZ, NY), jnp.float32),
        in_specs=[smem, smem, vmem, vmem],
        out_specs=vmem,
        scratch_shapes=[
            pltpu.VMEM((CZ * CX, NY), jnp.float32),
            pltpu.VMEM((NY // LANES, 3 * PADX * CZ, LANES), jnp.float32),
            pltpu.SemaphoreType.DMA((2, 3)),
            pltpu.SemaphoreType.DMA((2, 3)),
        ],
        compiler_params=pltpu.CompilerParams(
            vmem_limit_bytes=VMEM_LIMIT, collective_id=1, has_side_effects=True
        ),
    )(
        jnp.asarray(z_taps(n_rad).reshape(-1)),
        x_weights(width_class, n_lat).reshape(-1),
        summed,
        jnp.asarray(band_matrix(NY, 2.5, HY).T.astype(np.float32)),
    )

ROW_TILES = 3
Z_BINS = 11
Y_TILES = 17
WINDOW = CZ + 2 * HZ
DEPTH = 2 * CX * WINDOW
SUM_WAYS = 24
SUM_GROUP = 4
CUTS = 3


def gather_kernel(n_lat, n_rad, block, width_ref, tiles_hbm, cells_hbm, kern_hbm, data_ref, words_ref, whi_ref, wlo_ref,
                  kern_ref, tiles_ref, cells_ref, index_ref, compact_ref, in_sem, is_sem, ir_sem, zs, zr, xs, xr, ys, yr, bs, br):
    lat, rad = lax.axis_index("lat"), lax.axis_index("rad")
    levels = n_lat // 2
    z, x = lax.div(lat, 2), lax.rem(lat, 2)
    y, k = lax.div(rad, 2), lax.rem(rad, 2)
    across_x, across_y, across_k = lat + 1 - 2 * x, rad + 2 - 4 * y, rad + 1 - 2 * k
    barrier = pltpu.get_barrier_semaphore()

    @pl.loop(1, n_lat)
    def _(step):
        pl.semaphore_signal(barrier, inc=1, device_id=(lax.rem(lat + step, n_lat), rad), device_id_type=MESH)

    for peer in (across_y, across_k):
        pl.semaphore_signal(barrier, inc=1, device_id=(lat, peer), device_id_type=MESH)
    points = kern_hbm.shape[1]
    split = block // 6 * LANES
    brought = [
        pltpu.make_async_copy(kern_hbm.at[:, :split], kern_ref.at[:, :split], in_sem.at[0]),
        pltpu.make_async_copy(kern_hbm.at[:, split:], kern_ref.at[:, split:points], in_sem.at[3]),
        pltpu.make_async_copy(tiles_hbm, tiles_ref, in_sem.at[1]),
        pltpu.make_async_copy(cells_hbm, cells_ref, in_sem.at[2]),
    ]
    for copy in brought:
        copy.start()
    if kern_ref.shape[1] > points:
        kern_ref[:, points:] = jnp.zeros((3, kern_ref.shape[1] - points), jnp.float32)

    half = block // 2
    part = half // 2
    mine = k * half
    piece = part // CUTS
    starts = [mine + (y if j < CUTS else 1 - y) * part + j % CUTS * piece for j in range(2 * CUTS)]

    def move(row, count, send_sem, recv_sem, device):
        rows = data_ref.at[pl.ds(pl.multiple_of(row, 8), count)]
        return pltpu.make_async_remote_copy(
            src_ref=rows, dst_ref=rows, send_sem=send_sem, recv_sem=recv_sem,
            device_id=device, device_id_type=MESH)

    def z_move(i, j, up):
        way = 0 if up else 1
        return move(i * block + starts[j], piece, zs.at[i, way], zr.at[i, j], (lat + (2 if up else -2), rad))

    def x_move(i, j):
        return move(i * block + starts[j], piece, xs.at[j // CUTS], xr.at[i, j], (across_x, rad))

    def y_move(i, j):
        return move(i * block + starts[j], piece, ys, yr.at[i, j % CUTS], (lat, across_y))

    def k_move(i):
        return move(i * block + mine, half, bs, br, (lat, across_k))

    def sized(rows, send_sem, recv_sem, device):
        return move(0, rows, send_sem, recv_sem, device)

    def index_move(step):
        to = lax.rem(lat + step, n_lat)
        return pltpu.make_async_remote_copy(
            src_ref=index_ref.at[lat], dst_ref=index_ref.at[lat], send_sem=is_sem, recv_sem=ir_sem,
            device_id=(to, rad), device_id_type=MESH)

    def index_all():
        others = index_ref.at[pl.ds(0, n_lat - 1)]
        return pltpu.make_async_remote_copy(
            src_ref=others, dst_ref=others, send_sem=is_sem, recv_sem=ir_sem,
            device_id=(across_x, rad), device_id_type=MESH)

    can_up, can_down = z < levels - 1, z > 0
    at_end = (z == 0) | (z == levels - 1)
    long_up, long_down = z < levels - 2, z > 1
    base = pl.multiple_of(lat * block, 8)
    sets = block // 24

    def pack(first, count):
        @pl.loop(0, count, unroll=4)
        def _(g):
            at = (first + g) * 8 * LANES
            rows = [kern_ref[:, pl.ds(pl.multiple_of(at + u * LANES, LANES), LANES)] for u in range(8)]
            data_ref[pl.ds(base + pl.multiple_of((first + g) * 24, 8), 24), :] = jnp.concatenate(rows, axis=0)

    def pack_part(j):
        pack(k * (sets // 2) + (y if j == 0 else 1 - y) * (sets // 4), sets // 4)

    @pl.when(k == 0)
    def _():
        brought[0].wait()

    @pl.when(k == 1)
    def _():
        brought[1].wait()

    pack_part(0)
    pl.semaphore_wait(barrier, n_lat - 1 + 2)

    def own_z(j, up):
        able = (long_up if up else long_down) if j >= CUTS else (can_up if up else can_down)

        @pl.when(able)
        def _():
            z_move(lat, j, up).start()

    for j in range(CUTS):
        own_z(j, True)
        own_z(j, False)
        x_move(lat, j).start()
    pack_part(1)
    for j in range(CUTS, 2 * CUTS):
        for up in (True, False):
            if j == CUTS:
                own_z(j, up)
            else:
                pl.when(z == (0 if up else levels - 1))(functools.partial(own_z, j, up))

    brought[2].wait()
    brought[3].wait()
    index_ref[lat] = jnp.concatenate([tiles_ref[...], cells_ref[...], jnp.zeros((4, tiles_ref.shape[1]), jnp.int32)], axis=0)

    @pl.loop(1, n_lat)
    def _(step):
        index_move(step).start()

    @pl.when(k == 1)
    def _():
        brought[0].wait()

    @pl.when(k == 0)
    def _():
        brought[1].wait()

    pack((1 - k) * (sets // 2), sets // 2)

    def weights():
        col = lax.broadcasted_iota(jnp.int32, (8, DEPTH), 1)
        beside = col >= CX * WINDOW
        rest = jnp.where(beside, col - CX * WINDOW, col)
        xl = lax.shift_right_logical(rest * 1639, 16)
        zc = rest - WINDOW * xl
        place = jnp.where(beside, jnp.where(xl < HW, xl + CX, xl - CX), xl)
        sub = lax.broadcasted_iota(jnp.int32, (8, DEPTH), 0)
        sigma = 1.0 + 0.75 * jnp.full((8, DEPTH), width_ref[0], jnp.int32).astype(jnp.float32)
        twice = 2.0 * sigma * sigma

        def bell(d, reach, scale):
            square = (d * d).astype(jnp.float32)
            return jnp.where(jnp.abs(d) <= reach, jnp.exp(-square / scale), 0.0)

        norm = jnp.zeros((8, DEPTH), jnp.float32)
        for d in range(-HW, HW + 1):
            at = lat * CX + sub + d
            norm += jnp.where((at >= 0) & (at < CX * n_lat), jnp.exp(-float(d * d) / twice), 0.0)
        wx = bell(place - sub, HW, twice) / norm
        for zv in range(CZ // 8):
            norm = jnp.zeros((8, DEPTH), jnp.float32)
            zz = sub + 8 * zv
            for d in range(-HZ, HZ + 1):
                at = rad * CZ + zz + d
                norm += jnp.where((at >= 0) & (at < CZ * n_rad), float(np.exp(-d * d / 4.5)), 0.0)
            kern_w[zv * 8 : zv * 8 + 8, :] = bell(zc - HZ - zz, HZ, 4.5) / norm
        for xx in range(CX):
            both = kern_w[...] * wx[xx : xx + 1, :]
            high = both.astype(jnp.bfloat16)
            whi_ref[xx * CZ : xx * CZ + CZ, :] = high
            wlo_ref[xx * CZ : xx * CZ + CZ, :] = (both - high.astype(jnp.float32)).astype(jnp.bfloat16)

    kern_w = compact_ref.at[pl.ds(0, CZ)]
    weights()

    def lists():
        index_all().wait_recv()
        elements = index_ref.shape[2]
        shape = (n_lat, elements)
        rel = index_ref[:, 0, :] - lat
        x0 = index_ref[:, 1, :]
        zq = index_ref[:, 2, :] - rad * CZ + HZ + 8
        y0 = index_ref[:, 3, :]
        keep = (rel >= -1) & (rel <= 1) & (zq >= 4) & (zq < WINDOW + 8)
        before = lax.broadcasted_iota(jnp.int32, (elements, elements), 0) < lax.broadcasted_iota(jnp.int32, (elements, elements), 1)
        flags = jnp.where(keep, 1.0, 0.0)
        rank = jnp.dot(flags.astype(jnp.bfloat16), jnp.where(before, 1.0, 0.0).astype(jnp.bfloat16), preferred_element_type=jnp.float32)
        total = jnp.sum(flags, axis=1, keepdims=True).astype(jnp.int32)
        rank = jnp.where(keep, rank, -1.0)
        low = jnp.maximum(x0, jnp.where(rel < 0, HW, 0))
        high = jnp.minimum(x0 + 4, jnp.where(rel > 0, HW - 1, CX - 1))
        code = low + 8 * (high - low + 1)
        lane = lax.broadcasted_iota(jnp.int32, shape, 1)
        fields = [lane, zq, y0, x0, code, jnp.where(rel == 0, 0, 1)]
        fields = [jnp.where(keep, f, 0).astype(jnp.float32) for f in fields]
        slot = lax.broadcasted_iota(jnp.int32, (elements, elements), 0).astype(jnp.float32)
        zero = jnp.zeros((1, elements), jnp.float32)
        for i in range(n_lat):
            stack = jnp.concatenate([f[i : i + 1] for f in fields] + [zero, zero], axis=0).astype(jnp.bfloat16)
            pick = jnp.where(rank[i : i + 1] == slot, 1.0, 0.0).astype(jnp.bfloat16)
            compact_ref[8 * i : 8 * i + 8, :elements] = lax.dot_general(
                stack, pick, (((1,), (1,)), ((), ())), preferred_element_type=jnp.float32)

        def field(f):
            return jnp.concatenate([compact_ref[8 * i + f : 8 * i + f + 1, :elements] for i in range(n_lat)], axis=0).astype(jnp.int32)

        e, zq, y0, x0, code, beside = [field(f) for f in range(6)]
        start = e * NGLL
        row = lax.broadcasted_iota(jnp.int32, shape, 0) * block + 3 * lax.shift_right_logical(start, 7)
        off = start & (LANES - 1)
        words = row | (off << 16) | (((off - 25 * x0) & (LANES - 1)) << 23)
        words_ref[0] = jnp.where(lane == elements - 1, total, words)
        zb = jnp.maximum(lax.shift_right_logical(zq, 2) - 1, 0)
        at = ((beside * Z_BINS + zb) * Y_TILES + lax.shift_right_logical(y0, 4)) * 8
        words_ref[1] = at | ((zq & 7) << 12) | ((y0 & 127) << 16) | (code << 24)

    def when_there(d, up, body):
        zi = z - d if up else z + d

        @pl.when((zi >= 0) & (zi < levels))
        def _():
            body(2 * zi)

    def later_own():
        for j in range(CUTS + 1, 2 * CUTS):
            for up in (True, False):
                pl.when(z != (0 if up else levels - 1))(functools.partial(own_z, j, up))

    def extra(d, up, farthest):
        end = (z == d) if up else (z == levels - 1 - d)

        @pl.when(end if farthest else jnp.logical_not(end))
        def _():
            for j in range(CUTS, 2 * CUTS):
                line(d, up, j)

    def line(d, up, j):
        more = can_up if up else can_down

        def body(i):
            i = i + x
            if j < CUTS:
                z_move(i, j, up).wait_recv()

                @pl.when(more)
                def _():
                    z_move(i, j, up).start()

                x_move(i, j).start()
                if d == 1:
                    @pl.when(jnp.logical_not(more))
                    def _():
                        y_move(i, j).start()
            elif d > 1:
                z_move(i, j, up).wait_recv()

                @pl.when(more)
                def _():
                    z_move(i, j, up).start()

                if d == levels - 1:
                    x_move(i, j).start()
                if j == 2 * CUTS - 1:
                    k_move(i).start()
            else:
                @pl.when(more)
                def _():
                    z_move(i, j, up).wait_recv()
                    z_move(i, j, up).start()
                    if j == 2 * CUTS - 1:
                        k_move(i).start()

        when_there(d, up, body)

    def cross(d, up, j):
        def body(i):
            i = i + 1 - x
            if j < CUTS:
                x_move(i, j).wait_recv()
                if d < levels - 1:
                    y_move(i, j).start()
            elif d == levels - 1:
                x_move(i, j).wait_recv()
                if j == 2 * CUTS - 1:
                    k_move(i).start()

        when_there(d, up, body)

    def y_done(d, up, own_column):
        def body(i):
            i = i + (x if own_column else 1 - x)

            def finish():
                for j in range(CUTS):
                    y_move(i, CUTS + j).wait_recv()
                k_move(i).start()

            if own_column:
                pl.when(jnp.logical_not(can_up if up else can_down))(finish)
            else:
                finish()

        when_there(d, up, body)

    ways = lambda d: (True, False) if d else (True,)
    for d in range(1, levels + 1):
        for j in range(CUTS):
            if d < levels:
                for up in ways(d):
                    line(d, up, j)
            for up in ways(d - 1):
                cross(d - 1, up, j)
            if d == 3 and j == 0:
                for up in ways(1):
                    extra(1, up, False)
        if d < levels:
            for up in ways(d):
                extra(d, up, True)
        if d == 1:
            later_own()
        if d == 3:
            for up in ways(2):
                extra(2, up, False)
            lists()
        if d == levels:
            for j in range(CUTS, 2 * CUTS):
                for up in ways(d - 1):
                    cross(d - 1, up, j)
        if d == 2:
            for up in ways(1):
                y_done(1, up, True)
        if 2 <= d <= levels:
            for up in ways(d - 2):
                y_done(d - 2, up, False)

    index_all().wait_send()
    sized(levels * part, xs.at[0], xr.at[0, 0], (across_x, rad)).wait_send()

    @pl.when(at_end)
    def _():
        sized(part, xs.at[1], xr.at[0, 1], (across_x, rad)).wait_send()

    for up in (True, False):
        way = 0 if up else 1
        peer = (lat + (2 if up else -2), rad)

        @pl.when(can_up if up else can_down)
        def _():
            for zi in range(levels):
                passed = (zi <= z) if up else (zi >= z)
                both = zi < levels - 2 if up else zi > 1

                @pl.when(passed)
                def _():
                    sized(2 * part if both else part, zs.at[2 * zi + x, way], zr.at[0, 0], peer).wait_send()

    sized(levels * part, ys, yr.at[0, 0], (lat, across_y)).wait_send()
    everything = sized((n_lat - 1) * half, bs, br, (lat, across_k))
    everything.wait_send()
    everything.wait_recv()


def grid_kernel(n_lat, words_ref, data_ref, whi_ref, wlo_ref, ghi_hbm, glo_hbm, out_hbm, acc0, acc1, acc2, fields, result, words, todo, ghi_ref, glo_ref, sem, smooth_sem, out_sem):
    accs = (acc0, acc1, acc2)
    smooth = [pltpu.make_async_copy(ghi_hbm, ghi_ref, smooth_sem.at[0]), pltpu.make_async_copy(glo_hbm, glo_ref, smooth_sem.at[1])]
    bring = pltpu.make_async_copy(words_ref, words.at[:, pl.ds(0, n_lat), :], sem)
    bring.start()
    for copy in smooth:
        copy.start()
    rows = acc0.shape[0]

    @pl.loop(0, rows // 8, unroll=11)
    def _(r):
        for acc in accs:
            acc[pl.ds(pl.multiple_of(r * 8, 8), 8), :] = jnp.zeros((8, LANES), jnp.float32)

    bring.wait()
    lane = lax.broadcasted_iota(jnp.int32, (8, LANES), 1)
    sub = lax.broadcasted_iota(jnp.int32, (8, LANES), 0)
    across = lane & 15
    along = lax.shift_right_logical(lane, 4)
    elements = words.shape[2]

    for u in range(SUM_GROUP):
        words[0, n_lat, u] = 0
        words[1, n_lat, u] = 0

    def listed(i, n):
        many = lax.div(words[0, i, elements - 1] + SUM_GROUP - 1, SUM_GROUP)

        @pl.loop(0, lax.div(many + 7, 8))
        def _(t):
            for u in range(8):
                todo[n + t * 8 + u] = (i << 16) + (t * 8 + u) * SUM_GROUP

        return n + many

    groups = lax.fori_loop(0, n_lat, listed, 0)
    batch = SUM_WAYS // SUM_GROUP
    for u in range(batch):
        todo[groups + u] = n_lat << 16

    @pl.loop(0, lax.div(groups + batch - 1, batch))
    def _(step):
        for g in range(batch):
            first_slot = todo[step * batch + g]
            i = lax.shift_right_logical(first_slot, 16)
            p0 = first_slot & 0xFFFF
            for u in range(SUM_GROUP):
                w0, w1 = words[0, i, p0 + u], words[1, i, p0 + u]
                row = w0 & 0xFFFF
                at = pl.multiple_of(w1 & 0xFFF, 8)
                v0, v1 = jnp.full((8, LANES), w0, jnp.int32), jnp.full((8, LANES), w1, jnp.int32)
                off = lax.shift_right_logical(v0, 16) & 127
                shift = lax.shift_right_logical(v0, 23)
                zq = lax.shift_right_logical(v1, 12)
                y0 = lax.shift_right_logical(v1, 16)
                low = lax.shift_right_logical(v1, 24)
                wide = lax.shift_right_logical(v1, 27)
                tz = (sub - zq) & 7
                turned = (lane - y0) & (LANES - 1)
                ty = turned & 15
                xl = lax.shift_right_logical(turned, 4)
                tx = (xl - low) & 7
                index = (25 * xl + shift + 5 * tz + ty) & (LANES - 1)
                good = (jnp.maximum(tz, ty) < 5) & (tx < wide)
                first = across >= (y0 & 15)
                here, there = good & first, good & jnp.logical_not(first)
                head = lane >= off
                for c in range(3):
                    a = data_ref[pl.ds(row + c, 1), :]
                    b = data_ref[pl.ds(row + 3 + c, 1), :]
                    v = jnp.broadcast_to(jnp.where(head[0:1], a, b), (8, LANES))
                    v = jnp.take_along_axis(v, index, axis=1, mode="promise_in_bounds")
                    accs[c][pl.ds(at, 8), :] += jnp.where(here, v, 0.0)
                    accs[c][pl.ds(at + 8, 8), :] += jnp.where(there, v, 0.0)

    low_half = sub < 4
    for copy in smooth:
        copy.wait()
    for c in range(3):
        acc, field = accs[c], fields.at[c]

        @pl.loop(0, 2, unroll=2)
        def _(g):
            @pl.loop(0, WINDOW // 8, unroll=WINDOW // 8)
            def _(h):
                for side in range(2):
                    v = []
                    for t in range(8):
                        def bins(n):
                            r = ((g * Z_BINS + 2 * h + n) * Y_TILES + side * 8 + t) * 8
                            return acc[pl.ds(pl.multiple_of(r, 8), 8), :]

                        v.append(bins(1) + jnp.where(low_half, bins(0), bins(2)))
                    for bit in (1, 2, 4):
                        v = [jnp.where((along & bit) == 0, v[t], v[(t + bit) % 8]) for t in range(8)]
                    v = [v[0]] + [pltpu.roll(v[8 - xl], LANES - 16 * xl, 1) for xl in range(1, 8)]
                    for xl in range(8):
                        r = pl.multiple_of(g * (CX * WINDOW) + xl * WINDOW + h * 8, 8)
                        field[pl.ds(r, 8), side * LANES : (side + 1) * LANES] = v[xl]

        def split(a):
            high = a.astype(jnp.bfloat16)
            return high, (a - high.astype(jnp.float32)).astype(jnp.bfloat16)

        def dot(a, b):
            return jnp.dot(a, b, preferred_element_type=jnp.float32)

        high, low = split(field[...])
        whi = whi_ref[...]
        mixed = dot(whi, high) + dot(wlo_ref[...], high) + dot(whi, low)
        high, low = split(mixed)
        ghi = ghi_ref[...]
        done = dot(high, ghi) + dot(low, ghi) + dot(high, glo_ref[...])
        result[c] = done.reshape(CX, CZ, NY)
        pltpu.make_async_copy(result.at[c], out_hbm.at[c], out_sem.at[c]).start()
    for c in range(3):
        pltpu.make_async_copy(result.at[c], out_hbm.at[c], out_sem.at[c]).wait()


def on_device_whole(n_lat, n_rad, kernels, cells, tiles, width_class):
    elements = tiles.shape[0]
    block = -(-kernels.shape[1] // LANES * 3 // 96) * 96
    smem = pl.BlockSpec(memory_space=pltpu.SMEM)
    vmem = pl.BlockSpec(memory_space=pltpu.VMEM)
    hbm = pl.BlockSpec(memory_space=pltpu.HBM)
    dma = pltpu.SemaphoreType.DMA
    stay = functools.partial(pltpu.with_memory_space_constraint, memory_space=pltpu.HBM)
    data, words, whi, wlo = pl.pallas_call(
        functools.partial(gather_kernel, n_lat, n_rad, block),
        out_shape=[
            jax.ShapeDtypeStruct((n_lat * block + 8, LANES), jnp.float32),
            jax.ShapeDtypeStruct((2, n_lat, elements), jnp.int32),
            jax.ShapeDtypeStruct((CX * CZ, DEPTH), jnp.bfloat16),
            jax.ShapeDtypeStruct((CX * CZ, DEPTH), jnp.bfloat16),
        ],
        in_specs=[smem, hbm, hbm, hbm],
        out_specs=[vmem] * 4,
        scratch_shapes=[
            pltpu.VMEM((3, block // 3 * LANES), jnp.float32),
            pltpu.VMEM((1, elements), jnp.int32),
            pltpu.VMEM(cells.shape, jnp.int32),
            pltpu.VMEM((n_lat, 8, elements), jnp.int32),
            pltpu.VMEM((8 * n_lat, DEPTH), jnp.float32),
            dma((4,)), dma, dma,
            dma((n_lat, 2)), dma((n_lat, 2 * CUTS)), dma((2,)), dma((n_lat, 2 * CUTS)),
            dma, dma((n_lat, CUTS)), dma, dma,
        ],
        compiler_params=pltpu.CompilerParams(
            vmem_limit_bytes=VMEM_LIMIT, collective_id=0, has_side_effects=True
        ),
    )(width_class, *map(stay, (tiles.reshape(1, elements), cells, kernels)))
    smooth = band_matrix(NY, 2.5, HY).T.astype(np.float32)
    high = smooth.astype(jnp.bfloat16)
    low = (smooth - high.astype(np.float32)).astype(jnp.bfloat16)
    rows = 2 * Z_BINS * Y_TILES * 8
    return pl.pallas_call(
        functools.partial(grid_kernel, n_lat),
        out_shape=jax.ShapeDtypeStruct((3, CX, CZ, NY), jnp.float32),
        in_specs=[vmem] * 4 + [hbm] * 2,
        out_specs=hbm,
        scratch_shapes=[
            pltpu.VMEM((rows, LANES), jnp.float32),
            pltpu.VMEM((rows, LANES), jnp.float32),
            pltpu.VMEM((rows, LANES), jnp.float32),
            pltpu.VMEM((3, DEPTH, NY), jnp.float32),
            pltpu.VMEM((3, CX, CZ, NY), jnp.float32),
            pltpu.SMEM((2, n_lat + 1, elements), jnp.int32),
            pltpu.SMEM((n_lat * elements // SUM_GROUP + 16,), jnp.int32),
            pltpu.VMEM((NY, NY), jnp.bfloat16),
            pltpu.VMEM((NY, NY), jnp.bfloat16),
            dma, dma((2,)), dma((3,)),
        ],
        compiler_params=pltpu.CompilerParams(vmem_limit_bytes=VMEM_LIMIT),
    )(words, data, whi, wlo, stay(jnp.asarray(high)), stay(jnp.asarray(low)))


def solution(mesh):
    n_lat, n_rad = mesh.shape["lat"], mesh.shape["rad"]
    whole = n_lat == 8 and n_rad == 4
    return jax.shard_map(
        functools.partial(on_device_whole if whole else on_device, n_lat, n_rad),
        mesh=mesh,
        in_specs=(P(None, "lat"), P(None, "lat"), P("lat", None), P("lat")),
        out_specs=P(None, "lat", "rad", None),
        check_vma=False,
    )
```

```python
import functools

import jax
import jax.numpy as jnp
import numpy as np
from jax import lax
from jax.experimental import pallas as pl
from jax.experimental.pallas import tpu as pltpu
from jax.sharding import PartitionSpec as P

CX = 8
NY = 256
CZ = 32
NGLL = 125
HW = 4
HY = 8
HZ = 4
ZP = CZ + 4 * HZ
LANES = 128
TAPS = 2 * HZ + 1
PADX = CX + 2 * HW
PACK_UNROLL = 4
SUM_UNROLL = 4
VMEM_LIMIT = 48 * 2**20
MESH = pl.DeviceIdType.MESH


def band_matrix(count, sigma, half):
    place = np.arange(count)
    gap = place[None, :] - place[:, None]
    gauss = np.where(np.abs(gap) <= half, np.exp(-(gap**2) / (2.0 * sigma**2)), 0.0)
    return gauss / gauss.sum(axis=1, keepdims=True)


def z_taps(n_rad):
    full = np.pad(band_matrix(CZ * n_rad, 1.5, HZ), ((0, 0), (HZ, HZ)))
    return np.stack([full[z, z : z + TAPS] for z in range(CZ * n_rad)]).astype(np.float32)


def pack_kernel(
    n_lat, n_rad, share, elements, tiles_ref, cells_hbm, kern_hbm, out_ref, count, todo, place, cells_ref, kern_ref, sems
):
    slab = lax.axis_index("rad")
    rows = elements * NGLL // LANES
    bring_cells = pltpu.make_async_copy(cells_hbm, cells_ref, sems.at[0])
    bring_kern = pltpu.make_async_copy(kern_hbm, kern_ref, sems.at[1])
    bring_cells.start()
    bring_kern.start()
    out_ref[...] = jnp.full(out_ref.shape, -1000.0, jnp.float32)
    lane = lax.broadcasted_iota(jnp.int32, (3, LANES), 1)

    @pl.loop(0, n_lat)
    def _(t):
        count[t] = 0

    def listed(e, n):
        t = tiles_ref[e]
        rank = count[t]
        count[t] = rank + 1
        slot = lax.div(rank, n_rad)
        todo[n] = e
        place[n] = t * share + slot
        return n + jnp.where(rank - slot * n_rad == slab, 1, 0)

    n = lax.fori_loop(0, elements, listed, 0, unroll=4)
    for more in range(PACK_UNROLL):
        todo[n + more] = 0
        place[n + more] = n_lat * share
    bring_cells.wait()
    bring_kern.wait()

    def packed(step, _):
        for u in range(PACK_UNROLL):
            e = todo[step * PACK_UNROLL + u]
            at = place[step * PACK_UNROLL + u]
            start = e * NGLL
            row = lax.shift_right_logical(start, 7)
            off = start & (LANES - 1)
            after = jnp.minimum(row + 1, rows - 1)
            a = kern_ref[:, pl.ds(pl.multiple_of(row * LANES, LANES), LANES)]
            b = kern_ref[:, pl.ds(pl.multiple_of(after * LANES, LANES), LANES)]
            v = pltpu.roll(jnp.where(lane >= off, a, b), (LANES - off) & (LANES - 1), 1)
            v = jnp.where(lane == NGLL, cells_ref[0, e].astype(jnp.float32), v)
            v = jnp.where(lane == NGLL + 1, cells_ref[1, e].astype(jnp.float32), v)
            v = jnp.where(lane == NGLL + 2, cells_ref[2, e].astype(jnp.float32), v)
            t = lax.div(at, share)
            slot = at - t * share
            for c in range(3):
                out_ref[t, pl.ds(c * share + slot, 1), :] = v[c : c + 1]
        return 0

    lax.fori_loop(0, lax.div(n + PACK_UNROLL - 1, PACK_UNROLL), packed, 0)


def exchange_kernel(n_lat, n_rad, send_ref, recv_ref, own_sem, send_sem, recv_sem, fwd_sem, got_sem):
    tile, slab = lax.axis_index("lat"), lax.axis_index("rad")
    barrier = pltpu.get_barrier_semaphore()

    @pl.loop(1, n_lat)
    def _(k):
        pl.semaphore_signal(barrier, inc=1, device_id=(lax.rem(tile + k, n_lat), slab), device_id_type=MESH)

    pair = slab + 1 - 2 * lax.rem(slab, 2)
    other = slab + 2 - 4 * lax.div(slab, 2)
    for peer in (pair, other):
        pl.semaphore_signal(barrier, inc=1, device_id=(tile, peer), device_id_type=MESH)
    pl.semaphore_wait(barrier, n_lat - 1 + 2)

    def across(k):
        to = lax.rem(tile + k, n_lat)
        return pltpu.make_async_remote_copy(
            src_ref=send_ref.at[to],
            dst_ref=recv_ref.at[slab, tile],
            send_sem=send_sem.at[k],
            recv_sem=recv_sem.at[k],
            device_id=(to, slab),
            device_id_type=MESH,
        )

    def share(k, of, to, way):
        block = recv_ref.at[of, lax.rem(tile + n_lat - k, n_lat)]
        return pltpu.make_async_remote_copy(
            src_ref=block,
            dst_ref=block,
            send_sem=fwd_sem.at[way, k],
            recv_sem=got_sem.at[way, k],
            device_id=(tile, to),
            device_id_type=MESH,
        )

    def forward(k):
        share(k, slab, other, 0).start()
        share(k, slab, pair, 1).start()

    def relay(k):
        share(k, other, other, 0).wait_recv()
        share(k, other, pair, 2).start()

    @pl.loop(1, n_lat)
    def _(k):
        across(k).start()

    own = pltpu.make_async_copy(send_ref.at[tile], recv_ref.at[slab, tile], own_sem)
    own.start()
    own.wait()
    forward(0)

    @pl.loop(1, n_lat)
    def _(k):
        across(k).wait_recv()
        forward(k)

    @pl.loop(0, n_lat)
    def _(k):
        relay(k)

    @pl.loop(0, n_lat)
    def _(k):
        share(k, pair, pair, 1).wait_recv()
        share(k, other + pair - slab, pair, 2).wait_recv()

    @pl.loop(1, n_lat)
    def _(k):
        across(k).wait_send()

    @pl.loop(0, n_lat)
    def _(k):
        share(k, slab, other, 0).wait_send()
        share(k, slab, pair, 1).wait_send()
        share(k, other, pair, 2).wait_send()


def sum_kernel(blocks, share, meta_ref, recv_ref, acc, todo):
    slab = lax.axis_index("rad")
    slots = blocks * share
    acc[...] = jnp.zeros(acc.shape, jnp.float32)
    lane = lax.broadcasted_iota(jnp.int32, (8, LANES), 1)
    sub = lax.broadcasted_iota(jnp.int32, (8, LANES), 0)
    ramp = 25 * sub + lane
    low = slab * CZ - 2 * HZ

    def listed(s, n):
        zb = meta_ref[slots + s] - low
        todo[n] = s
        return n + jnp.where((zb >= 0) & (zb < CZ + 3 * HZ), 1, 0)

    n = lax.fori_loop(0, slots, listed, 0, unroll=8)
    for more in range(SUM_UNROLL):
        todo[n + more] = 0

    def place(at, values, index, mask):
        for j in range(5):
            picked = jnp.where(mask, index + 5 * j, NGLL)
            for c in range(3):
                piece = jnp.take_along_axis(values[c], picked, axis=1, mode="promise_in_bounds")
                acc[pl.ds(pl.multiple_of(at + (3 * j + c) * 8, 8), 8), :] += piece

    def summed(step, _):
        later = []
        for u in range(SUM_UNROLL):
            s = todo[step * SUM_UNROLL + u]
            good = step * SUM_UNROLL + u < n
            x0 = jnp.clip(meta_ref[s], 0, CX - 5)
            zb = jnp.clip(meta_ref[slots + s] - low, 0, CZ + 3 * HZ - 1)
            y0 = jnp.clip(meta_ref[2 * slots + s], 0, NY - 5)
            block = lax.div(s, share)
            slot = s - block * share
            values = []
            for c in range(3):
                row = jnp.broadcast_to(recv_ref[block, pl.ds(c * share + slot, 1), :], (8, LANES))
                values.append(jnp.where(lane < NGLL, row, 0.0))
            half = lax.shift_right_logical(y0, 7)
            yl = y0 & (LANES - 1)
            index = ramp - (25 * x0 + yl)
            rows = (sub >= x0) & (sub < jnp.where(good, x0 + 5, 0))
            at = (half * ZP + zb) * 24
            place(at, values, index, rows & (lane >= yl) & (lane < yl + 5))
            later.append((at, values, index, rows, yl))
        widest = functools.reduce(jnp.maximum, [entry[4] for entry in later])

        @pl.when(widest > LANES - 5)
        def _():
            for at, values, index, rows, yl in later:
                over = rows & (lane < yl + 5 - LANES)

                @pl.when(yl > LANES - 5)
                def _():
                    place(at + ZP * 24, values, index + LANES, over)

        return 0

    lax.fori_loop(0, lax.div(n + SUM_UNROLL - 1, SUM_UNROLL), summed, 0)


def finish_kernel(n_lat, taps_ref, wx_ref, acc, wy_ref, out_ref, planes, rows_ref, send_sem, recv_sem):
    tile, slab = lax.axis_index("lat"), lax.axis_index("rad")
    barrier = pltpu.get_barrier_semaphore()
    has_prev, has_next = tile > 0, tile < n_lat - 1
    halo = HW * CZ

    @pl.when(has_prev)
    def _():
        pl.semaphore_signal(barrier, inc=1, device_id=(tile - 1, slab), device_id_type=MESH)

    @pl.when(has_next)
    def _():
        pl.semaphore_signal(barrier, inc=1, device_id=(tile + 1, slab), device_id_type=MESH)

    def at(c, row, count):
        return rows_ref.at[:, pl.ds(c * PADX * CZ + row, count), :]

    def to_next(c):
        return pltpu.make_async_remote_copy(
            src_ref=at(c, CX * CZ, halo),
            dst_ref=at(c, 0, halo),
            send_sem=send_sem.at[0, c],
            recv_sem=recv_sem.at[0, c],
            device_id=(tile + 1, slab),
            device_id_type=MESH,
        )

    def to_prev(c):
        return pltpu.make_async_remote_copy(
            src_ref=at(c, halo, halo),
            dst_ref=at(c, halo + CX * CZ, halo),
            send_sem=send_sem.at[1, c],
            recv_sem=recv_sem.at[1, c],
            device_id=(tile - 1, slab),
            device_id_type=MESH,
        )

    for c in range(3):

        @pl.loop(0, CZ, unroll=4)
        def _(z):
            for half in range(NY // LANES):
                total = jnp.zeros((CX, LANES), jnp.float32)
                for d in range(TAPS):
                    weight = taps_ref[(slab * CZ + z) * TAPS + d]
                    row = pl.multiple_of(((half * ZP + z + HZ + d) * 3 + c) * CX, 8)
                    total = total + weight * acc[pl.ds(row, CX), :]
                cols = slice(half * LANES, (half + 1) * LANES)
                planes[pl.ds(pl.multiple_of(z * CX, 8), CX), cols] = total

        product = jnp.dot(planes[...], wy_ref[...], precision=lax.Precision.HIGHEST)
        for z in range(CZ):
            for half in range(NY // LANES):
                piece = product[z * CX : (z + 1) * CX, half * LANES : (half + 1) * LANES]
                rows_ref[half, pl.ds(c * PADX * CZ + halo + z, CX, stride=CZ), :] = piece

        if c == 0:
            beside = jnp.minimum(tile, 1) + jnp.minimum(n_lat - 1 - tile, 1)
            pl.semaphore_wait(barrier, beside)

        @pl.when(has_next)
        def _():
            to_next(c).start()

        @pl.when(has_prev)
        def _():
            to_prev(c).start()

        zeros = jnp.zeros((NY // LANES, halo, LANES), jnp.float32)

        @pl.when(tile == 0)
        def _():
            rows_ref[:, c * PADX * CZ : c * PADX * CZ + halo, :] = zeros

        @pl.when(tile == n_lat - 1)
        def _():
            rows_ref[:, c * PADX * CZ + halo + CX * CZ : (c + 1) * PADX * CZ, :] = zeros

    for c in range(3):

        @pl.when(has_prev)
        def _():
            to_next(c).wait_recv()

        @pl.when(has_next)
        def _():
            to_prev(c).wait_recv()

        @pl.loop(0, CX)
        def _(x):
            for half in range(NY // LANES):
                total = jnp.zeros((CZ, LANES), jnp.float32)
                for d in range(2 * HW + 1):
                    row = pl.multiple_of(c * PADX * CZ + (x + d) * CZ, 8)
                    total = total + wx_ref[x * (2 * HW + 1) + d] * rows_ref[half, pl.ds(row, CZ), :]
                out_ref[c, x, :, half * LANES : (half + 1) * LANES] = total

    for c in range(3):

        @pl.when(has_next)
        def _():
            to_next(c).wait_send()

        @pl.when(has_prev)
        def _():
            to_prev(c).wait_send()


def x_weights(width_class, n_lat):
    rows = lax.axis_index("lat") * CX + jnp.arange(CX)
    sigma = 1.0 + 0.75 * width_class[0].astype(jnp.float32)
    offsets = jnp.arange(-HW, HW + 1)
    target = rows[:, None] + offsets[None, :]
    valid = (target >= 0) & (target < CX * n_lat)
    gauss = jnp.exp(-(offsets[None, :].astype(jnp.float32) ** 2) / (2.0 * sigma**2))
    gauss = jnp.where(valid, gauss, 0.0)
    return gauss / jnp.sum(gauss, axis=1, keepdims=True)


def on_device(n_lat, n_rad, kernels, cells, tiles, width_class):
    elements = tiles.shape[0]
    cap = max(2, 2 * elements // n_lat)
    share = -(-cap // n_rad)
    blocks = n_rad * n_lat
    slots = blocks * share
    params = pltpu.CompilerParams(vmem_limit_bytes=VMEM_LIMIT)
    smem = pl.BlockSpec(memory_space=pltpu.SMEM)
    vmem = pl.BlockSpec(memory_space=pltpu.VMEM)
    hbm = pl.BlockSpec(memory_space=pl.ANY)
    send = pl.pallas_call(
        functools.partial(pack_kernel, n_lat, n_rad, share, elements),
        out_shape=jax.ShapeDtypeStruct((n_lat + 1, 3 * share, LANES), jnp.float32),
        in_specs=[smem, hbm, hbm],
        out_specs=vmem,
        scratch_shapes=[
            pltpu.SMEM((n_lat,), jnp.int32),
            pltpu.SMEM((elements + PACK_UNROLL,), jnp.int32),
            pltpu.SMEM((elements + PACK_UNROLL,), jnp.int32),
            pltpu.SMEM(cells.shape, jnp.int32),
            pltpu.VMEM(kernels.shape, jnp.float32),
            pltpu.SemaphoreType.DMA((2,)),
        ],
        compiler_params=params,
    )(tiles.reshape(-1), cells, kernels)
    recv = pl.pallas_call(
        functools.partial(exchange_kernel, n_lat, n_rad),
        out_shape=jax.ShapeDtypeStruct((n_rad, n_lat, 3 * share, LANES), jnp.float32),
        in_specs=[vmem],
        out_specs=vmem,
        scratch_shapes=[
            pltpu.SemaphoreType.DMA,
            pltpu.SemaphoreType.DMA((n_lat,)),
            pltpu.SemaphoreType.DMA((n_lat,)),
            pltpu.SemaphoreType.DMA((3, n_lat)),
            pltpu.SemaphoreType.DMA((3, n_lat)),
        ],
        compiler_params=pltpu.CompilerParams(
            vmem_limit_bytes=VMEM_LIMIT, collective_id=0, has_side_effects=True
        ),
    )(send)
    recv = recv.reshape(blocks, 3 * share, LANES)
    meta = recv[:, :share, NGLL:].transpose(2, 0, 1).reshape(-1).astype(jnp.int32)
    grid_rows = NY // LANES * ZP * 24
    summed = pl.pallas_call(
        functools.partial(sum_kernel, blocks, share),
        out_shape=jax.ShapeDtypeStruct((grid_rows, LANES), jnp.float32),
        in_specs=[smem, vmem],
        out_specs=vmem,
        scratch_shapes=[pltpu.SMEM((slots + SUM_UNROLL,), jnp.int32)],
        compiler_params=params,
    )(meta, recv)
    return pl.pallas_call(
        functools.partial(finish_kernel, n_lat),
        out_shape=jax.ShapeDtypeStruct((3, CX, CZ, NY), jnp.float32),
        in_specs=[smem, smem, vmem, vmem],
        out_specs=vmem,
        scratch_shapes=[
            pltpu.VMEM((CZ * CX, NY), jnp.float32),
            pltpu.VMEM((NY // LANES, 3 * PADX * CZ, LANES), jnp.float32),
            pltpu.SemaphoreType.DMA((2, 3)),
            pltpu.SemaphoreType.DMA((2, 3)),
        ],
        compiler_params=pltpu.CompilerParams(
            vmem_limit_bytes=VMEM_LIMIT, collective_id=1, has_side_effects=True
        ),
    )(
        jnp.asarray(z_taps(n_rad).reshape(-1)),
        x_weights(width_class, n_lat).reshape(-1),
        summed,
        jnp.asarray(band_matrix(NY, 2.5, HY).T.astype(np.float32)),
    )

ROW_TILES = 3
Z_BINS = 11
Y_TILES = 17
WINDOW = CZ + 2 * HZ
DEPTH = 2 * CX * WINDOW
SUM_WAYS = 32
SUM_GROUP = 4
CUTS = 3


def gather_kernel(n_lat, n_rad, block, width_ref, tiles_hbm, cells_hbm, kern_hbm, data_ref, words_ref, whi_ref, wlo_ref,
                  kern_ref, tiles_ref, cells_ref, index_ref, compact_ref, in_sem, is_sem, ir_sem, zs, zr, xs, xr, ys, yr, bs, br):
    lat, rad = lax.axis_index("lat"), lax.axis_index("rad")
    levels = n_lat // 2
    z, x = lax.div(lat, 2), lax.rem(lat, 2)
    y, k = lax.div(rad, 2), lax.rem(rad, 2)
    across_x, across_y, across_k = lat + 1 - 2 * x, rad + 2 - 4 * y, rad + 1 - 2 * k
    barrier = pltpu.get_barrier_semaphore()

    @pl.loop(1, n_lat)
    def _(step):
        pl.semaphore_signal(barrier, inc=1, device_id=(lax.rem(lat + step, n_lat), rad), device_id_type=MESH)

    for peer in (across_y, across_k):
        pl.semaphore_signal(barrier, inc=1, device_id=(lat, peer), device_id_type=MESH)
    points = kern_hbm.shape[1]
    split = block // 6 * LANES
    brought = [
        pltpu.make_async_copy(kern_hbm.at[:, :split], kern_ref.at[:, :split], in_sem.at[0]),
        pltpu.make_async_copy(kern_hbm.at[:, split:], kern_ref.at[:, split:points], in_sem.at[3]),
        pltpu.make_async_copy(tiles_hbm, tiles_ref, in_sem.at[1]),
        pltpu.make_async_copy(cells_hbm, cells_ref, in_sem.at[2]),
    ]
    for copy in brought:
        copy.start()
    if kern_ref.shape[1] > points:
        kern_ref[:, points:] = jnp.zeros((3, kern_ref.shape[1] - points), jnp.float32)

    half = block // 2
    part = half // 2
    mine = k * half
    piece = part // CUTS
    starts = [mine + (y if j < CUTS else 1 - y) * part + j % CUTS * piece for j in range(2 * CUTS)]

    def move(row, count, send_sem, recv_sem, device):
        rows = data_ref.at[pl.ds(pl.multiple_of(row, 8), count)]
        return pltpu.make_async_remote_copy(
            src_ref=rows, dst_ref=rows, send_sem=send_sem, recv_sem=recv_sem,
            device_id=device, device_id_type=MESH)

    def z_move(i, j, up):
        way = 0 if up else 1
        return move(i * block + starts[j], piece, zs.at[i, way], zr.at[i, j], (lat + (2 if up else -2), rad))

    def x_move(i, j):
        return move(i * block + starts[j], piece, xs.at[j // CUTS], xr.at[i, j], (across_x, rad))

    def y_move(i, j):
        return move(i * block + starts[j], piece, ys, yr.at[i, j % CUTS], (lat, across_y))

    def k_move(i):
        return move(i * block + mine, half, bs, br, (lat, across_k))

    def sized(rows, send_sem, recv_sem, device):
        return move(0, rows, send_sem, recv_sem, device)

    def index_move(step):
        to = lax.rem(lat + step, n_lat)
        return pltpu.make_async_remote_copy(
            src_ref=index_ref.at[lat], dst_ref=index_ref.at[lat], send_sem=is_sem, recv_sem=ir_sem,
            device_id=(to, rad), device_id_type=MESH)

    def index_all():
        others = index_ref.at[pl.ds(0, n_lat - 1)]
        return pltpu.make_async_remote_copy(
            src_ref=others, dst_ref=others, send_sem=is_sem, recv_sem=ir_sem,
            device_id=(across_x, rad), device_id_type=MESH)

    can_up, can_down = z < levels - 1, z > 0
    at_end = (z == 0) | (z == levels - 1)
    long_up, long_down = z < levels - 2, z > 1
    base = pl.multiple_of(lat * block, 8)
    sets = block // 24

    def pack(first, count):
        @pl.loop(0, count, unroll=4)
        def _(g):
            at = (first + g) * 8 * LANES
            rows = [kern_ref[:, pl.ds(pl.multiple_of(at + u * LANES, LANES), LANES)] for u in range(8)]
            data_ref[pl.ds(base + pl.multiple_of((first + g) * 24, 8), 24), :] = jnp.concatenate(rows, axis=0)

    def pack_part(j):
        pack(k * (sets // 2) + (y if j == 0 else 1 - y) * (sets // 4), sets // 4)

    @pl.when(k == 0)
    def _():
        brought[0].wait()

    @pl.when(k == 1)
    def _():
        brought[1].wait()

    pack_part(0)
    pl.semaphore_wait(barrier, n_lat - 1 + 2)

    def own_z(j, up):
        able = (long_up if up else long_down) if j >= CUTS else (can_up if up else can_down)

        @pl.when(able)
        def _():
            z_move(lat, j, up).start()

    for j in range(CUTS):
        own_z(j, True)
        own_z(j, False)
        x_move(lat, j).start()
    pack_part(1)
    for j in range(CUTS, 2 * CUTS):
        for up in (True, False):
            if j == CUTS:
                own_z(j, up)
            else:
                pl.when(z == (0 if up else levels - 1))(functools.partial(own_z, j, up))

    brought[2].wait()
    brought[3].wait()
    index_ref[lat] = jnp.concatenate([tiles_ref[...], cells_ref[...], jnp.zeros((4, tiles_ref.shape[1]), jnp.int32)], axis=0)

    @pl.loop(1, n_lat)
    def _(step):
        index_move(step).start()

    @pl.when(k == 1)
    def _():
        brought[0].wait()

    @pl.when(k == 0)
    def _():
        brought[1].wait()

    pack((1 - k) * (sets // 2), sets // 2)

    def weights():
        col = lax.broadcasted_iota(jnp.int32, (8, DEPTH), 1)
        beside = col >= CX * WINDOW
        rest = jnp.where(beside, col - CX * WINDOW, col)
        xl = lax.shift_right_logical(rest * 1639, 16)
        zc = rest - WINDOW * xl
        place = jnp.where(beside, jnp.where(xl < HW, xl + CX, xl - CX), xl)
        sub = lax.broadcasted_iota(jnp.int32, (8, DEPTH), 0)
        sigma = 1.0 + 0.75 * jnp.full((8, DEPTH), width_ref[0], jnp.int32).astype(jnp.float32)
        twice = 2.0 * sigma * sigma

        def bell(d, reach, scale):
            square = (d * d).astype(jnp.float32)
            return jnp.where(jnp.abs(d) <= reach, jnp.exp(-square / scale), 0.0)

        norm = jnp.zeros((8, DEPTH), jnp.float32)
        for d in range(-HW, HW + 1):
            at = lat * CX + sub + d
            norm += jnp.where((at >= 0) & (at < CX * n_lat), jnp.exp(-float(d * d) / twice), 0.0)
        wx = bell(place - sub, HW, twice) / norm
        for zv in range(CZ // 8):
            norm = jnp.zeros((8, DEPTH), jnp.float32)
            zz = sub + 8 * zv
            for d in range(-HZ, HZ + 1):
                at = rad * CZ + zz + d
                norm += jnp.where((at >= 0) & (at < CZ * n_rad), float(np.exp(-d * d / 4.5)), 0.0)
            kern_w[zv * 8 : zv * 8 + 8, :] = bell(zc - HZ - zz, HZ, 4.5) / norm
        for xx in range(CX):
            both = kern_w[...] * wx[xx : xx + 1, :]
            high = both.astype(jnp.bfloat16)
            whi_ref[xx * CZ : xx * CZ + CZ, :] = high
            wlo_ref[xx * CZ : xx * CZ + CZ, :] = (both - high.astype(jnp.float32)).astype(jnp.bfloat16)

    kern_w = compact_ref.at[pl.ds(0, CZ)]
    weights()

    def lists():
        index_all().wait_recv()
        elements = index_ref.shape[2]
        shape = (n_lat, elements)
        rel = index_ref[:, 0, :] - lat
        x0 = index_ref[:, 1, :]
        zq = index_ref[:, 2, :] - rad * CZ + HZ + 8
        y0 = index_ref[:, 3, :]
        keep = (rel >= -1) & (rel <= 1) & (zq >= 4) & (zq < WINDOW + 8)
        before = lax.broadcasted_iota(jnp.int32, (elements, elements), 0) < lax.broadcasted_iota(jnp.int32, (elements, elements), 1)
        flags = jnp.where(keep, 1.0, 0.0)
        rank = jnp.dot(flags.astype(jnp.bfloat16), jnp.where(before, 1.0, 0.0).astype(jnp.bfloat16), preferred_element_type=jnp.float32)
        total = jnp.sum(flags, axis=1, keepdims=True).astype(jnp.int32)
        rank = jnp.where(keep, rank, -1.0)
        low = jnp.maximum(x0, jnp.where(rel < 0, HW, 0))
        high = jnp.minimum(x0 + 4, jnp.where(rel > 0, HW - 1, CX - 1))
        code = low + 8 * (high - low + 1)
        lane = lax.broadcasted_iota(jnp.int32, shape, 1)
        fields = [lane, zq, y0, x0, code, jnp.where(rel == 0, 0, 1)]
        fields = [jnp.where(keep, f, 0).astype(jnp.float32) for f in fields]
        slot = lax.broadcasted_iota(jnp.int32, (elements, elements), 0).astype(jnp.float32)
        zero = jnp.zeros((1, elements), jnp.float32)
        for i in range(n_lat):
            stack = jnp.concatenate([f[i : i + 1] for f in fields] + [zero, zero], axis=0).astype(jnp.bfloat16)
            pick = jnp.where(rank[i : i + 1] == slot, 1.0, 0.0).astype(jnp.bfloat16)
            compact_ref[8 * i : 8 * i + 8, :elements] = lax.dot_general(
                stack, pick, (((1,), (1,)), ((), ())), preferred_element_type=jnp.float32)

        def field(f):
            return jnp.concatenate([compact_ref[8 * i + f : 8 * i + f + 1, :elements] for i in range(n_lat)], axis=0).astype(jnp.int32)

        e, zq, y0, x0, code, beside = [field(f) for f in range(6)]
        start = e * NGLL
        row = lax.broadcasted_iota(jnp.int32, shape, 0) * block + 3 * lax.shift_right_logical(start, 7)
        off = start & (LANES - 1)
        words = row | (off << 16) | (((off - 25 * x0) & (LANES - 1)) << 23)
        words_ref[0] = jnp.where(lane == elements - 1, total, words)
        zb = jnp.maximum(lax.shift_right_logical(zq, 2) - 1, 0)
        at = ((beside * Z_BINS + zb) * Y_TILES + lax.shift_right_logical(y0, 4)) * 8
        words_ref[1] = at | ((zq & 7) << 12) | ((y0 & 127) << 16) | (code << 24)

    def when_there(d, up, body):
        zi = z - d if up else z + d

        @pl.when((zi >= 0) & (zi < levels))
        def _():
            body(2 * zi)

    def later_own():
        for j in range(CUTS + 1, 2 * CUTS):
            for up in (True, False):
                pl.when(z != (0 if up else levels - 1))(functools.partial(own_z, j, up))

    def extra(d, up, farthest):
        end = (z == d) if up else (z == levels - 1 - d)

        @pl.when(end if farthest else jnp.logical_not(end))
        def _():
            for j in range(CUTS, 2 * CUTS):
                line(d, up, j)

    def line(d, up, j):
        more = can_up if up else can_down

        def body(i):
            i = i + x
            if j < CUTS:
                z_move(i, j, up).wait_recv()

                @pl.when(more)
                def _():
                    z_move(i, j, up).start()

                x_move(i, j).start()
                if d == 1:
                    @pl.when(jnp.logical_not(more))
                    def _():
                        y_move(i, j).start()
            elif d > 1:
                z_move(i, j, up).wait_recv()

                @pl.when(more)
                def _():
                    z_move(i, j, up).start()

                if d == levels - 1:
                    x_move(i, j).start()
                if j == 2 * CUTS - 1:
                    k_move(i).start()
            else:
                @pl.when(more)
                def _():
                    z_move(i, j, up).wait_recv()
                    z_move(i, j, up).start()
                    if j == 2 * CUTS - 1:
                        k_move(i).start()

        when_there(d, up, body)

    def cross(d, up, j):
        def body(i):
            i = i + 1 - x
            if j < CUTS:
                x_move(i, j).wait_recv()
                if d < levels - 1:
                    y_move(i, j).start()
            elif d == levels - 1:
                x_move(i, j).wait_recv()
                if j == 2 * CUTS - 1:
                    k_move(i).start()

        when_there(d, up, body)

    def y_done(d, up, own_column):
        def body(i):
            i = i + (x if own_column else 1 - x)

            def finish():
                for j in range(CUTS):
                    y_move(i, CUTS + j).wait_recv()
                k_move(i).start()

            if own_column:
                pl.when(jnp.logical_not(can_up if up else can_down))(finish)
            else:
                finish()

        when_there(d, up, body)

    ways = lambda d: (True, False) if d else (True,)
    for d in range(1, levels + 1):
        for j in range(CUTS):
            if d < levels:
                for up in ways(d):
                    line(d, up, j)
            for up in ways(d - 1):
                cross(d - 1, up, j)
            if d == 3 and j == 0:
                for up in ways(1):
                    extra(1, up, False)
        if d < levels:
            for up in ways(d):
                extra(d, up, True)
        if d == 1:
            later_own()
        if d == 3:
            for up in ways(2):
                extra(2, up, False)
            lists()
        if d == levels:
            for j in range(CUTS, 2 * CUTS):
                for up in ways(d - 1):
                    cross(d - 1, up, j)
        if d == 2:
            for up in ways(1):
                y_done(1, up, True)
        if 2 <= d <= levels:
            for up in ways(d - 2):
                y_done(d - 2, up, False)

    index_all().wait_send()
    sized(levels * part, xs.at[0], xr.at[0, 0], (across_x, rad)).wait_send()

    @pl.when(at_end)
    def _():
        sized(part, xs.at[1], xr.at[0, 1], (across_x, rad)).wait_send()

    for up in (True, False):
        way = 0 if up else 1
        peer = (lat + (2 if up else -2), rad)

        @pl.when(can_up if up else can_down)
        def _():
            for zi in range(levels):
                passed = (zi <= z) if up else (zi >= z)
                both = zi < levels - 2 if up else zi > 1

                @pl.when(passed)
                def _():
                    sized(2 * part if both else part, zs.at[2 * zi + x, way], zr.at[0, 0], peer).wait_send()

    sized(levels * part, ys, yr.at[0, 0], (lat, across_y)).wait_send()
    everything = sized((n_lat - 1) * half, bs, br, (lat, across_k))
    everything.wait_send()
    everything.wait_recv()


def grid_kernel(n_lat, words_ref, data_ref, whi_ref, wlo_ref, ghi_hbm, glo_hbm, out_hbm, acc0, acc1, acc2, fields, result, words, todo, ghi_ref, glo_ref, sem, smooth_sem, out_sem):
    accs = (acc0, acc1, acc2)
    smooth = [pltpu.make_async_copy(ghi_hbm, ghi_ref, smooth_sem.at[0]), pltpu.make_async_copy(glo_hbm, glo_ref, smooth_sem.at[1])]
    bring = pltpu.make_async_copy(words_ref, words.at[:, pl.ds(0, n_lat), :], sem)
    bring.start()
    for copy in smooth:
        copy.start()
    rows = acc0.shape[0]

    @pl.loop(0, rows // 8, unroll=11)
    def _(r):
        for acc in accs:
            acc[pl.ds(pl.multiple_of(r * 8, 8), 8), :] = jnp.zeros((8, LANES), jnp.float32)

    bring.wait()
    lane = lax.broadcasted_iota(jnp.int32, (8, LANES), 1)
    sub = lax.broadcasted_iota(jnp.int32, (8, LANES), 0)
    across = lane & 15
    along = lax.shift_right_logical(lane, 4)
    elements = words.shape[2]

    for u in range(SUM_GROUP):
        words[0, n_lat, u] = 0
        words[1, n_lat, u] = 0

    def listed(i, n):
        many = lax.div(words[0, i, elements - 1] + SUM_GROUP - 1, SUM_GROUP)

        @pl.loop(0, lax.div(many + 7, 8))
        def _(t):
            for u in range(8):
                todo[n + t * 8 + u] = (i << 16) + (t * 8 + u) * SUM_GROUP

        return n + many

    groups = lax.fori_loop(0, n_lat, listed, 0)
    batch = SUM_WAYS // SUM_GROUP
    for u in range(batch):
        todo[groups + u] = n_lat << 16

    @pl.loop(0, lax.div(groups + batch - 1, batch))
    def _(step):
        for g in range(batch):
            first_slot = todo[step * batch + g]
            i = lax.shift_right_logical(first_slot, 16)
            p0 = first_slot & 0xFFFF
            for u in range(SUM_GROUP):
                w0, w1 = words[0, i, p0 + u], words[1, i, p0 + u]
                row = w0 & 0xFFFF
                at = pl.multiple_of(w1 & 0xFFF, 8)
                v0, v1 = jnp.full((8, LANES), w0, jnp.int32), jnp.full((8, LANES), w1, jnp.int32)
                off = lax.shift_right_logical(v0, 16) & 127
                shift = lax.shift_right_logical(v0, 23)
                zq = lax.shift_right_logical(v1, 12)
                y0 = lax.shift_right_logical(v1, 16)
                low = lax.shift_right_logical(v1, 24)
                wide = lax.shift_right_logical(v1, 27)
                tz = (sub - zq) & 7
                turned = (lane - y0) & (LANES - 1)
                ty = turned & 15
                xl = lax.shift_right_logical(turned, 4)
                tx = (xl - low) & 7
                index = (25 * xl + shift + 5 * tz + ty) & (LANES - 1)
                good = (jnp.maximum(tz, ty) < 5) & (tx < wide)
                first = across >= (y0 & 15)
                here, there = good & first, good & jnp.logical_not(first)
                head = lane >= off
                for c in range(3):
                    a = data_ref[pl.ds(row + c, 1), :]
                    b = data_ref[pl.ds(row + 3 + c, 1), :]
                    v = jnp.broadcast_to(jnp.where(head[0:1], a, b), (8, LANES))
                    v = jnp.take_along_axis(v, index, axis=1, mode="promise_in_bounds")
                    accs[c][pl.ds(at, 8), :] += jnp.where(here, v, 0.0)
                    accs[c][pl.ds(at + 8, 8), :] += jnp.where(there, v, 0.0)

    low_half = sub < 4
    for copy in smooth:
        copy.wait()
    for c in range(3):
        acc, field = accs[c], fields.at[c]

        @pl.loop(0, 2, unroll=2)
        def _(g):
            @pl.loop(0, WINDOW // 8, unroll=WINDOW // 8)
            def _(h):
                for side in range(2):
                    v = []
                    for t in range(8):
                        def bins(n):
                            r = ((g * Z_BINS + 2 * h + n) * Y_TILES + side * 8 + t) * 8
                            return acc[pl.ds(pl.multiple_of(r, 8), 8), :]

                        v.append(bins(1) + jnp.where(low_half, bins(0), bins(2)))
                    for bit in (1, 2, 4):
                        v = [jnp.where((along & bit) == 0, v[t], v[(t + bit) % 8]) for t in range(8)]
                    v = [v[0]] + [pltpu.roll(v[8 - xl], LANES - 16 * xl, 1) for xl in range(1, 8)]
                    for xl in range(8):
                        r = pl.multiple_of(g * (CX * WINDOW) + xl * WINDOW + h * 8, 8)
                        field[pl.ds(r, 8), side * LANES : (side + 1) * LANES] = v[xl]

        def split(a):
            high = a.astype(jnp.bfloat16)
            return high, (a - high.astype(jnp.float32)).astype(jnp.bfloat16)

        def dot(a, b):
            return jnp.dot(a, b, preferred_element_type=jnp.float32)

        high, low = split(field[...])
        whi = whi_ref[...]
        mixed = dot(whi, high) + dot(wlo_ref[...], high) + dot(whi, low)
        high, low = split(mixed)
        ghi = ghi_ref[...]
        done = dot(high, ghi) + dot(low, ghi) + dot(high, glo_ref[...])
        result[c] = done.reshape(CX, CZ, NY)
        pltpu.make_async_copy(result.at[c], out_hbm.at[c], out_sem.at[c]).start()
    for c in range(3):
        pltpu.make_async_copy(result.at[c], out_hbm.at[c], out_sem.at[c]).wait()


def on_device_whole(n_lat, n_rad, kernels, cells, tiles, width_class):
    elements = tiles.shape[0]
    block = -(-kernels.shape[1] // LANES * 3 // 96) * 96
    smem = pl.BlockSpec(memory_space=pltpu.SMEM)
    vmem = pl.BlockSpec(memory_space=pltpu.VMEM)
    hbm = pl.BlockSpec(memory_space=pltpu.HBM)
    dma = pltpu.SemaphoreType.DMA
    stay = functools.partial(pltpu.with_memory_space_constraint, memory_space=pltpu.HBM)
    data, words, whi, wlo = pl.pallas_call(
        functools.partial(gather_kernel, n_lat, n_rad, block),
        out_shape=[
            jax.ShapeDtypeStruct((n_lat * block + 8, LANES), jnp.float32),
            jax.ShapeDtypeStruct((2, n_lat, elements), jnp.int32),
            jax.ShapeDtypeStruct((CX * CZ, DEPTH), jnp.bfloat16),
            jax.ShapeDtypeStruct((CX * CZ, DEPTH), jnp.bfloat16),
        ],
        in_specs=[smem, hbm, hbm, hbm],
        out_specs=[vmem] * 4,
        scratch_shapes=[
            pltpu.VMEM((3, block // 3 * LANES), jnp.float32),
            pltpu.VMEM((1, elements), jnp.int32),
            pltpu.VMEM(cells.shape, jnp.int32),
            pltpu.VMEM((n_lat, 8, elements), jnp.int32),
            pltpu.VMEM((8 * n_lat, DEPTH), jnp.float32),
            dma((4,)), dma, dma,
            dma((n_lat, 2)), dma((n_lat, 2 * CUTS)), dma((2,)), dma((n_lat, 2 * CUTS)),
            dma, dma((n_lat, CUTS)), dma, dma,
        ],
        compiler_params=pltpu.CompilerParams(
            vmem_limit_bytes=VMEM_LIMIT, collective_id=0, has_side_effects=True
        ),
    )(width_class, *map(stay, (tiles.reshape(1, elements), cells, kernels)))
    smooth = band_matrix(NY, 2.5, HY).T.astype(np.float32)
    high = smooth.astype(jnp.bfloat16)
    low = (smooth - high.astype(np.float32)).astype(jnp.bfloat16)
    rows = 2 * Z_BINS * Y_TILES * 8
    return pl.pallas_call(
        functools.partial(grid_kernel, n_lat),
        out_shape=jax.ShapeDtypeStruct((3, CX, CZ, NY), jnp.float32),
        in_specs=[vmem] * 4 + [hbm] * 2,
        out_specs=hbm,
        scratch_shapes=[
            pltpu.VMEM((rows, LANES), jnp.float32),
            pltpu.VMEM((rows, LANES), jnp.float32),
            pltpu.VMEM((rows, LANES), jnp.float32),
            pltpu.VMEM((3, DEPTH, NY), jnp.float32),
            pltpu.VMEM((3, CX, CZ, NY), jnp.float32),
            pltpu.SMEM((2, n_lat + 1, elements), jnp.int32),
            pltpu.SMEM((n_lat * elements // SUM_GROUP + 16,), jnp.int32),
            pltpu.VMEM((NY, NY), jnp.bfloat16),
            pltpu.VMEM((NY, NY), jnp.bfloat16),
            dma, dma((2,)), dma((3,)),
        ],
        compiler_params=pltpu.CompilerParams(vmem_limit_bytes=VMEM_LIMIT),
    )(words, data, whi, wlo, stay(jnp.asarray(high)), stay(jnp.asarray(low)))


def solution(mesh):
    n_lat, n_rad = mesh.shape["lat"], mesh.shape["rad"]
    whole = n_lat == 8 and n_rad == 4
    return jax.shard_map(
        functools.partial(on_device_whole if whole else on_device, n_lat, n_rad),
        mesh=mesh,
        in_specs=(P(None, "lat"), P(None, "lat"), P("lat", None), P("lat")),
        out_specs=P(None, "lat", "rad", None),
        check_vma=False,
    )
```

```python
import functools

import jax
import jax.numpy as jnp
import numpy as np
from jax import lax
from jax.experimental import pallas as pl
from jax.experimental.pallas import tpu as pltpu
from jax.sharding import PartitionSpec as P

CX = 8
NY = 256
CZ = 32
NGLL = 125
HW = 4
HY = 8
HZ = 4
ZP = CZ + 4 * HZ
LANES = 128
TAPS = 2 * HZ + 1
PADX = CX + 2 * HW
PACK_UNROLL = 4
SUM_UNROLL = 4
VMEM_LIMIT = 48 * 2**20
MESH = pl.DeviceIdType.MESH


def band_matrix(count, sigma, half):
    place = np.arange(count)
    gap = place[None, :] - place[:, None]
    gauss = np.where(np.abs(gap) <= half, np.exp(-(gap**2) / (2.0 * sigma**2)), 0.0)
    return gauss / gauss.sum(axis=1, keepdims=True)


def z_taps(n_rad):
    full = np.pad(band_matrix(CZ * n_rad, 1.5, HZ), ((0, 0), (HZ, HZ)))
    return np.stack([full[z, z : z + TAPS] for z in range(CZ * n_rad)]).astype(np.float32)


def pack_kernel(
    n_lat, n_rad, share, elements, tiles_ref, cells_hbm, kern_hbm, out_ref, count, todo, place, cells_ref, kern_ref, sems
):
    slab = lax.axis_index("rad")
    rows = elements * NGLL // LANES
    bring_cells = pltpu.make_async_copy(cells_hbm, cells_ref, sems.at[0])
    bring_kern = pltpu.make_async_copy(kern_hbm, kern_ref, sems.at[1])
    bring_cells.start()
    bring_kern.start()
    out_ref[...] = jnp.full(out_ref.shape, -1000.0, jnp.float32)
    lane = lax.broadcasted_iota(jnp.int32, (3, LANES), 1)

    @pl.loop(0, n_lat)
    def _(t):
        count[t] = 0

    def listed(e, n):
        t = tiles_ref[e]
        rank = count[t]
        count[t] = rank + 1
        slot = lax.div(rank, n_rad)
        todo[n] = e
        place[n] = t * share + slot
        return n + jnp.where(rank - slot * n_rad == slab, 1, 0)

    n = lax.fori_loop(0, elements, listed, 0, unroll=4)
    for more in range(PACK_UNROLL):
        todo[n + more] = 0
        place[n + more] = n_lat * share
    bring_cells.wait()
    bring_kern.wait()

    def packed(step, _):
        for u in range(PACK_UNROLL):
            e = todo[step * PACK_UNROLL + u]
            at = place[step * PACK_UNROLL + u]
            start = e * NGLL
            row = lax.shift_right_logical(start, 7)
            off = start & (LANES - 1)
            after = jnp.minimum(row + 1, rows - 1)
            a = kern_ref[:, pl.ds(pl.multiple_of(row * LANES, LANES), LANES)]
            b = kern_ref[:, pl.ds(pl.multiple_of(after * LANES, LANES), LANES)]
            v = pltpu.roll(jnp.where(lane >= off, a, b), (LANES - off) & (LANES - 1), 1)
            v = jnp.where(lane == NGLL, cells_ref[0, e].astype(jnp.float32), v)
            v = jnp.where(lane == NGLL + 1, cells_ref[1, e].astype(jnp.float32), v)
            v = jnp.where(lane == NGLL + 2, cells_ref[2, e].astype(jnp.float32), v)
            t = lax.div(at, share)
            slot = at - t * share
            for c in range(3):
                out_ref[t, pl.ds(c * share + slot, 1), :] = v[c : c + 1]
        return 0

    lax.fori_loop(0, lax.div(n + PACK_UNROLL - 1, PACK_UNROLL), packed, 0)


def exchange_kernel(n_lat, n_rad, send_ref, recv_ref, own_sem, send_sem, recv_sem, fwd_sem, got_sem):
    tile, slab = lax.axis_index("lat"), lax.axis_index("rad")
    barrier = pltpu.get_barrier_semaphore()

    @pl.loop(1, n_lat)
    def _(k):
        pl.semaphore_signal(barrier, inc=1, device_id=(lax.rem(tile + k, n_lat), slab), device_id_type=MESH)

    pair = slab + 1 - 2 * lax.rem(slab, 2)
    other = slab + 2 - 4 * lax.div(slab, 2)
    for peer in (pair, other):
        pl.semaphore_signal(barrier, inc=1, device_id=(tile, peer), device_id_type=MESH)
    pl.semaphore_wait(barrier, n_lat - 1 + 2)

    def across(k):
        to = lax.rem(tile + k, n_lat)
        return pltpu.make_async_remote_copy(
            src_ref=send_ref.at[to],
            dst_ref=recv_ref.at[slab, tile],
            send_sem=send_sem.at[k],
            recv_sem=recv_sem.at[k],
            device_id=(to, slab),
            device_id_type=MESH,
        )

    def share(k, of, to, way):
        block = recv_ref.at[of, lax.rem(tile + n_lat - k, n_lat)]
        return pltpu.make_async_remote_copy(
            src_ref=block,
            dst_ref=block,
            send_sem=fwd_sem.at[way, k],
            recv_sem=got_sem.at[way, k],
            device_id=(tile, to),
            device_id_type=MESH,
        )

    def forward(k):
        share(k, slab, other, 0).start()
        share(k, slab, pair, 1).start()

    def relay(k):
        share(k, other, other, 0).wait_recv()
        share(k, other, pair, 2).start()

    @pl.loop(1, n_lat)
    def _(k):
        across(k).start()

    own = pltpu.make_async_copy(send_ref.at[tile], recv_ref.at[slab, tile], own_sem)
    own.start()
    own.wait()
    forward(0)

    @pl.loop(1, n_lat)
    def _(k):
        across(k).wait_recv()
        forward(k)

    @pl.loop(0, n_lat)
    def _(k):
        relay(k)

    @pl.loop(0, n_lat)
    def _(k):
        share(k, pair, pair, 1).wait_recv()
        share(k, other + pair - slab, pair, 2).wait_recv()

    @pl.loop(1, n_lat)
    def _(k):
        across(k).wait_send()

    @pl.loop(0, n_lat)
    def _(k):
        share(k, slab, other, 0).wait_send()
        share(k, slab, pair, 1).wait_send()
        share(k, other, pair, 2).wait_send()


def sum_kernel(blocks, share, meta_ref, recv_ref, acc, todo):
    slab = lax.axis_index("rad")
    slots = blocks * share
    acc[...] = jnp.zeros(acc.shape, jnp.float32)
    lane = lax.broadcasted_iota(jnp.int32, (8, LANES), 1)
    sub = lax.broadcasted_iota(jnp.int32, (8, LANES), 0)
    ramp = 25 * sub + lane
    low = slab * CZ - 2 * HZ

    def listed(s, n):
        zb = meta_ref[slots + s] - low
        todo[n] = s
        return n + jnp.where((zb >= 0) & (zb < CZ + 3 * HZ), 1, 0)

    n = lax.fori_loop(0, slots, listed, 0, unroll=8)
    for more in range(SUM_UNROLL):
        todo[n + more] = 0

    def place(at, values, index, mask):
        for j in range(5):
            picked = jnp.where(mask, index + 5 * j, NGLL)
            for c in range(3):
                piece = jnp.take_along_axis(values[c], picked, axis=1, mode="promise_in_bounds")
                acc[pl.ds(pl.multiple_of(at + (3 * j + c) * 8, 8), 8), :] += piece

    def summed(step, _):
        later = []
        for u in range(SUM_UNROLL):
            s = todo[step * SUM_UNROLL + u]
            good = step * SUM_UNROLL + u < n
            x0 = jnp.clip(meta_ref[s], 0, CX - 5)
            zb = jnp.clip(meta_ref[slots + s] - low, 0, CZ + 3 * HZ - 1)
            y0 = jnp.clip(meta_ref[2 * slots + s], 0, NY - 5)
            block = lax.div(s, share)
            slot = s - block * share
            values = []
            for c in range(3):
                row = jnp.broadcast_to(recv_ref[block, pl.ds(c * share + slot, 1), :], (8, LANES))
                values.append(jnp.where(lane < NGLL, row, 0.0))
            half = lax.shift_right_logical(y0, 7)
            yl = y0 & (LANES - 1)
            index = ramp - (25 * x0 + yl)
            rows = (sub >= x0) & (sub < jnp.where(good, x0 + 5, 0))
            at = (half * ZP + zb) * 24
            place(at, values, index, rows & (lane >= yl) & (lane < yl + 5))
            later.append((at, values, index, rows, yl))
        widest = functools.reduce(jnp.maximum, [entry[4] for entry in later])

        @pl.when(widest > LANES - 5)
        def _():
            for at, values, index, rows, yl in later:
                over = rows & (lane < yl + 5 - LANES)

                @pl.when(yl > LANES - 5)
                def _():
                    place(at + ZP * 24, values, index + LANES, over)

        return 0

    lax.fori_loop(0, lax.div(n + SUM_UNROLL - 1, SUM_UNROLL), summed, 0)


def finish_kernel(n_lat, taps_ref, wx_ref, acc, wy_ref, out_ref, planes, rows_ref, send_sem, recv_sem):
    tile, slab = lax.axis_index("lat"), lax.axis_index("rad")
    barrier = pltpu.get_barrier_semaphore()
    has_prev, has_next = tile > 0, tile < n_lat - 1
    halo = HW * CZ

    @pl.when(has_prev)
    def _():
        pl.semaphore_signal(barrier, inc=1, device_id=(tile - 1, slab), device_id_type=MESH)

    @pl.when(has_next)
    def _():
        pl.semaphore_signal(barrier, inc=1, device_id=(tile + 1, slab), device_id_type=MESH)

    def at(c, row, count):
        return rows_ref.at[:, pl.ds(c * PADX * CZ + row, count), :]

    def to_next(c):
        return pltpu.make_async_remote_copy(
            src_ref=at(c, CX * CZ, halo),
            dst_ref=at(c, 0, halo),
            send_sem=send_sem.at[0, c],
            recv_sem=recv_sem.at[0, c],
            device_id=(tile + 1, slab),
            device_id_type=MESH,
        )

    def to_prev(c):
        return pltpu.make_async_remote_copy(
            src_ref=at(c, halo, halo),
            dst_ref=at(c, halo + CX * CZ, halo),
            send_sem=send_sem.at[1, c],
            recv_sem=recv_sem.at[1, c],
            device_id=(tile - 1, slab),
            device_id_type=MESH,
        )

    for c in range(3):

        @pl.loop(0, CZ, unroll=4)
        def _(z):
            for half in range(NY // LANES):
                total = jnp.zeros((CX, LANES), jnp.float32)
                for d in range(TAPS):
                    weight = taps_ref[(slab * CZ + z) * TAPS + d]
                    row = pl.multiple_of(((half * ZP + z + HZ + d) * 3 + c) * CX, 8)
                    total = total + weight * acc[pl.ds(row, CX), :]
                cols = slice(half * LANES, (half + 1) * LANES)
                planes[pl.ds(pl.multiple_of(z * CX, 8), CX), cols] = total

        product = jnp.dot(planes[...], wy_ref[...], precision=lax.Precision.HIGHEST)
        for z in range(CZ):
            for half in range(NY // LANES):
                piece = product[z * CX : (z + 1) * CX, half * LANES : (half + 1) * LANES]
                rows_ref[half, pl.ds(c * PADX * CZ + halo + z, CX, stride=CZ), :] = piece

        if c == 0:
            beside = jnp.minimum(tile, 1) + jnp.minimum(n_lat - 1 - tile, 1)
            pl.semaphore_wait(barrier, beside)

        @pl.when(has_next)
        def _():
            to_next(c).start()

        @pl.when(has_prev)
        def _():
            to_prev(c).start()

        zeros = jnp.zeros((NY // LANES, halo, LANES), jnp.float32)

        @pl.when(tile == 0)
        def _():
            rows_ref[:, c * PADX * CZ : c * PADX * CZ + halo, :] = zeros

        @pl.when(tile == n_lat - 1)
        def _():
            rows_ref[:, c * PADX * CZ + halo + CX * CZ : (c + 1) * PADX * CZ, :] = zeros

    for c in range(3):

        @pl.when(has_prev)
        def _():
            to_next(c).wait_recv()

        @pl.when(has_next)
        def _():
            to_prev(c).wait_recv()

        @pl.loop(0, CX)
        def _(x):
            for half in range(NY // LANES):
                total = jnp.zeros((CZ, LANES), jnp.float32)
                for d in range(2 * HW + 1):
                    row = pl.multiple_of(c * PADX * CZ + (x + d) * CZ, 8)
                    total = total + wx_ref[x * (2 * HW + 1) + d] * rows_ref[half, pl.ds(row, CZ), :]
                out_ref[c, x, :, half * LANES : (half + 1) * LANES] = total

    for c in range(3):

        @pl.when(has_next)
        def _():
            to_next(c).wait_send()

        @pl.when(has_prev)
        def _():
            to_prev(c).wait_send()


def x_weights(width_class, n_lat):
    rows = lax.axis_index("lat") * CX + jnp.arange(CX)
    sigma = 1.0 + 0.75 * width_class[0].astype(jnp.float32)
    offsets = jnp.arange(-HW, HW + 1)
    target = rows[:, None] + offsets[None, :]
    valid = (target >= 0) & (target < CX * n_lat)
    gauss = jnp.exp(-(offsets[None, :].astype(jnp.float32) ** 2) / (2.0 * sigma**2))
    gauss = jnp.where(valid, gauss, 0.0)
    return gauss / jnp.sum(gauss, axis=1, keepdims=True)


def on_device(n_lat, n_rad, kernels, cells, tiles, width_class):
    elements = tiles.shape[0]
    cap = max(2, 2 * elements // n_lat)
    share = -(-cap // n_rad)
    blocks = n_rad * n_lat
    slots = blocks * share
    params = pltpu.CompilerParams(vmem_limit_bytes=VMEM_LIMIT)
    smem = pl.BlockSpec(memory_space=pltpu.SMEM)
    vmem = pl.BlockSpec(memory_space=pltpu.VMEM)
    hbm = pl.BlockSpec(memory_space=pl.ANY)
    send = pl.pallas_call(
        functools.partial(pack_kernel, n_lat, n_rad, share, elements),
        out_shape=jax.ShapeDtypeStruct((n_lat + 1, 3 * share, LANES), jnp.float32),
        in_specs=[smem, hbm, hbm],
        out_specs=vmem,
        scratch_shapes=[
            pltpu.SMEM((n_lat,), jnp.int32),
            pltpu.SMEM((elements + PACK_UNROLL,), jnp.int32),
            pltpu.SMEM((elements + PACK_UNROLL,), jnp.int32),
            pltpu.SMEM(cells.shape, jnp.int32),
            pltpu.VMEM(kernels.shape, jnp.float32),
            pltpu.SemaphoreType.DMA((2,)),
        ],
        compiler_params=params,
    )(tiles.reshape(-1), cells, kernels)
    recv = pl.pallas_call(
        functools.partial(exchange_kernel, n_lat, n_rad),
        out_shape=jax.ShapeDtypeStruct((n_rad, n_lat, 3 * share, LANES), jnp.float32),
        in_specs=[vmem],
        out_specs=vmem,
        scratch_shapes=[
            pltpu.SemaphoreType.DMA,
            pltpu.SemaphoreType.DMA((n_lat,)),
            pltpu.SemaphoreType.DMA((n_lat,)),
            pltpu.SemaphoreType.DMA((3, n_lat)),
            pltpu.SemaphoreType.DMA((3, n_lat)),
        ],
        compiler_params=pltpu.CompilerParams(
            vmem_limit_bytes=VMEM_LIMIT, collective_id=0, has_side_effects=True
        ),
    )(send)
    recv = recv.reshape(blocks, 3 * share, LANES)
    meta = recv[:, :share, NGLL:].transpose(2, 0, 1).reshape(-1).astype(jnp.int32)
    grid_rows = NY // LANES * ZP * 24
    summed = pl.pallas_call(
        functools.partial(sum_kernel, blocks, share),
        out_shape=jax.ShapeDtypeStruct((grid_rows, LANES), jnp.float32),
        in_specs=[smem, vmem],
        out_specs=vmem,
        scratch_shapes=[pltpu.SMEM((slots + SUM_UNROLL,), jnp.int32)],
        compiler_params=params,
    )(meta, recv)
    return pl.pallas_call(
        functools.partial(finish_kernel, n_lat),
        out_shape=jax.ShapeDtypeStruct((3, CX, CZ, NY), jnp.float32),
        in_specs=[smem, smem, vmem, vmem],
        out_specs=vmem,
        scratch_shapes=[
            pltpu.VMEM((CZ * CX, NY), jnp.float32),
            pltpu.VMEM((NY // LANES, 3 * PADX * CZ, LANES), jnp.float32),
            pltpu.SemaphoreType.DMA((2, 3)),
            pltpu.SemaphoreType.DMA((2, 3)),
        ],
        compiler_params=pltpu.CompilerParams(
            vmem_limit_bytes=VMEM_LIMIT, collective_id=1, has_side_effects=True
        ),
    )(
        jnp.asarray(z_taps(n_rad).reshape(-1)),
        x_weights(width_class, n_lat).reshape(-1),
        summed,
        jnp.asarray(band_matrix(NY, 2.5, HY).T.astype(np.float32)),
    )

ROW_TILES = 3
Z_BINS = 11
Y_TILES = 17
WINDOW = CZ + 2 * HZ
DEPTH = 2 * CX * WINDOW
SUM_WAYS = 32
SUM_GROUP = 4
CUTS = 4


def gather_kernel(n_lat, n_rad, block, width_ref, tiles_hbm, cells_hbm, kern_hbm, data_ref, words_ref, whi_ref, wlo_ref,
                  kern_ref, tiles_ref, cells_ref, index_ref, compact_ref, in_sem, is_sem, ir_sem, zs, zr, xs, xr, ys, yr, bs, br):
    lat, rad = lax.axis_index("lat"), lax.axis_index("rad")
    levels = n_lat // 2
    z, x = lax.div(lat, 2), lax.rem(lat, 2)
    y, k = lax.div(rad, 2), lax.rem(rad, 2)
    across_x, across_y, across_k = lat + 1 - 2 * x, rad + 2 - 4 * y, rad + 1 - 2 * k
    barrier = pltpu.get_barrier_semaphore()

    @pl.loop(1, n_lat)
    def _(step):
        pl.semaphore_signal(barrier, inc=1, device_id=(lax.rem(lat + step, n_lat), rad), device_id_type=MESH)

    for peer in (across_y, across_k):
        pl.semaphore_signal(barrier, inc=1, device_id=(lat, peer), device_id_type=MESH)
    points = kern_hbm.shape[1]
    split = block // 6 * LANES
    brought = [
        pltpu.make_async_copy(kern_hbm.at[:, :split], kern_ref.at[:, :split], in_sem.at[0]),
        pltpu.make_async_copy(kern_hbm.at[:, split:], kern_ref.at[:, split:points], in_sem.at[3]),
        pltpu.make_async_copy(tiles_hbm, tiles_ref, in_sem.at[1]),
        pltpu.make_async_copy(cells_hbm, cells_ref, in_sem.at[2]),
    ]
    for copy in brought:
        copy.start()
    if kern_ref.shape[1] > points:
        kern_ref[:, points:] = jnp.zeros((3, kern_ref.shape[1] - points), jnp.float32)

    half = block // 2
    part = half // 2
    mine = k * half
    piece = part // CUTS
    starts = [mine + (y if j < CUTS else 1 - y) * part + j % CUTS * piece for j in range(2 * CUTS)]

    def move(row, count, send_sem, recv_sem, device):
        rows = data_ref.at[pl.ds(pl.multiple_of(row, 8), count)]
        return pltpu.make_async_remote_copy(
            src_ref=rows, dst_ref=rows, send_sem=send_sem, recv_sem=recv_sem,
            device_id=device, device_id_type=MESH)

    def z_move(i, j, up):
        way = 0 if up else 1
        return move(i * block + starts[j], piece, zs.at[i, way], zr.at[i, j], (lat + (2 if up else -2), rad))

    def x_move(i, j):
        return move(i * block + starts[j], piece, xs.at[j // CUTS], xr.at[i, j], (across_x, rad))

    def y_move(i, j):
        return move(i * block + starts[j], piece, ys, yr.at[i, j % CUTS], (lat, across_y))

    def k_move(i):
        return move(i * block + mine, half, bs, br, (lat, across_k))

    def sized(rows, send_sem, recv_sem, device):
        return move(0, rows, send_sem, recv_sem, device)

    def index_move(step):
        to = lax.rem(lat + step, n_lat)
        return pltpu.make_async_remote_copy(
            src_ref=index_ref.at[lat], dst_ref=index_ref.at[lat], send_sem=is_sem, recv_sem=ir_sem,
            device_id=(to, rad), device_id_type=MESH)

    def index_all():
        others = index_ref.at[pl.ds(0, n_lat - 1)]
        return pltpu.make_async_remote_copy(
            src_ref=others, dst_ref=others, send_sem=is_sem, recv_sem=ir_sem,
            device_id=(across_x, rad), device_id_type=MESH)

    can_up, can_down = z < levels - 1, z > 0
    at_end = (z == 0) | (z == levels - 1)
    long_up, long_down = z < levels - 2, z > 1
    base = pl.multiple_of(lat * block, 8)
    sets = block // 24

    def pack(first, count):
        @pl.loop(0, count, unroll=4)
        def _(g):
            at = (first + g) * 8 * LANES
            rows = [kern_ref[:, pl.ds(pl.multiple_of(at + u * LANES, LANES), LANES)] for u in range(8)]
            data_ref[pl.ds(base + pl.multiple_of((first + g) * 24, 8), 24), :] = jnp.concatenate(rows, axis=0)

    def pack_part(j):
        pack(k * (sets // 2) + (y if j == 0 else 1 - y) * (sets // 4), sets // 4)

    @pl.when(k == 0)
    def _():
        brought[0].wait()

    @pl.when(k == 1)
    def _():
        brought[1].wait()

    pack_part(0)
    pl.semaphore_wait(barrier, n_lat - 1 + 2)

    def own_z(j, up):
        able = (long_up if up else long_down) if j >= CUTS else (can_up if up else can_down)

        @pl.when(able)
        def _():
            z_move(lat, j, up).start()

    for j in range(CUTS):
        own_z(j, True)
        own_z(j, False)
        x_move(lat, j).start()
    pack_part(1)
    for j in range(CUTS, 2 * CUTS):
        for up in (True, False):
            if j == CUTS:
                own_z(j, up)
            else:
                pl.when(z == (0 if up else levels - 1))(functools.partial(own_z, j, up))

    brought[2].wait()
    brought[3].wait()
    index_ref[lat] = jnp.concatenate([tiles_ref[...], cells_ref[...], jnp.zeros((4, tiles_ref.shape[1]), jnp.int32)], axis=0)

    @pl.loop(1, n_lat)
    def _(step):
        index_move(step).start()

    @pl.when(k == 1)
    def _():
        brought[0].wait()

    @pl.when(k == 0)
    def _():
        brought[1].wait()

    pack((1 - k) * (sets // 2), sets // 2)

    def weights():
        col = lax.broadcasted_iota(jnp.int32, (8, DEPTH), 1)
        beside = col >= CX * WINDOW
        rest = jnp.where(beside, col - CX * WINDOW, col)
        xl = lax.shift_right_logical(rest * 1639, 16)
        zc = rest - WINDOW * xl
        place = jnp.where(beside, jnp.where(xl < HW, xl + CX, xl - CX), xl)
        sub = lax.broadcasted_iota(jnp.int32, (8, DEPTH), 0)
        sigma = 1.0 + 0.75 * jnp.full((8, DEPTH), width_ref[0], jnp.int32).astype(jnp.float32)
        twice = 2.0 * sigma * sigma

        def bell(d, reach, scale):
            square = (d * d).astype(jnp.float32)
            return jnp.where(jnp.abs(d) <= reach, jnp.exp(-square / scale), 0.0)

        norm = jnp.zeros((8, DEPTH), jnp.float32)
        for d in range(-HW, HW + 1):
            at = lat * CX + sub + d
            norm += jnp.where((at >= 0) & (at < CX * n_lat), jnp.exp(-float(d * d) / twice), 0.0)
        wx = bell(place - sub, HW, twice) / norm
        for zv in range(CZ // 8):
            norm = jnp.zeros((8, DEPTH), jnp.float32)
            zz = sub + 8 * zv
            for d in range(-HZ, HZ + 1):
                at = rad * CZ + zz + d
                norm += jnp.where((at >= 0) & (at < CZ * n_rad), float(np.exp(-d * d / 4.5)), 0.0)
            kern_w[zv * 8 : zv * 8 + 8, :] = bell(zc - HZ - zz, HZ, 4.5) / norm
        for xx in range(CX):
            both = kern_w[...] * wx[xx : xx + 1, :]
            high = both.astype(jnp.bfloat16)
            whi_ref[xx * CZ : xx * CZ + CZ, :] = high
            wlo_ref[xx * CZ : xx * CZ + CZ, :] = (both - high.astype(jnp.float32)).astype(jnp.bfloat16)

    kern_w = compact_ref.at[pl.ds(0, CZ)]
    weights()

    def lists():
        index_all().wait_recv()
        elements = index_ref.shape[2]
        shape = (n_lat, elements)
        rel = index_ref[:, 0, :] - lat
        x0 = index_ref[:, 1, :]
        zq = index_ref[:, 2, :] - rad * CZ + HZ + 8
        y0 = index_ref[:, 3, :]
        keep = (rel >= -1) & (rel <= 1) & (zq >= 4) & (zq < WINDOW + 8)
        before = lax.broadcasted_iota(jnp.int32, (elements, elements), 0) < lax.broadcasted_iota(jnp.int32, (elements, elements), 1)
        flags = jnp.where(keep, 1.0, 0.0)
        rank = jnp.dot(flags.astype(jnp.bfloat16), jnp.where(before, 1.0, 0.0).astype(jnp.bfloat16), preferred_element_type=jnp.float32)
        total = jnp.sum(flags, axis=1, keepdims=True).astype(jnp.int32)
        rank = jnp.where(keep, rank, -1.0)
        low = jnp.maximum(x0, jnp.where(rel < 0, HW, 0))
        high = jnp.minimum(x0 + 4, jnp.where(rel > 0, HW - 1, CX - 1))
        code = low + 8 * (high - low + 1)
        lane = lax.broadcasted_iota(jnp.int32, shape, 1)
        fields = [lane, zq, y0, x0, code, jnp.where(rel == 0, 0, 1)]
        fields = [jnp.where(keep, f, 0).astype(jnp.float32) for f in fields]
        slot = lax.broadcasted_iota(jnp.int32, (elements, elements), 0).astype(jnp.float32)
        zero = jnp.zeros((1, elements), jnp.float32)
        for i in range(n_lat):
            stack = jnp.concatenate([f[i : i + 1] for f in fields] + [zero, zero], axis=0).astype(jnp.bfloat16)
            pick = jnp.where(rank[i : i + 1] == slot, 1.0, 0.0).astype(jnp.bfloat16)
            compact_ref[8 * i : 8 * i + 8, :elements] = lax.dot_general(
                stack, pick, (((1,), (1,)), ((), ())), preferred_element_type=jnp.float32)

        def field(f):
            return jnp.concatenate([compact_ref[8 * i + f : 8 * i + f + 1, :elements] for i in range(n_lat)], axis=0).astype(jnp.int32)

        e, zq, y0, x0, code, beside = [field(f) for f in range(6)]
        start = e * NGLL
        row = lax.broadcasted_iota(jnp.int32, shape, 0) * block + 3 * lax.shift_right_logical(start, 7)
        off = start & (LANES - 1)
        words = row | (off << 16) | (((off - 25 * x0) & (LANES - 1)) << 23)
        words_ref[0] = jnp.where(lane == elements - 1, total, words)
        zb = jnp.maximum(lax.shift_right_logical(zq, 2) - 1, 0)
        at = ((beside * Z_BINS + zb) * Y_TILES + lax.shift_right_logical(y0, 4)) * 8
        words_ref[1] = at | ((zq & 7) << 12) | ((y0 & 127) << 16) | (code << 24)

    def when_there(d, up, body):
        zi = z - d if up else z + d

        @pl.when((zi >= 0) & (zi < levels))
        def _():
            body(2 * zi)

    def later_own():
        for j in range(CUTS + 1, 2 * CUTS):
            for up in (True, False):
                pl.when(z != (0 if up else levels - 1))(functools.partial(own_z, j, up))

    def extra(d, up, farthest):
        end = (z == d) if up else (z == levels - 1 - d)

        @pl.when(end if farthest else jnp.logical_not(end))
        def _():
            for j in range(CUTS, 2 * CUTS):
                line(d, up, j)

    def line(d, up, j):
        more = can_up if up else can_down

        def body(i):
            i = i + x
            if j < CUTS:
                z_move(i, j, up).wait_recv()

                @pl.when(more)
                def _():
                    z_move(i, j, up).start()

                x_move(i, j).start()
                if d == 1:
                    @pl.when(jnp.logical_not(more))
                    def _():
                        y_move(i, j).start()
            elif d > 1:
                z_move(i, j, up).wait_recv()

                @pl.when(more)
                def _():
                    z_move(i, j, up).start()

                if d == levels - 1:
                    x_move(i, j).start()
                if j == 2 * CUTS - 1:
                    k_move(i).start()
            else:
                @pl.when(more)
                def _():
                    z_move(i, j, up).wait_recv()
                    z_move(i, j, up).start()
                    if j == 2 * CUTS - 1:
                        k_move(i).start()

        when_there(d, up, body)

    def cross(d, up, j):
        def body(i):
            i = i + 1 - x
            if j < CUTS:
                x_move(i, j).wait_recv()
                if d < levels - 1:
                    y_move(i, j).start()
            elif d == levels - 1:
                x_move(i, j).wait_recv()
                if j == 2 * CUTS - 1:
                    k_move(i).start()

        when_there(d, up, body)

    def y_done(d, up, own_column):
        def body(i):
            i = i + (x if own_column else 1 - x)

            def finish():
                for j in range(CUTS):
                    y_move(i, CUTS + j).wait_recv()
                k_move(i).start()

            if own_column:
                pl.when(jnp.logical_not(can_up if up else can_down))(finish)
            else:
                finish()

        when_there(d, up, body)

    ways = lambda d: (True, False) if d else (True,)
    for d in range(1, levels + 1):
        for j in range(CUTS):
            if d < levels:
                for up in ways(d):
                    line(d, up, j)
            for up in ways(d - 1):
                cross(d - 1, up, j)
            if d == 3 and j == 0:
                for up in ways(1):
                    extra(1, up, False)
        if d < levels:
            for up in ways(d):
                extra(d, up, True)
        if d == 1:
            later_own()
        if d == 3:
            for up in ways(2):
                extra(2, up, False)
            lists()
        if d == levels:
            for j in range(CUTS, 2 * CUTS):
                for up in ways(d - 1):
                    cross(d - 1, up, j)
        if d == 2:
            for up in ways(1):
                y_done(1, up, True)
        if 2 <= d <= levels:
            for up in ways(d - 2):
                y_done(d - 2, up, False)

    index_all().wait_send()
    sized(levels * part, xs.at[0], xr.at[0, 0], (across_x, rad)).wait_send()

    @pl.when(at_end)
    def _():
        sized(part, xs.at[1], xr.at[0, 1], (across_x, rad)).wait_send()

    for up in (True, False):
        way = 0 if up else 1
        peer = (lat + (2 if up else -2), rad)

        @pl.when(can_up if up else can_down)
        def _():
            for zi in range(levels):
                passed = (zi <= z) if up else (zi >= z)
                both = zi < levels - 2 if up else zi > 1

                @pl.when(passed)
                def _():
                    sized(2 * part if both else part, zs.at[2 * zi + x, way], zr.at[0, 0], peer).wait_send()

    sized(levels * part, ys, yr.at[0, 0], (lat, across_y)).wait_send()
    everything = sized((n_lat - 1) * half, bs, br, (lat, across_k))
    everything.wait_send()
    everything.wait_recv()


def grid_kernel(n_lat, words_ref, data_ref, whi_ref, wlo_ref, ghi_hbm, glo_hbm, out_hbm, acc0, acc1, acc2, fields, result, words, todo, ghi_ref, glo_ref, sem, smooth_sem, out_sem):
    accs = (acc0, acc1, acc2)
    smooth = [pltpu.make_async_copy(ghi_hbm, ghi_ref, smooth_sem.at[0]), pltpu.make_async_copy(glo_hbm, glo_ref, smooth_sem.at[1])]
    bring = pltpu.make_async_copy(words_ref, words.at[:, pl.ds(0, n_lat), :], sem)
    bring.start()
    for copy in smooth:
        copy.start()
    rows = acc0.shape[0]

    @pl.loop(0, rows // 8, unroll=11)
    def _(r):
        for acc in accs:
            acc[pl.ds(pl.multiple_of(r * 8, 8), 8), :] = jnp.zeros((8, LANES), jnp.float32)

    bring.wait()
    lane = lax.broadcasted_iota(jnp.int32, (8, LANES), 1)
    sub = lax.broadcasted_iota(jnp.int32, (8, LANES), 0)
    across = lane & 15
    along = lax.shift_right_logical(lane, 4)
    elements = words.shape[2]

    for u in range(SUM_GROUP):
        words[0, n_lat, u] = 0
        words[1, n_lat, u] = 0

    def listed(i, n):
        many = lax.div(words[0, i, elements - 1] + SUM_GROUP - 1, SUM_GROUP)

        @pl.loop(0, lax.div(many + 7, 8))
        def _(t):
            for u in range(8):
                todo[n + t * 8 + u] = (i << 16) + (t * 8 + u) * SUM_GROUP

        return n + many

    groups = lax.fori_loop(0, n_lat, listed, 0)
    batch = SUM_WAYS // SUM_GROUP
    for u in range(batch):
        todo[groups + u] = n_lat << 16

    @pl.loop(0, lax.div(groups + batch - 1, batch))
    def _(step):
        for g in range(batch):
            first_slot = todo[step * batch + g]
            i = lax.shift_right_logical(first_slot, 16)
            p0 = first_slot & 0xFFFF
            for u in range(SUM_GROUP):
                w0, w1 = words[0, i, p0 + u], words[1, i, p0 + u]
                row = w0 & 0xFFFF
                at = pl.multiple_of(w1 & 0xFFF, 8)
                v0, v1 = jnp.full((8, LANES), w0, jnp.int32), jnp.full((8, LANES), w1, jnp.int32)
                off = lax.shift_right_logical(v0, 16) & 127
                shift = lax.shift_right_logical(v0, 23)
                zq = lax.shift_right_logical(v1, 12)
                y0 = lax.shift_right_logical(v1, 16)
                low = lax.shift_right_logical(v1, 24)
                wide = lax.shift_right_logical(v1, 27)
                tz = (sub - zq) & 7
                turned = (lane - y0) & (LANES - 1)
                ty = turned & 15
                xl = lax.shift_right_logical(turned, 4)
                tx = (xl - low) & 7
                index = (25 * xl + shift + 5 * tz + ty) & (LANES - 1)
                good = (jnp.maximum(tz, ty) < 5) & (tx < wide)
                first = across >= (y0 & 15)
                here, there = good & first, good & jnp.logical_not(first)
                head = lane >= off
                for c in range(3):
                    a = data_ref[pl.ds(row + c, 1), :]
                    b = data_ref[pl.ds(row + 3 + c, 1), :]
                    v = jnp.broadcast_to(jnp.where(head[0:1], a, b), (8, LANES))
                    v = jnp.take_along_axis(v, index, axis=1, mode="promise_in_bounds")
                    accs[c][pl.ds(at, 8), :] += jnp.where(here, v, 0.0)
                    accs[c][pl.ds(at + 8, 8), :] += jnp.where(there, v, 0.0)

    low_half = sub < 4
    for copy in smooth:
        copy.wait()
    for c in range(3):
        acc, field = accs[c], fields.at[c]

        @pl.loop(0, 2, unroll=2)
        def _(g):
            @pl.loop(0, WINDOW // 8, unroll=WINDOW // 8)
            def _(h):
                for side in range(2):
                    v = []
                    for t in range(8):
                        def bins(n):
                            r = ((g * Z_BINS + 2 * h + n) * Y_TILES + side * 8 + t) * 8
                            return acc[pl.ds(pl.multiple_of(r, 8), 8), :]

                        v.append(bins(1) + jnp.where(low_half, bins(0), bins(2)))
                    for bit in (1, 2, 4):
                        v = [jnp.where((along & bit) == 0, v[t], v[(t + bit) % 8]) for t in range(8)]
                    v = [v[0]] + [pltpu.roll(v[8 - xl], LANES - 16 * xl, 1) for xl in range(1, 8)]
                    for xl in range(8):
                        r = pl.multiple_of(g * (CX * WINDOW) + xl * WINDOW + h * 8, 8)
                        field[pl.ds(r, 8), side * LANES : (side + 1) * LANES] = v[xl]

        def split(a):
            high = a.astype(jnp.bfloat16)
            return high, (a - high.astype(jnp.float32)).astype(jnp.bfloat16)

        def dot(a, b):
            return jnp.dot(a, b, preferred_element_type=jnp.float32)

        high, low = split(field[...])
        whi = whi_ref[...]
        mixed = dot(whi, high) + dot(wlo_ref[...], high) + dot(whi, low)
        high, low = split(mixed)
        ghi = ghi_ref[...]
        done = dot(high, ghi) + dot(low, ghi) + dot(high, glo_ref[...])
        result[c] = done.reshape(CX, CZ, NY)
        pltpu.make_async_copy(result.at[c], out_hbm.at[c], out_sem.at[c]).start()
    for c in range(3):
        pltpu.make_async_copy(result.at[c], out_hbm.at[c], out_sem.at[c]).wait()


def on_device_whole(n_lat, n_rad, kernels, cells, tiles, width_class):
    elements = tiles.shape[0]
    block = -(-kernels.shape[1] // LANES * 3 // 96) * 96
    smem = pl.BlockSpec(memory_space=pltpu.SMEM)
    vmem = pl.BlockSpec(memory_space=pltpu.VMEM)
    hbm = pl.BlockSpec(memory_space=pltpu.HBM)
    dma = pltpu.SemaphoreType.DMA
    stay = functools.partial(pltpu.with_memory_space_constraint, memory_space=pltpu.HBM)
    data, words, whi, wlo = pl.pallas_call(
        functools.partial(gather_kernel, n_lat, n_rad, block),
        out_shape=[
            jax.ShapeDtypeStruct((n_lat * block + 8, LANES), jnp.float32),
            jax.ShapeDtypeStruct((2, n_lat, elements), jnp.int32),
            jax.ShapeDtypeStruct((CX * CZ, DEPTH), jnp.bfloat16),
            jax.ShapeDtypeStruct((CX * CZ, DEPTH), jnp.bfloat16),
        ],
        in_specs=[smem, hbm, hbm, hbm],
        out_specs=[vmem] * 4,
        scratch_shapes=[
            pltpu.VMEM((3, block // 3 * LANES), jnp.float32),
            pltpu.VMEM((1, elements), jnp.int32),
            pltpu.VMEM(cells.shape, jnp.int32),
            pltpu.VMEM((n_lat, 8, elements), jnp.int32),
            pltpu.VMEM((8 * n_lat, DEPTH), jnp.float32),
            dma((4,)), dma, dma,
            dma((n_lat, 2)), dma((n_lat, 2 * CUTS)), dma((2,)), dma((n_lat, 2 * CUTS)),
            dma, dma((n_lat, CUTS)), dma, dma,
        ],
        compiler_params=pltpu.CompilerParams(
            vmem_limit_bytes=VMEM_LIMIT, collective_id=0, has_side_effects=True
        ),
    )(width_class, *map(stay, (tiles.reshape(1, elements), cells, kernels)))
    smooth = band_matrix(NY, 2.5, HY).T.astype(np.float32)
    high = smooth.astype(jnp.bfloat16)
    low = (smooth - high.astype(np.float32)).astype(jnp.bfloat16)
    rows = 2 * Z_BINS * Y_TILES * 8
    return pl.pallas_call(
        functools.partial(grid_kernel, n_lat),
        out_shape=jax.ShapeDtypeStruct((3, CX, CZ, NY), jnp.float32),
        in_specs=[vmem] * 4 + [hbm] * 2,
        out_specs=hbm,
        scratch_shapes=[
            pltpu.VMEM((rows, LANES), jnp.float32),
            pltpu.VMEM((rows, LANES), jnp.float32),
            pltpu.VMEM((rows, LANES), jnp.float32),
            pltpu.VMEM((3, DEPTH, NY), jnp.float32),
            pltpu.VMEM((3, CX, CZ, NY), jnp.float32),
            pltpu.SMEM((2, n_lat + 1, elements), jnp.int32),
            pltpu.SMEM((n_lat * elements // SUM_GROUP + 16,), jnp.int32),
            pltpu.VMEM((NY, NY), jnp.bfloat16),
            pltpu.VMEM((NY, NY), jnp.bfloat16),
            dma, dma((2,)), dma((3,)),
        ],
        compiler_params=pltpu.CompilerParams(vmem_limit_bytes=VMEM_LIMIT),
    )(words, data, whi, wlo, stay(jnp.asarray(high)), stay(jnp.asarray(low)))


def solution(mesh):
    n_lat, n_rad = mesh.shape["lat"], mesh.shape["rad"]
    whole = n_lat == 8 and n_rad == 4
    return jax.shard_map(
        functools.partial(on_device_whole if whole else on_device, n_lat, n_rad),
        mesh=mesh,
        in_specs=(P(None, "lat"), P(None, "lat"), P("lat", None), P("lat")),
        out_specs=P(None, "lat", "rad", None),
        check_vma=False,
    )
```

```python
import functools

import jax
import jax.numpy as jnp
import numpy as np
from jax import lax
from jax.experimental import pallas as pl
from jax.experimental.pallas import tpu as pltpu
from jax.sharding import PartitionSpec as P

CX = 8
NY = 256
CZ = 32
NGLL = 125
HW = 4
HY = 8
HZ = 4
ZP = CZ + 4 * HZ
LANES = 128
TAPS = 2 * HZ + 1
PADX = CX + 2 * HW
PACK_UNROLL = 4
SUM_UNROLL = 4
VMEM_LIMIT = 48 * 2**20
MESH = pl.DeviceIdType.MESH


def band_matrix(count, sigma, half):
    place = np.arange(count)
    gap = place[None, :] - place[:, None]
    gauss = np.where(np.abs(gap) <= half, np.exp(-(gap**2) / (2.0 * sigma**2)), 0.0)
    return gauss / gauss.sum(axis=1, keepdims=True)


def z_taps(n_rad):
    full = np.pad(band_matrix(CZ * n_rad, 1.5, HZ), ((0, 0), (HZ, HZ)))
    return np.stack([full[z, z : z + TAPS] for z in range(CZ * n_rad)]).astype(np.float32)


def pack_kernel(
    n_lat, n_rad, share, elements, tiles_ref, cells_hbm, kern_hbm, out_ref, count, todo, place, cells_ref, kern_ref, sems
):
    slab = lax.axis_index("rad")
    rows = elements * NGLL // LANES
    bring_cells = pltpu.make_async_copy(cells_hbm, cells_ref, sems.at[0])
    bring_kern = pltpu.make_async_copy(kern_hbm, kern_ref, sems.at[1])
    bring_cells.start()
    bring_kern.start()
    out_ref[...] = jnp.full(out_ref.shape, -1000.0, jnp.float32)
    lane = lax.broadcasted_iota(jnp.int32, (3, LANES), 1)

    @pl.loop(0, n_lat)
    def _(t):
        count[t] = 0

    def listed(e, n):
        t = tiles_ref[e]
        rank = count[t]
        count[t] = rank + 1
        slot = lax.div(rank, n_rad)
        todo[n] = e
        place[n] = t * share + slot
        return n + jnp.where(rank - slot * n_rad == slab, 1, 0)

    n = lax.fori_loop(0, elements, listed, 0, unroll=4)
    for more in range(PACK_UNROLL):
        todo[n + more] = 0
        place[n + more] = n_lat * share
    bring_cells.wait()
    bring_kern.wait()

    def packed(step, _):
        for u in range(PACK_UNROLL):
            e = todo[step * PACK_UNROLL + u]
            at = place[step * PACK_UNROLL + u]
            start = e * NGLL
            row = lax.shift_right_logical(start, 7)
            off = start & (LANES - 1)
            after = jnp.minimum(row + 1, rows - 1)
            a = kern_ref[:, pl.ds(pl.multiple_of(row * LANES, LANES), LANES)]
            b = kern_ref[:, pl.ds(pl.multiple_of(after * LANES, LANES), LANES)]
            v = pltpu.roll(jnp.where(lane >= off, a, b), (LANES - off) & (LANES - 1), 1)
            v = jnp.where(lane == NGLL, cells_ref[0, e].astype(jnp.float32), v)
            v = jnp.where(lane == NGLL + 1, cells_ref[1, e].astype(jnp.float32), v)
            v = jnp.where(lane == NGLL + 2, cells_ref[2, e].astype(jnp.float32), v)
            t = lax.div(at, share)
            slot = at - t * share
            for c in range(3):
                out_ref[t, pl.ds(c * share + slot, 1), :] = v[c : c + 1]
        return 0

    lax.fori_loop(0, lax.div(n + PACK_UNROLL - 1, PACK_UNROLL), packed, 0)


def exchange_kernel(n_lat, n_rad, send_ref, recv_ref, own_sem, send_sem, recv_sem, fwd_sem, got_sem):
    tile, slab = lax.axis_index("lat"), lax.axis_index("rad")
    barrier = pltpu.get_barrier_semaphore()

    @pl.loop(1, n_lat)
    def _(k):
        pl.semaphore_signal(barrier, inc=1, device_id=(lax.rem(tile + k, n_lat), slab), device_id_type=MESH)

    pair = slab + 1 - 2 * lax.rem(slab, 2)
    other = slab + 2 - 4 * lax.div(slab, 2)
    for peer in (pair, other):
        pl.semaphore_signal(barrier, inc=1, device_id=(tile, peer), device_id_type=MESH)
    pl.semaphore_wait(barrier, n_lat - 1 + 2)

    def across(k):
        to = lax.rem(tile + k, n_lat)
        return pltpu.make_async_remote_copy(
            src_ref=send_ref.at[to],
            dst_ref=recv_ref.at[slab, tile],
            send_sem=send_sem.at[k],
            recv_sem=recv_sem.at[k],
            device_id=(to, slab),
            device_id_type=MESH,
        )

    def share(k, of, to, way):
        block = recv_ref.at[of, lax.rem(tile + n_lat - k, n_lat)]
        return pltpu.make_async_remote_copy(
            src_ref=block,
            dst_ref=block,
            send_sem=fwd_sem.at[way, k],
            recv_sem=got_sem.at[way, k],
            device_id=(tile, to),
            device_id_type=MESH,
        )

    def forward(k):
        share(k, slab, other, 0).start()
        share(k, slab, pair, 1).start()

    def relay(k):
        share(k, other, other, 0).wait_recv()
        share(k, other, pair, 2).start()

    @pl.loop(1, n_lat)
    def _(k):
        across(k).start()

    own = pltpu.make_async_copy(send_ref.at[tile], recv_ref.at[slab, tile], own_sem)
    own.start()
    own.wait()
    forward(0)

    @pl.loop(1, n_lat)
    def _(k):
        across(k).wait_recv()
        forward(k)

    @pl.loop(0, n_lat)
    def _(k):
        relay(k)

    @pl.loop(0, n_lat)
    def _(k):
        share(k, pair, pair, 1).wait_recv()
        share(k, other + pair - slab, pair, 2).wait_recv()

    @pl.loop(1, n_lat)
    def _(k):
        across(k).wait_send()

    @pl.loop(0, n_lat)
    def _(k):
        share(k, slab, other, 0).wait_send()
        share(k, slab, pair, 1).wait_send()
        share(k, other, pair, 2).wait_send()


def sum_kernel(blocks, share, meta_ref, recv_ref, acc, todo):
    slab = lax.axis_index("rad")
    slots = blocks * share
    acc[...] = jnp.zeros(acc.shape, jnp.float32)
    lane = lax.broadcasted_iota(jnp.int32, (8, LANES), 1)
    sub = lax.broadcasted_iota(jnp.int32, (8, LANES), 0)
    ramp = 25 * sub + lane
    low = slab * CZ - 2 * HZ

    def listed(s, n):
        zb = meta_ref[slots + s] - low
        todo[n] = s
        return n + jnp.where((zb >= 0) & (zb < CZ + 3 * HZ), 1, 0)

    n = lax.fori_loop(0, slots, listed, 0, unroll=8)
    for more in range(SUM_UNROLL):
        todo[n + more] = 0

    def place(at, values, index, mask):
        for j in range(5):
            picked = jnp.where(mask, index + 5 * j, NGLL)
            for c in range(3):
                piece = jnp.take_along_axis(values[c], picked, axis=1, mode="promise_in_bounds")
                acc[pl.ds(pl.multiple_of(at + (3 * j + c) * 8, 8), 8), :] += piece

    def summed(step, _):
        later = []
        for u in range(SUM_UNROLL):
            s = todo[step * SUM_UNROLL + u]
            good = step * SUM_UNROLL + u < n
            x0 = jnp.clip(meta_ref[s], 0, CX - 5)
            zb = jnp.clip(meta_ref[slots + s] - low, 0, CZ + 3 * HZ - 1)
            y0 = jnp.clip(meta_ref[2 * slots + s], 0, NY - 5)
            block = lax.div(s, share)
            slot = s - block * share
            values = []
            for c in range(3):
                row = jnp.broadcast_to(recv_ref[block, pl.ds(c * share + slot, 1), :], (8, LANES))
                values.append(jnp.where(lane < NGLL, row, 0.0))
            half = lax.shift_right_logical(y0, 7)
            yl = y0 & (LANES - 1)
            index = ramp - (25 * x0 + yl)
            rows = (sub >= x0) & (sub < jnp.where(good, x0 + 5, 0))
            at = (half * ZP + zb) * 24
            place(at, values, index, rows & (lane >= yl) & (lane < yl + 5))
            later.append((at, values, index, rows, yl))
        widest = functools.reduce(jnp.maximum, [entry[4] for entry in later])

        @pl.when(widest > LANES - 5)
        def _():
            for at, values, index, rows, yl in later:
                over = rows & (lane < yl + 5 - LANES)

                @pl.when(yl > LANES - 5)
                def _():
                    place(at + ZP * 24, values, index + LANES, over)

        return 0

    lax.fori_loop(0, lax.div(n + SUM_UNROLL - 1, SUM_UNROLL), summed, 0)


def finish_kernel(n_lat, taps_ref, wx_ref, acc, wy_ref, out_ref, planes, rows_ref, send_sem, recv_sem):
    tile, slab = lax.axis_index("lat"), lax.axis_index("rad")
    barrier = pltpu.get_barrier_semaphore()
    has_prev, has_next = tile > 0, tile < n_lat - 1
    halo = HW * CZ

    @pl.when(has_prev)
    def _():
        pl.semaphore_signal(barrier, inc=1, device_id=(tile - 1, slab), device_id_type=MESH)

    @pl.when(has_next)
    def _():
        pl.semaphore_signal(barrier, inc=1, device_id=(tile + 1, slab), device_id_type=MESH)

    def at(c, row, count):
        return rows_ref.at[:, pl.ds(c * PADX * CZ + row, count), :]

    def to_next(c):
        return pltpu.make_async_remote_copy(
            src_ref=at(c, CX * CZ, halo),
            dst_ref=at(c, 0, halo),
            send_sem=send_sem.at[0, c],
            recv_sem=recv_sem.at[0, c],
            device_id=(tile + 1, slab),
            device_id_type=MESH,
        )

    def to_prev(c):
        return pltpu.make_async_remote_copy(
            src_ref=at(c, halo, halo),
            dst_ref=at(c, halo + CX * CZ, halo),
            send_sem=send_sem.at[1, c],
            recv_sem=recv_sem.at[1, c],
            device_id=(tile - 1, slab),
            device_id_type=MESH,
        )

    for c in range(3):

        @pl.loop(0, CZ, unroll=4)
        def _(z):
            for half in range(NY // LANES):
                total = jnp.zeros((CX, LANES), jnp.float32)
                for d in range(TAPS):
                    weight = taps_ref[(slab * CZ + z) * TAPS + d]
                    row = pl.multiple_of(((half * ZP + z + HZ + d) * 3 + c) * CX, 8)
                    total = total + weight * acc[pl.ds(row, CX), :]
                cols = slice(half * LANES, (half + 1) * LANES)
                planes[pl.ds(pl.multiple_of(z * CX, 8), CX), cols] = total

        product = jnp.dot(planes[...], wy_ref[...], precision=lax.Precision.HIGHEST)
        for z in range(CZ):
            for half in range(NY // LANES):
                piece = product[z * CX : (z + 1) * CX, half * LANES : (half + 1) * LANES]
                rows_ref[half, pl.ds(c * PADX * CZ + halo + z, CX, stride=CZ), :] = piece

        if c == 0:
            beside = jnp.minimum(tile, 1) + jnp.minimum(n_lat - 1 - tile, 1)
            pl.semaphore_wait(barrier, beside)

        @pl.when(has_next)
        def _():
            to_next(c).start()

        @pl.when(has_prev)
        def _():
            to_prev(c).start()

        zeros = jnp.zeros((NY // LANES, halo, LANES), jnp.float32)

        @pl.when(tile == 0)
        def _():
            rows_ref[:, c * PADX * CZ : c * PADX * CZ + halo, :] = zeros

        @pl.when(tile == n_lat - 1)
        def _():
            rows_ref[:, c * PADX * CZ + halo + CX * CZ : (c + 1) * PADX * CZ, :] = zeros

    for c in range(3):

        @pl.when(has_prev)
        def _():
            to_next(c).wait_recv()

        @pl.when(has_next)
        def _():
            to_prev(c).wait_recv()

        @pl.loop(0, CX)
        def _(x):
            for half in range(NY // LANES):
                total = jnp.zeros((CZ, LANES), jnp.float32)
                for d in range(2 * HW + 1):
                    row = pl.multiple_of(c * PADX * CZ + (x + d) * CZ, 8)
                    total = total + wx_ref[x * (2 * HW + 1) + d] * rows_ref[half, pl.ds(row, CZ), :]
                out_ref[c, x, :, half * LANES : (half + 1) * LANES] = total

    for c in range(3):

        @pl.when(has_next)
        def _():
            to_next(c).wait_send()

        @pl.when(has_prev)
        def _():
            to_prev(c).wait_send()


def x_weights(width_class, n_lat):
    rows = lax.axis_index("lat") * CX + jnp.arange(CX)
    sigma = 1.0 + 0.75 * width_class[0].astype(jnp.float32)
    offsets = jnp.arange(-HW, HW + 1)
    target = rows[:, None] + offsets[None, :]
    valid = (target >= 0) & (target < CX * n_lat)
    gauss = jnp.exp(-(offsets[None, :].astype(jnp.float32) ** 2) / (2.0 * sigma**2))
    gauss = jnp.where(valid, gauss, 0.0)
    return gauss / jnp.sum(gauss, axis=1, keepdims=True)


def on_device(n_lat, n_rad, kernels, cells, tiles, width_class):
    elements = tiles.shape[0]
    cap = max(2, 2 * elements // n_lat)
    share = -(-cap // n_rad)
    blocks = n_rad * n_lat
    slots = blocks * share
    params = pltpu.CompilerParams(vmem_limit_bytes=VMEM_LIMIT)
    smem = pl.BlockSpec(memory_space=pltpu.SMEM)
    vmem = pl.BlockSpec(memory_space=pltpu.VMEM)
    hbm = pl.BlockSpec(memory_space=pl.ANY)
    send = pl.pallas_call(
        functools.partial(pack_kernel, n_lat, n_rad, share, elements),
        out_shape=jax.ShapeDtypeStruct((n_lat + 1, 3 * share, LANES), jnp.float32),
        in_specs=[smem, hbm, hbm],
        out_specs=vmem,
        scratch_shapes=[
            pltpu.SMEM((n_lat,), jnp.int32),
            pltpu.SMEM((elements + PACK_UNROLL,), jnp.int32),
            pltpu.SMEM((elements + PACK_UNROLL,), jnp.int32),
            pltpu.SMEM(cells.shape, jnp.int32),
            pltpu.VMEM(kernels.shape, jnp.float32),
            pltpu.SemaphoreType.DMA((2,)),
        ],
        compiler_params=params,
    )(tiles.reshape(-1), cells, kernels)
    recv = pl.pallas_call(
        functools.partial(exchange_kernel, n_lat, n_rad),
        out_shape=jax.ShapeDtypeStruct((n_rad, n_lat, 3 * share, LANES), jnp.float32),
        in_specs=[vmem],
        out_specs=vmem,
        scratch_shapes=[
            pltpu.SemaphoreType.DMA,
            pltpu.SemaphoreType.DMA((n_lat,)),
            pltpu.SemaphoreType.DMA((n_lat,)),
            pltpu.SemaphoreType.DMA((3, n_lat)),
            pltpu.SemaphoreType.DMA((3, n_lat)),
        ],
        compiler_params=pltpu.CompilerParams(
            vmem_limit_bytes=VMEM_LIMIT, collective_id=0, has_side_effects=True
        ),
    )(send)
    recv = recv.reshape(blocks, 3 * share, LANES)
    meta = recv[:, :share, NGLL:].transpose(2, 0, 1).reshape(-1).astype(jnp.int32)
    grid_rows = NY // LANES * ZP * 24
    summed = pl.pallas_call(
        functools.partial(sum_kernel, blocks, share),
        out_shape=jax.ShapeDtypeStruct((grid_rows, LANES), jnp.float32),
        in_specs=[smem, vmem],
        out_specs=vmem,
        scratch_shapes=[pltpu.SMEM((slots + SUM_UNROLL,), jnp.int32)],
        compiler_params=params,
    )(meta, recv)
    return pl.pallas_call(
        functools.partial(finish_kernel, n_lat),
        out_shape=jax.ShapeDtypeStruct((3, CX, CZ, NY), jnp.float32),
        in_specs=[smem, smem, vmem, vmem],
        out_specs=vmem,
        scratch_shapes=[
            pltpu.VMEM((CZ * CX, NY), jnp.float32),
            pltpu.VMEM((NY // LANES, 3 * PADX * CZ, LANES), jnp.float32),
            pltpu.SemaphoreType.DMA((2, 3)),
            pltpu.SemaphoreType.DMA((2, 3)),
        ],
        compiler_params=pltpu.CompilerParams(
            vmem_limit_bytes=VMEM_LIMIT, collective_id=1, has_side_effects=True
        ),
    )(
        jnp.asarray(z_taps(n_rad).reshape(-1)),
        x_weights(width_class, n_lat).reshape(-1),
        summed,
        jnp.asarray(band_matrix(NY, 2.5, HY).T.astype(np.float32)),
    )

ROW_TILES = 3
Z_BINS = 11
Y_TILES = 17
WINDOW = CZ + 2 * HZ
DEPTH = 2 * CX * WINDOW
SUM_WAYS = 40
SUM_GROUP = 4
CUTS = 4


def gather_kernel(n_lat, n_rad, block, width_ref, tiles_hbm, cells_hbm, kern_hbm, data_ref, words_ref, whi_ref, wlo_ref,
                  kern_ref, tiles_ref, cells_ref, index_ref, compact_ref, in_sem, is_sem, ir_sem, zs, zr, xs, xr, ys, yr, bs, br):
    lat, rad = lax.axis_index("lat"), lax.axis_index("rad")
    levels = n_lat // 2
    z, x = lax.div(lat, 2), lax.rem(lat, 2)
    y, k = lax.div(rad, 2), lax.rem(rad, 2)
    across_x, across_y, across_k = lat + 1 - 2 * x, rad + 2 - 4 * y, rad + 1 - 2 * k
    barrier = pltpu.get_barrier_semaphore()

    @pl.loop(1, n_lat)
    def _(step):
        pl.semaphore_signal(barrier, inc=1, device_id=(lax.rem(lat + step, n_lat), rad), device_id_type=MESH)

    for peer in (across_y, across_k):
        pl.semaphore_signal(barrier, inc=1, device_id=(lat, peer), device_id_type=MESH)
    points = kern_hbm.shape[1]
    split = block // 6 * LANES
    brought = [
        pltpu.make_async_copy(kern_hbm.at[:, :split], kern_ref.at[:, :split], in_sem.at[0]),
        pltpu.make_async_copy(kern_hbm.at[:, split:], kern_ref.at[:, split:points], in_sem.at[3]),
        pltpu.make_async_copy(tiles_hbm, tiles_ref, in_sem.at[1]),
        pltpu.make_async_copy(cells_hbm, cells_ref, in_sem.at[2]),
    ]
    for copy in brought:
        copy.start()
    if kern_ref.shape[1] > points:
        kern_ref[:, points:] = jnp.zeros((3, kern_ref.shape[1] - points), jnp.float32)

    half = block // 2
    part = half // 2
    mine = k * half
    piece = part // CUTS
    starts = [mine + (y if j < CUTS else 1 - y) * part + j % CUTS * piece for j in range(2 * CUTS)]

    def move(row, count, send_sem, recv_sem, device):
        rows = data_ref.at[pl.ds(pl.multiple_of(row, 8), count)]
        return pltpu.make_async_remote_copy(
            src_ref=rows, dst_ref=rows, send_sem=send_sem, recv_sem=recv_sem,
            device_id=device, device_id_type=MESH)

    def z_move(i, j, up):
        way = 0 if up else 1
        return move(i * block + starts[j], piece, zs.at[i, way], zr.at[i, j], (lat + (2 if up else -2), rad))

    def x_move(i, j):
        return move(i * block + starts[j], piece, xs.at[j // CUTS], xr.at[i, j], (across_x, rad))

    def y_move(i, j):
        return move(i * block + starts[j], piece, ys, yr.at[i, j % CUTS], (lat, across_y))

    def k_move(i):
        return move(i * block + mine, half, bs, br, (lat, across_k))

    def sized(rows, send_sem, recv_sem, device):
        return move(0, rows, send_sem, recv_sem, device)

    def index_move(step):
        to = lax.rem(lat + step, n_lat)
        return pltpu.make_async_remote_copy(
            src_ref=index_ref.at[lat], dst_ref=index_ref.at[lat], send_sem=is_sem, recv_sem=ir_sem,
            device_id=(to, rad), device_id_type=MESH)

    def index_all():
        others = index_ref.at[pl.ds(0, n_lat - 1)]
        return pltpu.make_async_remote_copy(
            src_ref=others, dst_ref=others, send_sem=is_sem, recv_sem=ir_sem,
            device_id=(across_x, rad), device_id_type=MESH)

    can_up, can_down = z < levels - 1, z > 0
    at_end = (z == 0) | (z == levels - 1)
    long_up, long_down = z < levels - 2, z > 1
    base = pl.multiple_of(lat * block, 8)
    sets = block // 24

    def pack(first, count):
        @pl.loop(0, count, unroll=4)
        def _(g):
            at = (first + g) * 8 * LANES
            rows = [kern_ref[:, pl.ds(pl.multiple_of(at + u * LANES, LANES), LANES)] for u in range(8)]
            data_ref[pl.ds(base + pl.multiple_of((first + g) * 24, 8), 24), :] = jnp.concatenate(rows, axis=0)

    def pack_part(j):
        pack(k * (sets // 2) + (y if j == 0 else 1 - y) * (sets // 4), sets // 4)

    @pl.when(k == 0)
    def _():
        brought[0].wait()

    @pl.when(k == 1)
    def _():
        brought[1].wait()

    pack_part(0)
    pl.semaphore_wait(barrier, n_lat - 1 + 2)

    def own_z(j, up):
        able = (long_up if up else long_down) if j >= CUTS else (can_up if up else can_down)

        @pl.when(able)
        def _():
            z_move(lat, j, up).start()

    for j in range(CUTS):
        own_z(j, True)
        own_z(j, False)
        x_move(lat, j).start()
    pack_part(1)
    for j in range(CUTS, 2 * CUTS):
        for up in (True, False):
            if j == CUTS:
                own_z(j, up)
            else:
                pl.when(z == (0 if up else levels - 1))(functools.partial(own_z, j, up))

    brought[2].wait()
    brought[3].wait()
    index_ref[lat] = jnp.concatenate([tiles_ref[...], cells_ref[...], jnp.zeros((4, tiles_ref.shape[1]), jnp.int32)], axis=0)

    @pl.loop(1, n_lat)
    def _(step):
        index_move(step).start()

    @pl.when(k == 1)
    def _():
        brought[0].wait()

    @pl.when(k == 0)
    def _():
        brought[1].wait()

    pack((1 - k) * (sets // 2), sets // 2)

    def weights():
        col = lax.broadcasted_iota(jnp.int32, (8, DEPTH), 1)
        beside = col >= CX * WINDOW
        rest = jnp.where(beside, col - CX * WINDOW, col)
        xl = lax.shift_right_logical(rest * 1639, 16)
        zc = rest - WINDOW * xl
        place = jnp.where(beside, jnp.where(xl < HW, xl + CX, xl - CX), xl)
        sub = lax.broadcasted_iota(jnp.int32, (8, DEPTH), 0)
        sigma = 1.0 + 0.75 * jnp.full((8, DEPTH), width_ref[0], jnp.int32).astype(jnp.float32)
        twice = 2.0 * sigma * sigma

        def bell(d, reach, scale):
            square = (d * d).astype(jnp.float32)
            return jnp.where(jnp.abs(d) <= reach, jnp.exp(-square / scale), 0.0)

        norm = jnp.zeros((8, DEPTH), jnp.float32)
        for d in range(-HW, HW + 1):
            at = lat * CX + sub + d
            norm += jnp.where((at >= 0) & (at < CX * n_lat), jnp.exp(-float(d * d) / twice), 0.0)
        wx = bell(place - sub, HW, twice) / norm
        for zv in range(CZ // 8):
            norm = jnp.zeros((8, DEPTH), jnp.float32)
            zz = sub + 8 * zv
            for d in range(-HZ, HZ + 1):
                at = rad * CZ + zz + d
                norm += jnp.where((at >= 0) & (at < CZ * n_rad), float(np.exp(-d * d / 4.5)), 0.0)
            kern_w[zv * 8 : zv * 8 + 8, :] = bell(zc - HZ - zz, HZ, 4.5) / norm
        for xx in range(CX):
            both = kern_w[...] * wx[xx : xx + 1, :]
            high = both.astype(jnp.bfloat16)
            whi_ref[xx * CZ : xx * CZ + CZ, :] = high
            wlo_ref[xx * CZ : xx * CZ + CZ, :] = (both - high.astype(jnp.float32)).astype(jnp.bfloat16)

    kern_w = compact_ref.at[pl.ds(0, CZ)]
    weights()

    def lists():
        index_all().wait_recv()
        elements = index_ref.shape[2]
        shape = (n_lat, elements)
        rel = index_ref[:, 0, :] - lat
        x0 = index_ref[:, 1, :]
        zq = index_ref[:, 2, :] - rad * CZ + HZ + 8
        y0 = index_ref[:, 3, :]
        keep = (rel >= -1) & (rel <= 1) & (zq >= 4) & (zq < WINDOW + 8)
        before = lax.broadcasted_iota(jnp.int32, (elements, elements), 0) < lax.broadcasted_iota(jnp.int32, (elements, elements), 1)
        flags = jnp.where(keep, 1.0, 0.0)
        rank = jnp.dot(flags.astype(jnp.bfloat16), jnp.where(before, 1.0, 0.0).astype(jnp.bfloat16), preferred_element_type=jnp.float32)
        total = jnp.sum(flags, axis=1, keepdims=True).astype(jnp.int32)
        rank = jnp.where(keep, rank, -1.0)
        low = jnp.maximum(x0, jnp.where(rel < 0, HW, 0))
        high = jnp.minimum(x0 + 4, jnp.where(rel > 0, HW - 1, CX - 1))
        code = low + 8 * (high - low + 1)
        lane = lax.broadcasted_iota(jnp.int32, shape, 1)
        fields = [lane, zq, y0, x0, code, jnp.where(rel == 0, 0, 1)]
        fields = [jnp.where(keep, f, 0).astype(jnp.float32) for f in fields]
        slot = lax.broadcasted_iota(jnp.int32, (elements, elements), 0).astype(jnp.float32)
        zero = jnp.zeros((1, elements), jnp.float32)
        for i in range(n_lat):
            stack = jnp.concatenate([f[i : i + 1] for f in fields] + [zero, zero], axis=0).astype(jnp.bfloat16)
            pick = jnp.where(rank[i : i + 1] == slot, 1.0, 0.0).astype(jnp.bfloat16)
            compact_ref[8 * i : 8 * i + 8, :elements] = lax.dot_general(
                stack, pick, (((1,), (1,)), ((), ())), preferred_element_type=jnp.float32)

        def field(f):
            return jnp.concatenate([compact_ref[8 * i + f : 8 * i + f + 1, :elements] for i in range(n_lat)], axis=0).astype(jnp.int32)

        e, zq, y0, x0, code, beside = [field(f) for f in range(6)]
        start = e * NGLL
        row = lax.broadcasted_iota(jnp.int32, shape, 0) * block + 3 * lax.shift_right_logical(start, 7)
        off = start & (LANES - 1)
        words = row | (off << 16) | (((off - 25 * x0) & (LANES - 1)) << 23)
        words_ref[0] = jnp.where(lane == elements - 1, total, words)
        zb = jnp.maximum(lax.shift_right_logical(zq, 2) - 1, 0)
        at = ((beside * Z_BINS + zb) * Y_TILES + lax.shift_right_logical(y0, 4)) * 8
        words_ref[1] = at | ((zq & 7) << 12) | ((y0 & 127) << 16) | (code << 24)

    def when_there(d, up, body):
        zi = z - d if up else z + d

        @pl.when((zi >= 0) & (zi < levels))
        def _():
            body(2 * zi)

    def later_own():
        for j in range(CUTS + 1, 2 * CUTS):
            for up in (True, False):
                pl.when(z != (0 if up else levels - 1))(functools.partial(own_z, j, up))

    def extra(d, up, farthest):
        end = (z == d) if up else (z == levels - 1 - d)

        @pl.when(end if farthest else jnp.logical_not(end))
        def _():
            for j in range(CUTS, 2 * CUTS):
                line(d, up, j)

    def line(d, up, j):
        more = can_up if up else can_down

        def body(i):
            i = i + x
            if j < CUTS:
                z_move(i, j, up).wait_recv()

                @pl.when(more)
                def _():
                    z_move(i, j, up).start()

                x_move(i, j).start()
                if d == 1:
                    @pl.when(jnp.logical_not(more))
                    def _():
                        y_move(i, j).start()
            elif d > 1:
                z_move(i, j, up).wait_recv()

                @pl.when(more)
                def _():
                    z_move(i, j, up).start()

                if d == levels - 1:
                    x_move(i, j).start()
                if j == 2 * CUTS - 1:
                    k_move(i).start()
            else:
                @pl.when(more)
                def _():
                    z_move(i, j, up).wait_recv()
                    z_move(i, j, up).start()
                    if j == 2 * CUTS - 1:
                        k_move(i).start()

        when_there(d, up, body)

    def cross(d, up, j):
        def body(i):
            i = i + 1 - x
            if j < CUTS:
                x_move(i, j).wait_recv()
                if d < levels - 1:
                    y_move(i, j).start()
            elif d == levels - 1:
                x_move(i, j).wait_recv()
                if j == 2 * CUTS - 1:
                    k_move(i).start()

        when_there(d, up, body)

    def y_done(d, up, own_column):
        def body(i):
            i = i + (x if own_column else 1 - x)

            def finish():
                for j in range(CUTS):
                    y_move(i, CUTS + j).wait_recv()
                k_move(i).start()

            if own_column:
                pl.when(jnp.logical_not(can_up if up else can_down))(finish)
            else:
                finish()

        when_there(d, up, body)

    ways = lambda d: (True, False) if d else (True,)
    for d in range(1, levels + 1):
        for j in range(CUTS):
            if d < levels:
                for up in ways(d):
                    line(d, up, j)
            for up in ways(d - 1):
                cross(d - 1, up, j)
            if d == 3 and j == 0:
                for up in ways(1):
                    extra(1, up, False)
        if d < levels:
            for up in ways(d):
                extra(d, up, True)
        if d == 1:
            later_own()
        if d == 3:
            for up in ways(2):
                extra(2, up, False)
            lists()
        if d == levels:
            for j in range(CUTS, 2 * CUTS):
                for up in ways(d - 1):
                    cross(d - 1, up, j)
        if d == 2:
            for up in ways(1):
                y_done(1, up, True)
        if 2 <= d <= levels:
            for up in ways(d - 2):
                y_done(d - 2, up, False)

    index_all().wait_send()
    sized(levels * part, xs.at[0], xr.at[0, 0], (across_x, rad)).wait_send()

    @pl.when(at_end)
    def _():
        sized(part, xs.at[1], xr.at[0, 1], (across_x, rad)).wait_send()

    for up in (True, False):
        way = 0 if up else 1
        peer = (lat + (2 if up else -2), rad)

        @pl.when(can_up if up else can_down)
        def _():
            for zi in range(levels):
                passed = (zi <= z) if up else (zi >= z)
                both = zi < levels - 2 if up else zi > 1

                @pl.when(passed)
                def _():
                    sized(2 * part if both else part, zs.at[2 * zi + x, way], zr.at[0, 0], peer).wait_send()

    sized(levels * part, ys, yr.at[0, 0], (lat, across_y)).wait_send()
    everything = sized((n_lat - 1) * half, bs, br, (lat, across_k))
    everything.wait_send()
    everything.wait_recv()


def grid_kernel(n_lat, words_ref, data_ref, whi_ref, wlo_ref, ghi_hbm, glo_hbm, out_hbm, acc0, acc1, acc2, fields, result, words, todo, ghi_ref, glo_ref, sem, smooth_sem, out_sem):
    accs = (acc0, acc1, acc2)
    smooth = [pltpu.make_async_copy(ghi_hbm, ghi_ref, smooth_sem.at[0]), pltpu.make_async_copy(glo_hbm, glo_ref, smooth_sem.at[1])]
    bring = pltpu.make_async_copy(words_ref, words.at[:, pl.ds(0, n_lat), :], sem)
    bring.start()
    for copy in smooth:
        copy.start()
    rows = acc0.shape[0]

    @pl.loop(0, rows // 8, unroll=11)
    def _(r):
        for acc in accs:
            acc[pl.ds(pl.multiple_of(r * 8, 8), 8), :] = jnp.zeros((8, LANES), jnp.float32)

    bring.wait()
    lane = lax.broadcasted_iota(jnp.int32, (8, LANES), 1)
    sub = lax.broadcasted_iota(jnp.int32, (8, LANES), 0)
    across = lane & 15
    along = lax.shift_right_logical(lane, 4)
    elements = words.shape[2]

    for u in range(SUM_GROUP):
        words[0, n_lat, u] = 0
        words[1, n_lat, u] = 0

    def listed(i, n):
        many = lax.div(words[0, i, elements - 1] + SUM_GROUP - 1, SUM_GROUP)

        @pl.loop(0, lax.div(many + 7, 8))
        def _(t):
            for u in range(8):
                todo[n + t * 8 + u] = (i << 16) + (t * 8 + u) * SUM_GROUP

        return n + many

    groups = lax.fori_loop(0, n_lat, listed, 0)
    batch = SUM_WAYS // SUM_GROUP
    for u in range(batch):
        todo[groups + u] = n_lat << 16

    @pl.loop(0, lax.div(groups + batch - 1, batch))
    def _(step):
        for g in range(batch):
            first_slot = todo[step * batch + g]
            i = lax.shift_right_logical(first_slot, 16)
            p0 = first_slot & 0xFFFF
            for u in range(SUM_GROUP):
                w0, w1 = words[0, i, p0 + u], words[1, i, p0 + u]
                row = w0 & 0xFFFF
                at = pl.multiple_of(w1 & 0xFFF, 8)
                v0, v1 = jnp.full((8, LANES), w0, jnp.int32), jnp.full((8, LANES), w1, jnp.int32)
                off = lax.shift_right_logical(v0, 16) & 127
                shift = lax.shift_right_logical(v0, 23)
                zq = lax.shift_right_logical(v1, 12)
                y0 = lax.shift_right_logical(v1, 16)
                low = lax.shift_right_logical(v1, 24)
                wide = lax.shift_right_logical(v1, 27)
                tz = (sub - zq) & 7
                turned = (lane - y0) & (LANES - 1)
                ty = turned & 15
                xl = lax.shift_right_logical(turned, 4)
                tx = (xl - low) & 7
                index = (25 * xl + shift + 5 * tz + ty) & (LANES - 1)
                good = (jnp.maximum(tz, ty) < 5) & (tx < wide)
                first = across >= (y0 & 15)
                here, there = good & first, good & jnp.logical_not(first)
                head = lane >= off
                for c in range(3):
                    a = data_ref[pl.ds(row + c, 1), :]
                    b = data_ref[pl.ds(row + 3 + c, 1), :]
                    v = jnp.broadcast_to(jnp.where(head[0:1], a, b), (8, LANES))
                    v = jnp.take_along_axis(v, index, axis=1, mode="promise_in_bounds")
                    accs[c][pl.ds(at, 8), :] += jnp.where(here, v, 0.0)
                    accs[c][pl.ds(at + 8, 8), :] += jnp.where(there, v, 0.0)

    low_half = sub < 4
    for copy in smooth:
        copy.wait()
    for c in range(3):
        acc, field = accs[c], fields.at[c]

        @pl.loop(0, 2, unroll=2)
        def _(g):
            @pl.loop(0, WINDOW // 8, unroll=WINDOW // 8)
            def _(h):
                for side in range(2):
                    v = []
                    for t in range(8):
                        def bins(n):
                            r = ((g * Z_BINS + 2 * h + n) * Y_TILES + side * 8 + t) * 8
                            return acc[pl.ds(pl.multiple_of(r, 8), 8), :]

                        v.append(bins(1) + jnp.where(low_half, bins(0), bins(2)))
                    for bit in (1, 2, 4):
                        v = [jnp.where((along & bit) == 0, v[t], v[(t + bit) % 8]) for t in range(8)]
                    v = [v[0]] + [pltpu.roll(v[8 - xl], LANES - 16 * xl, 1) for xl in range(1, 8)]
                    for xl in range(8):
                        r = pl.multiple_of(g * (CX * WINDOW) + xl * WINDOW + h * 8, 8)
                        field[pl.ds(r, 8), side * LANES : (side + 1) * LANES] = v[xl]

        def split(a):
            high = a.astype(jnp.bfloat16)
            return high, (a - high.astype(jnp.float32)).astype(jnp.bfloat16)

        def dot(a, b):
            return jnp.dot(a, b, preferred_element_type=jnp.float32)

        high, low = split(field[...])
        whi = whi_ref[...]
        mixed = dot(whi, high) + dot(wlo_ref[...], high) + dot(whi, low)
        high, low = split(mixed)
        ghi = ghi_ref[...]
        done = dot(high, ghi) + dot(low, ghi) + dot(high, glo_ref[...])
        result[c] = done.reshape(CX, CZ, NY)
        pltpu.make_async_copy(result.at[c], out_hbm.at[c], out_sem.at[c]).start()
    for c in range(3):
        pltpu.make_async_copy(result.at[c], out_hbm.at[c], out_sem.at[c]).wait()


def on_device_whole(n_lat, n_rad, kernels, cells, tiles, width_class):
    elements = tiles.shape[0]
    block = -(-kernels.shape[1] // LANES * 3 // 96) * 96
    smem = pl.BlockSpec(memory_space=pltpu.SMEM)
    vmem = pl.BlockSpec(memory_space=pltpu.VMEM)
    hbm = pl.BlockSpec(memory_space=pltpu.HBM)
    dma = pltpu.SemaphoreType.DMA
    stay = functools.partial(pltpu.with_memory_space_constraint, memory_space=pltpu.HBM)
    data, words, whi, wlo = pl.pallas_call(
        functools.partial(gather_kernel, n_lat, n_rad, block),
        out_shape=[
            jax.ShapeDtypeStruct((n_lat * block + 8, LANES), jnp.float32),
            jax.ShapeDtypeStruct((2, n_lat, elements), jnp.int32),
            jax.ShapeDtypeStruct((CX * CZ, DEPTH), jnp.bfloat16),
            jax.ShapeDtypeStruct((CX * CZ, DEPTH), jnp.bfloat16),
        ],
        in_specs=[smem, hbm, hbm, hbm],
        out_specs=[vmem] * 4,
        scratch_shapes=[
            pltpu.VMEM((3, block // 3 * LANES), jnp.float32),
            pltpu.VMEM((1, elements), jnp.int32),
            pltpu.VMEM(cells.shape, jnp.int32),
            pltpu.VMEM((n_lat, 8, elements), jnp.int32),
            pltpu.VMEM((8 * n_lat, DEPTH), jnp.float32),
            dma((4,)), dma, dma,
            dma((n_lat, 2)), dma((n_lat, 2 * CUTS)), dma((2,)), dma((n_lat, 2 * CUTS)),
            dma, dma((n_lat, CUTS)), dma, dma,
        ],
        compiler_params=pltpu.CompilerParams(
            vmem_limit_bytes=VMEM_LIMIT, collective_id=0, has_side_effects=True
        ),
    )(width_class, *map(stay, (tiles.reshape(1, elements), cells, kernels)))
    smooth = band_matrix(NY, 2.5, HY).T.astype(np.float32)
    high = smooth.astype(jnp.bfloat16)
    low = (smooth - high.astype(np.float32)).astype(jnp.bfloat16)
    rows = 2 * Z_BINS * Y_TILES * 8
    return pl.pallas_call(
        functools.partial(grid_kernel, n_lat),
        out_shape=jax.ShapeDtypeStruct((3, CX, CZ, NY), jnp.float32),
        in_specs=[vmem] * 4 + [hbm] * 2,
        out_specs=hbm,
        scratch_shapes=[
            pltpu.VMEM((rows, LANES), jnp.float32),
            pltpu.VMEM((rows, LANES), jnp.float32),
            pltpu.VMEM((rows, LANES), jnp.float32),
            pltpu.VMEM((3, DEPTH, NY), jnp.float32),
            pltpu.VMEM((3, CX, CZ, NY), jnp.float32),
            pltpu.SMEM((2, n_lat + 1, elements), jnp.int32),
            pltpu.SMEM((n_lat * elements // SUM_GROUP + 16,), jnp.int32),
            pltpu.VMEM((NY, NY), jnp.bfloat16),
            pltpu.VMEM((NY, NY), jnp.bfloat16),
            dma, dma((2,)), dma((3,)),
        ],
        compiler_params=pltpu.CompilerParams(vmem_limit_bytes=VMEM_LIMIT),
    )(words, data, whi, wlo, stay(jnp.asarray(high)), stay(jnp.asarray(low)))


def solution(mesh):
    n_lat, n_rad = mesh.shape["lat"], mesh.shape["rad"]
    whole = n_lat == 8 and n_rad == 4
    return jax.shard_map(
        functools.partial(on_device_whole if whole else on_device, n_lat, n_rad),
        mesh=mesh,
        in_specs=(P(None, "lat"), P(None, "lat"), P("lat", None), P("lat")),
        out_specs=P(None, "lat", "rad", None),
        check_vma=False,
    )
```
